32 devices in a mesh: dp: 4 (over y, x), expert: 8 (over z, core).
Axes of the slice: x: 2, y: 2, z: 4, core: 2. Of those that a mesh axis runs over, the one named last changes fastest.
Arguments:
- tokens: bfloat16 [4096, 2048], P(('dp', 'expert')), may hold values from -6 to 6
- cotangent: bfloat16 [4096, 2048], P(('dp', 'expert')), may hold values from -6 to 6
- gate_probs: float32 [4096, 2], P(('dp', 'expert')), may hold values from 0.05 to 1
- expert_ids: int32 [4096, 2], P(('dp', 'expert')), may hold values from 0 to 7, all different within a row; in each aligned block of 128 rows (0 to 127, 128 to 255, ...) at most 40 rows name the same one
- gate_up: bfloat16 [8, 2048, 1536], P('expert'), may hold values from -0.125 to 0.125
- down: bfloat16 [8, 768, 2048], P('expert'), may hold values from -0.21875 to 0.21875
Outputs:
- grad_probs: float32 [4096, 2], P(('dp', 'expert'))
- grad_gate_up: bfloat16 [8, 2048, 1536], P('expert', 'dp')
- grad_down: bfloat16 [8, 768, 2048], P('expert', None, 'dp')
The draws below stay inside these ranges and needn't reach their ends.
Inputs may be any that keep to these rules, and one draw needn't show every extreme that they name: `expert_ids`: each token names 2 different experts. Among the 128 rows of one device no expert is named more than 40 times, and in every draw some expert is named exactly 40 times by the rows of some device.
All inputs are finite; a program needn't handle non-finite values.
Results may differ from the reference program's by a relative error of at most 0.025.
Values may be sent and summed in bfloat16 or wider, within the bound.
No kernel may reach another device: no remote copies, remote signals or barrier semaphores. Data moves between devices by JAX's collectives and lax.ppermute only.
A program may use at most 128 MiB of HBM per device.

```python
import math
import jax
import jax.numpy as jnp
import numpy as np
from jax import lax

D = 2048
HID = 768
EXPERTS = 8
TOPK = 2
TOK_DEV = 128
CAP = 40
SLICES = 1
HD = 768
GROUPS = 4
GROUP_TOK = 1024
TOKENS = 4096
N_EXPERT = 8


def level_of(rng, extent, pieces, smallest, high):
    def one(position, blocks):
        steps = jax.random.uniform(jax.random.fold_in(jax.random.fold_in(rng, 6), position), (blocks,), jnp.float32, smallest / len(pieces), high / len(pieces))
        return jnp.repeat(jnp.exp(steps), extent[position] // blocks).reshape((-1,) + (1,) * (len(extent) - position - 1))

    level = one(*pieces[0])
    for cut in pieces[1:]:
        level = level * one(*cut)
    return level


def deal_out(rng, own, number, rows, number_of, top, reach, skew):
    order = jax.random.permutation(rng, number_of)
    packed, common = load_shares(number_of, rows * top, reach, skew, True), load_shares(number_of, rows * top, reach, skew, False)
    places = jnp.arange(number_of)

    def named(sizes, offset_by):
        used = int((sizes > 0).sum())
        fixed = max(1, used // 4)
        moved = fixed + (places - fixed + offset_by * (used - fixed)) % max(1, number_of - fixed)
        return jnp.zeros((number_of,), jnp.int32).at[order[jnp.where(places < fixed, places, moved)]].set(jnp.asarray(sizes, jnp.int32))

    sizes = jnp.where(number % 4 == 0, named(packed, number // 4), named(common, number - number // 4 - 1))
    mixed = jax.random.permutation(jax.random.fold_in(own, 3), number_of)
    giver, receiver = mixed[0:number_of // 2 * 2:2], mixed[1:number_of // 2 * 2:2]
    slack = jnp.minimum(sizes[giver] - 1, reach - sizes[receiver]) // 2
    slack = jnp.where((giver == order[0]) | (receiver == order[0]) | (sizes[receiver] == 0), 0, jnp.maximum(slack, 0))
    moved = jax.random.randint(jax.random.fold_in(own, 4), (number_of // 2,), 0, 1 << 20) % (slack + 1)
    sizes = sizes.at[giver].add(-moved).at[receiver].add(moved)
    members = jnp.searchsorted(jnp.cumsum(sizes), jnp.arange(rows * top), side="right").astype(jnp.int32)
    listing = members.reshape(top, rows).T
    listing = listing[jax.random.permutation(jax.random.fold_in(own, 1), rows)]
    offset_by = jax.random.randint(jax.random.fold_in(own, 2), (rows, 1), 0, top)
    return jnp.take_along_axis(listing, (jnp.arange(top)[None, :] + offset_by) % top, axis=1)


def load_shares(count, total, limit, skew, full):
    loads = [(1 << 20) // math.isqrt(grade ** skew) + 1 for grade in range(1, count + 1)]
    largest = limit if full else min(limit, max(-(-total // count), total * loads[0] // sum(loads)))
    least = 1 if total - largest >= count - 1 else 0
    given, spare = [largest] + [least] * (count - 1), total - largest - least * (count - 1)
    while spare > 0:
        free = [i for i in range(1, count) if given[i] < largest] or [i for i in range(1, count) if given[i] < limit]
        mass, remaining = sum([loads[i] for i in free]), spare
        for i in free:
            extra = min(limit - given[i], max(1, remaining * loads[i] // mass), spare)
            given[i] = given[i] + extra
            spare = spare - extra
    return np.array(given)


def noise(own_key, shape, scale, bound, cuts=(), kind=jnp.bfloat16):
    drawn = jax.random.normal(own_key, shape, jnp.float32) * scale
    if len(cuts) > 0:
        drawn = level_of(own_key, shape, cuts, -0.22, 0.18) * drawn
    return jnp.clip(drawn, min=-bound, max=bound).astype(kind)


def setup_inputs(seed: int = 0) -> dict:
    key_of = jax.random.split(jax.random.key(seed), 7)
    tokens = noise(key_of[0], (TOKENS, D), 1.0, 6.0, ((0, 32),))
    cotangent = noise(key_of[1], (TOKENS, D), 1.0, 6.0, ((0, 32),))
    gate_probs = jnp.clip(jnp.exp(math.log(1.0) - 2.9957323 * jax.random.uniform(key_of[2], (TOKENS, TOPK), jnp.float32) ** level_of(key_of[2], (TOKENS, TOPK), ((0, 32),), -0.2, 0.2)), 0.05, 1.0)
    expert_ids_keys = jax.random.split(jax.random.fold_in(key_of[3], 1), TOKENS // TOK_DEV)
    expert_ids_turns = jax.random.permutation(jax.random.fold_in(key_of[3], 3), TOKENS // TOK_DEV)
    expert_ids = jax.vmap(lambda own, number: deal_out(jax.random.fold_in(key_of[3], 2), own, number, TOK_DEV, EXPERTS, TOPK, CAP, 2))(expert_ids_keys, expert_ids_turns).reshape((TOKENS, TOPK))
    gate_up = noise(key_of[4], (N_EXPERT, D, 2 * HD), D ** -0.5, 0.125, ((0, 8),))
    down = noise(key_of[5], (N_EXPERT, HD, D), HID ** -0.5, 0.21875, ((0, 8),))
    return dict(tokens=tokens, cotangent=cotangent, gate_probs=gate_probs, expert_ids=expert_ids, gate_up=gate_up, down=down)


def expert_pass(rows_x, rows_dy, rows_p, gate_w, up_w, down_w):
    gate_pre = jnp.dot(rows_x, gate_w, preferred_element_type=jnp.float32)
    up_pre = jnp.dot(rows_x, up_w, preferred_element_type=jnp.float32)
    activated = jax.nn.silu(gate_pre)
    hidden = (activated * up_pre).astype(jnp.bfloat16)
    expert_out = jnp.dot(hidden, down_w, preferred_element_type=jnp.float32)
    dy_wide = rows_dy.astype(jnp.float32)
    inner = jnp.sum(expert_out * dy_wide, axis=1)
    scaled = (rows_p[:, None] * dy_wide).astype(jnp.bfloat16)
    grad_down = lax.dot_general(hidden, scaled, (((0,), (0,)), ((), ())), preferred_element_type=jnp.float32)
    grad_hidden = lax.dot_general(scaled, down_w, (((1,), (1,)), ((), ())), preferred_element_type=jnp.float32)
    sigmoid_gate = jax.nn.sigmoid(gate_pre)
    grad_gate_pre = (grad_hidden * up_pre * sigmoid_gate * (1.0 + gate_pre * (1.0 - sigmoid_gate))).astype(jnp.bfloat16)
    grad_up_pre = (grad_hidden * activated).astype(jnp.bfloat16)
    grad_gate = lax.dot_general(rows_x, grad_gate_pre, (((0,), (0,)), ((), ())), preferred_element_type=jnp.float32)
    grad_up = lax.dot_general(rows_x, grad_up_pre, (((0,), (0,)), ((), ())), preferred_element_type=jnp.float32)
    return grad_gate, grad_up, grad_down, inner


def rounded(values):
    return lax.optimization_barrier(values.astype(jnp.bfloat16)).astype(jnp.float32)


def reference(tokens, cotangent, gate_probs, expert_ids, gate_up, down):
    blocks = gate_up.reshape(EXPERTS, SLICES, D, 2, HD)
    gate_all = jnp.transpose(blocks[:, :, :, 0, :], (0, 2, 1, 3)).reshape(EXPERTS, D, HID)
    up_all = jnp.transpose(blocks[:, :, :, 1, :], (0, 2, 1, 3)).reshape(EXPERTS, D, HID)
    down_all = down.reshape(EXPERTS, HID, D)
    assigns = GROUP_TOK * TOPK
    buffer_rows = N_EXPERT * CAP

    def group_step(carry, group):
        acc_gate, acc_up, acc_down = carry
        group_x, group_dy, group_p, group_ids = group
        flat_ids = group_ids.reshape(-1).astype(jnp.int32)
        flat_p = group_p.reshape(-1)
        order = jnp.argsort(flat_ids, stable=True).astype(jnp.int32)
        counts = jnp.sum((flat_ids[:, None] == jnp.arange(EXPERTS, dtype=jnp.int32)[None, :]).astype(jnp.int32), axis=0)
        starts = (jnp.cumsum(counts) - counts).astype(jnp.int32)
        order_pad = jnp.concatenate([order, jnp.zeros((buffer_rows,), jnp.int32)])
        sorted_ids = jnp.concatenate([flat_ids[order], jnp.full((buffer_rows,), -1, jnp.int32)])
        grad_p = jnp.zeros((assigns,), jnp.float32)
        for expert in range(EXPERTS):
            index_rows = lax.dynamic_slice(order_pad, (starts[expert],), (buffer_rows,))
            valid = lax.dynamic_slice(sorted_ids, (starts[expert],), (buffer_rows,)) == expert
            token_rows = index_rows // TOPK
            rows_x = jnp.where(valid[:, None], group_x[token_rows], jnp.zeros((), jnp.bfloat16))
            rows_dy = jnp.where(valid[:, None], group_dy[token_rows], jnp.zeros((), jnp.bfloat16))
            rows_p = jnp.where(valid, flat_p[index_rows], jnp.zeros((), jnp.float32))
            grad_gate, grad_up, grad_down, inner = expert_pass(rows_x, rows_dy, rows_p, gate_all[expert], up_all[expert], down_all[expert])
            acc_gate = acc_gate.at[expert].add(rounded(grad_gate))
            acc_up = acc_up.at[expert].add(rounded(grad_up))
            acc_down = acc_down.at[expert].add(rounded(grad_down))
            grad_p = grad_p.at[jnp.where(valid, index_rows, 0)].add(jnp.where(valid, inner, jnp.zeros((), jnp.float32)))
        return (acc_gate, acc_up, acc_down), grad_p

    init = (jnp.zeros((EXPERTS, D, HID), jnp.float32), jnp.zeros((EXPERTS, D, HID), jnp.float32), jnp.zeros((EXPERTS, HID, D), jnp.float32))
    groups = (tokens.reshape(GROUPS, GROUP_TOK, D), cotangent.reshape(GROUPS, GROUP_TOK, D), gate_probs.reshape(GROUPS, GROUP_TOK, TOPK), expert_ids.reshape(GROUPS, GROUP_TOK, TOPK))
    (acc_gate, acc_up, acc_down), grad_p = lax.scan(group_step, init, groups)
    grad_probs = grad_p.reshape(TOKENS, TOPK)
    gate_part = acc_gate.reshape(EXPERTS, D, SLICES, HD)
    up_part = acc_up.reshape(EXPERTS, D, SLICES, HD)
    joined = jnp.stack([gate_part, up_part], axis=3)
    joined = jnp.transpose(joined, (0, 2, 1, 3, 4)).reshape(N_EXPERT, D, 2 * HD)
    grad_gate_up = joined.astype(jnp.bfloat16)
    grad_down = acc_down.reshape(N_EXPERT, HD, D).astype(jnp.bfloat16)
    return grad_probs, grad_gate_up, grad_down
```

```python
import functools

import jax
import jax.numpy as jnp
from jax import lax
from jax.experimental import pallas as pl
from jax.experimental.pallas import tpu as pltpu
from jax.sharding import PartitionSpec as P

EXPERTS = 8
CAP = 40
VMEM_LIMIT = 56 * 1024 * 1024
BF16 = jnp.bfloat16
F32 = jnp.float32


def dispatch_kernel(ids_ref, probs_ref, x_ref, dy_ref, *outs):
    row_refs, slot_ref = outs[:-1], outs[-1]
    me = lax.axis_index("expert")
    tok = x_ref.shape[0]
    width = x_ref.shape[1]
    numbers = lax.broadcasted_iota(jnp.int32, (EXPERTS, tok), 0)
    first = jnp.bitwise_xor(ids_ref[0:1, :], me) == numbers
    second = jnp.bitwise_xor(ids_ref[1:2, :], me) == numbers
    either = jnp.where(first | second, 1.0, 0.0)
    prob = jnp.where(first, probs_ref[0:1, :], 0.0) + jnp.where(second, probs_ref[1:2, :], 0.0)
    before = jnp.where(
        lax.broadcasted_iota(jnp.int32, (tok, tok), 0)
        < lax.broadcasted_iota(jnp.int32, (tok, tok), 1),
        1.0,
        0.0,
    )
    position = jnp.dot(either.astype(BF16), before.astype(BF16), preferred_element_type=F32)
    slot = position.astype(jnp.int32) + numbers * CAP
    slot_ref[0:1, :] = jnp.sum(jnp.where(first, slot, 0), axis=0, keepdims=True)
    slot_ref[1:2, :] = jnp.sum(jnp.where(second, slot, 0), axis=0, keepdims=True)
    target = jnp.where(either > 0.5, position, -1.0)
    places = lax.broadcasted_iota(jnp.int32, (CAP, tok), 0).astype(F32)
    picks = [
        jnp.where(places == target[e : e + 1, :], 1.0, 0.0) for e in range(EXPERTS)
    ]
    row_prob = [
        jnp.sum(picks[e] * prob[e : e + 1, :], axis=1, keepdims=True) for e in range(EXPERTS)
    ]
    pick = jnp.concatenate(picks, axis=0).astype(BF16)
    step = 512
    for at in range(0, width, step):
        rows_x = jnp.dot(pick, x_ref[:, at : at + step], preferred_element_type=F32)
        rows_dy = jnp.dot(pick, dy_ref[:, at : at + step], preferred_element_type=F32)
        for e in range(EXPERTS):
            part = slice(e * CAP, (e + 1) * CAP)
            row_refs[e][:, at : at + step] = rows_x[part].astype(BF16)
            row_refs[e][:, width + at : width + at + step] = (row_prob[e] * rows_dy[part]).astype(
                BF16
            )


def dispatch_rows(ids, probs, tokens, cotangent):
    tok, width = tokens.shape
    return pl.pallas_call(
        dispatch_kernel,
        out_shape=[jax.ShapeDtypeStruct((CAP, 2 * width), BF16)] * EXPERTS
        + [jax.ShapeDtypeStruct((2, tok), jnp.int32)],
        compiler_params=pltpu.CompilerParams(vmem_limit_bytes=VMEM_LIMIT),
        cost_estimate=pl.CostEstimate(
            flops=4 * EXPERTS * CAP * tok * width, bytes_accessed=4_000_000, transcendentals=0
        ),
        name="dispatch_rows",
    )(ids, probs, tokens, cotangent)


def expert_kernel(a_ref, b_ref, gate_ref, up_ref, down_ref, *rest):
    groups = len(rest) - 4
    message_refs, inner_ref, x_rows, s_rows, total = rest[:groups], *rest[groups:]
    width = gate_ref.shape[0]
    tile = gate_ref.shape[1]
    half = tile * pl.num_programs(0)
    quarter = width // groups
    factors = message_refs[0].shape[1] - 2 * quarter
    step = pl.program_id(0)
    group = lax.axis_index("dp")

    @pl.when(step == 0)
    def _():
        for rows, start in ((x_rows, 0), (s_rows, width)):
            rows[...] = jnp.concatenate(
                [
                    a_ref[:, start : start + width].astype(F32),
                    b_ref[:, start : start + width].astype(F32),
                ],
                axis=0,
            ).astype(BF16)
        for m in range(groups):
            at = pl.multiple_of(jnp.bitwise_xor(group, m) * quarter, quarter)
            message_refs[m][:, factors : factors + quarter] = x_rows[:, pl.ds(at, quarter)]
            message_refs[m][:, factors + quarter :] = s_rows[:, pl.ds(at, quarter)]
        total[...] = jnp.zeros_like(total)

    x, s = x_rows[...], s_rows[...]
    gate = jnp.dot(x, gate_ref[...], preferred_element_type=F32)
    up = jnp.dot(x, up_ref[...], preferred_element_type=F32)
    grad_hidden = lax.dot_general(
        s, down_ref[...], (((1,), (1,)), ((), ())), preferred_element_type=F32
    )
    sigmoid = 1.0 / (1.0 + jnp.exp(-gate))
    activated = gate * sigmoid
    hidden = (activated * up).astype(BF16)
    grad_gate = (grad_hidden * up * sigmoid * (1.0 + gate * (1.0 - sigmoid))).astype(BF16)
    grad_up = (grad_hidden * activated).astype(BF16)
    total[...] += jnp.sum(hidden.astype(F32) * grad_hidden, axis=1, keepdims=True)
    for part, values in enumerate((grad_gate, grad_up, hidden)):
        at = pl.multiple_of(part * half + step * tile, tile)
        for message in message_refs:
            message[:, pl.ds(at, tile)] = values

    @pl.when(step == pl.num_programs(0) - 1)
    def _():
        inner_ref[...] = total[...]


def expert_rows(rows_a, rows_b, weight_gu, weight_down, groups):
    width, both = weight_gu.shape
    half = both // 2
    tile = 256
    steps = half // tile
    count = 2 * CAP
    message = jax.ShapeDtypeStruct((count, 3 * half + 2 * (width // groups)), BF16)

    def whole(shape):
        return pl.BlockSpec(shape, lambda h: (0, 0))

    return pl.pallas_call(
        expert_kernel,
        grid=(steps,),
        in_specs=[
            whole(rows_a.shape),
            whole(rows_b.shape),
            pl.BlockSpec((width, tile), lambda h: (0, h)),
            pl.BlockSpec((width, tile), lambda h: (0, h + steps)),
            pl.BlockSpec((tile, width), lambda h: (h, 0)),
        ],
        out_specs=[whole(message.shape)] * groups + [whole((count, 1))],
        out_shape=[message] * groups + [jax.ShapeDtypeStruct((count, 1), F32)],
        scratch_shapes=[
            pltpu.VMEM((count, width), BF16),
            pltpu.VMEM((count, width), BF16),
            pltpu.VMEM((count, 1), F32),
        ],
        compiler_params=pltpu.CompilerParams(vmem_limit_bytes=VMEM_LIMIT),
        cost_estimate=pl.CostEstimate(
            flops=2 * 256 * width * 3 * half * 2,
            bytes_accessed=2 * width * 3 * half,
            transcendentals=count * half,
        ),
        name="expert_rows",
    )(rows_a, rows_b, weight_gu, weight_gu, weight_down)


def gradient_kernel(pieces, half, final, *refs):
    piece_refs = refs[:pieces]
    if final:
        acc_gu, acc_down, out_gu, out_down, rows, turned, sems = refs[pieces:]
    else:
        out_gu, out_down, rows, turned, sems = refs[pieces:]
    count = piece_refs[0].shape[0]
    quarter = out_gu.shape[0]
    copies = [
        pltpu.make_async_copy(ref, rows.at[pl.ds(n * count, count), :], sems.at[n])
        for n, ref in enumerate(piece_refs)
    ]
    for copy in copies:
        copy.start()
    for copy in copies:
        copy.wait()
    factors = 3 * half
    tile = 256
    turned[...] = rows[:, factors : factors + quarter].T
    for at in range(0, 2 * half, tile):
        grad = jnp.dot(turned[...], rows[:, at : at + tile], preferred_element_type=F32)
        if final:
            grad = grad + acc_gu[:, at : at + tile]
        out_gu[:, at : at + tile] = grad.astype(out_gu.dtype)
    for at in range(0, half, tile):
        grad = jnp.dot(
            rows[:, 2 * half + at : 2 * half + at + tile].T,
            rows[:, factors + quarter :],
            preferred_element_type=F32,
        )
        if final:
            grad = grad + acc_down[at : at + tile, :]
        out_down[at : at + tile, :] = grad.astype(out_down.dtype)


def gradients(pieces, half, quarter, sums=None):
    final = sums is not None
    kept = BF16 if final else F32
    count, message = pieces[0].shape
    rows = count * len(pieces)
    vmem = pl.BlockSpec(memory_space=pltpu.VMEM)
    return pl.pallas_call(
        functools.partial(gradient_kernel, len(pieces), half, final),
        in_specs=[pl.BlockSpec(memory_space=pl.ANY)] * len(pieces) + ([vmem] * 2 if final else []),
        out_specs=[vmem] * 2,
        out_shape=[
            jax.ShapeDtypeStruct((quarter, 2 * half), kept),
            jax.ShapeDtypeStruct((half, quarter), kept),
        ],
        scratch_shapes=[
            pltpu.VMEM((rows, message), BF16),
            pltpu.VMEM((quarter, rows), BF16),
            pltpu.SemaphoreType.DMA((len(pieces),)),
        ],
        compiler_params=pltpu.CompilerParams(vmem_limit_bytes=VMEM_LIMIT),
        cost_estimate=pl.CostEstimate(
            flops=2 * rows * quarter * 3 * half,
            bytes_accessed=2 * rows * message,
            transcendentals=0,
        ),
        name="gradients",
    )(*pieces, *(sums or ()))


def exchange(values, axis, mask):
    size = lax.axis_size(axis)
    return lax.ppermute(values, axis, [(n, n ^ mask) for n in range(size)])


def plane_body(tokens, cotangent, gate_probs, expert_ids, gate_up, down):
    groups = lax.axis_size("dp")
    me = lax.axis_index("expert")
    half = gate_up.shape[2] // 2
    quarter = tokens.shape[1] // groups
    ids, probs = expert_ids.T, gate_probs.T
    *local, slots = dispatch_rows(ids, probs, tokens, cotangent)
    arrived = [local[0]] + [exchange(local[k], "expert", k) for k in range(1, EXPERTS)]
    pieces, inner = [], []
    for chunk in range(EXPERTS // 2):
        *messages, chunk_inner = expert_rows(
            arrived[2 * chunk], arrived[2 * chunk + 1], gate_up[0], down[0], groups
        )
        inner.append(chunk_inner.reshape(-1))
        pieces.append(
            [messages[0]] + [exchange(messages[m], "dp", m) for m in range(1, groups)]
        )
    early = [piece for chunk in pieces[:-1] for piece in chunk]
    sums = gradients(early, half, quarter)
    grad_gu, grad_down = gradients(pieces[-1], half, quarter, tuple(sums))
    gathered = lax.all_gather(jnp.concatenate(inner), "expert").reshape(EXPERTS, EXPERTS, CAP)
    numbers = jnp.arange(EXPERTS, dtype=jnp.int32)
    mine = numbers[:, None] == jnp.bitwise_xor(numbers, me)[None, :]
    returned = jnp.sum(jnp.where(mine[:, :, None], gathered, 0.0), axis=0).reshape(-1)
    chosen = slots[:, None, :] == jnp.arange(EXPERTS * CAP, dtype=jnp.int32)[None, :, None]
    grad_probs = jnp.sum(jnp.where(chosen, returned[None, :, None], 0.0), axis=1) / probs
    return (grad_probs.T, grad_gu[None], grad_down[None])


def widen(values, slices, expert_count):
    tail = values.shape[1:]
    spread = values.reshape((EXPERTS, 1, CAP) + tail)
    spread = jnp.broadcast_to(spread, (EXPERTS, slices, CAP) + tail)
    return spread.reshape((expert_count, CAP) + tail)


def swap(values):
    return lax.all_to_all(values, "expert", split_axis=0, concat_axis=0, tiled=True)


def sliced_body(tokens, cotangent, gate_probs, expert_ids, gate_up, down):
    expert_count = lax.axis_size("expert")
    slices = expert_count // EXPERTS
    tok_count, width = tokens.shape
    choose_count = expert_ids.shape[1]
    half = gate_up.shape[2] // 2
    slot_rows = EXPERTS * CAP
    flat_ids = expert_ids.reshape(-1)
    choose = (flat_ids[:, None] == jnp.arange(EXPERTS, dtype=jnp.int32)[None, :]).astype(jnp.int32)
    earlier = jnp.cumsum(choose, axis=0) - choose
    slot_of = flat_ids * CAP + jnp.sum(earlier * choose, axis=1)
    picked = jnp.arange(slot_rows, dtype=jnp.int32)[:, None] == slot_of[None, :]
    picked_tok = jnp.any(picked.reshape(slot_rows, tok_count, choose_count), axis=2).astype(BF16)
    slot_prob = jnp.sum(jnp.where(picked, gate_probs.reshape(-1)[None, :], 0.0), axis=1)
    local_x = jnp.dot(picked_tok, tokens, preferred_element_type=F32).astype(BF16)
    local_dy = jnp.dot(picked_tok, cotangent, preferred_element_type=F32)
    local_scaled = (slot_prob[:, None] * local_dy).astype(BF16)
    rows_x = swap(widen(local_x, slices, expert_count)).reshape(-1, width)
    rows_s = swap(widen(local_scaled, slices, expert_count)).reshape(-1, width)
    both = jnp.dot(rows_x, gate_up[0], preferred_element_type=F32)
    gate, up = both[:, :half], both[:, half:]
    sigmoid = jax.nn.sigmoid(gate)
    activated = gate * sigmoid
    hidden = (activated * up).astype(BF16)
    grad_hidden = lax.dot_general(
        rows_s, down[0], (((1,), (1,)), ((), ())), preferred_element_type=F32
    )
    inner = jnp.sum(hidden.astype(F32) * grad_hidden, axis=1)
    grad_gate = (grad_hidden * up * sigmoid * (1.0 + gate * (1.0 - sigmoid))).astype(BF16)
    grad_up = (grad_hidden * activated).astype(BF16)
    grad_both = jnp.concatenate([grad_gate, grad_up], axis=1)
    over_rows = (((0,), (0,)), ((), ()))
    grad_gu = lax.dot_general(rows_x, grad_both, over_rows, preferred_element_type=F32)
    grad_down = lax.dot_general(hidden, rows_s, over_rows, preferred_element_type=F32)
    returned = swap(inner.reshape(expert_count, CAP))
    per_slot = jnp.sum(returned.reshape(EXPERTS, slices, CAP), axis=1).reshape(slot_rows)
    grad_probs = jnp.sum(jnp.where(picked, per_slot[:, None], 0.0), axis=0)
    grad_probs = grad_probs.reshape(tok_count, choose_count) / gate_probs
    reduced_gu = lax.psum_scatter(grad_gu.astype(BF16), "dp", scatter_dimension=0, tiled=True)
    reduced_down = lax.psum_scatter(grad_down.astype(BF16), "dp", scatter_dimension=1, tiled=True)
    return (grad_probs, reduced_gu[None], reduced_down[None])


def solution(mesh):
    whole_experts = mesh.shape["expert"] == EXPERTS and mesh.shape["dp"] == 4
    return jax.shard_map(
        plane_body if whole_experts else sliced_body,
        mesh=mesh,
        in_specs=(
            P(("dp", "expert"), None),
            P(("dp", "expert"), None),
            P(("dp", "expert"), None),
            P(("dp", "expert"), None),
            P("expert", None, None),
            P("expert", None, None),
        ),
        out_specs=(P(("dp", "expert"), None), P("expert", "dp", None), P("expert", None, "dp")),
        check_vma=False,
    )
```

```python
import functools

import jax
import jax.numpy as jnp
from jax import lax
from jax.experimental import pallas as pl
from jax.experimental.pallas import tpu as pltpu
from jax.sharding import PartitionSpec as P

EXPERTS = 8
CAP = 40
VMEM_LIMIT = 56 * 1024 * 1024
BF16 = jnp.bfloat16
F32 = jnp.float32


def dispatch_kernel(ids_ref, probs_ref, x_ref, dy_ref, *outs):
    row_refs, slot_ref = outs[:-1], outs[-1]
    me = lax.axis_index("expert")
    tok = x_ref.shape[0]
    width = x_ref.shape[1]
    numbers = lax.broadcasted_iota(jnp.int32, (EXPERTS, tok), 0)
    first = jnp.bitwise_xor(ids_ref[0:1, :], me) == numbers
    second = jnp.bitwise_xor(ids_ref[1:2, :], me) == numbers
    either = jnp.where(first | second, 1.0, 0.0)
    prob = jnp.where(first, probs_ref[0:1, :], 0.0) + jnp.where(second, probs_ref[1:2, :], 0.0)
    before = jnp.where(
        lax.broadcasted_iota(jnp.int32, (tok, tok), 0)
        < lax.broadcasted_iota(jnp.int32, (tok, tok), 1),
        1.0,
        0.0,
    )
    position = jnp.dot(either.astype(BF16), before.astype(BF16), preferred_element_type=F32)
    slot = position.astype(jnp.int32) + numbers * CAP
    slot_ref[0:1, :] = jnp.sum(jnp.where(first, slot, 0), axis=0, keepdims=True)
    slot_ref[1:2, :] = jnp.sum(jnp.where(second, slot, 0), axis=0, keepdims=True)
    target = jnp.where(either > 0.5, position, -1.0)
    places = lax.broadcasted_iota(jnp.int32, (CAP, tok), 0).astype(F32)
    picks = [
        jnp.where(places == target[e : e + 1, :], 1.0, 0.0) for e in range(EXPERTS)
    ]
    row_prob = [
        jnp.sum(picks[e] * prob[e : e + 1, :], axis=1, keepdims=True) for e in range(EXPERTS)
    ]
    pick = jnp.concatenate(picks, axis=0).astype(BF16)
    step = 512
    for at in range(0, width, step):
        rows_x = jnp.dot(pick, x_ref[:, at : at + step], preferred_element_type=F32)
        rows_dy = jnp.dot(pick, dy_ref[:, at : at + step], preferred_element_type=F32)
        for e in range(EXPERTS):
            part = slice(e * CAP, (e + 1) * CAP)
            row_refs[e][:, at : at + step] = rows_x[part].astype(BF16)
            row_refs[e][:, width + at : width + at + step] = (row_prob[e] * rows_dy[part]).astype(
                BF16
            )


def dispatch_rows(ids, probs, tokens, cotangent):
    tok, width = tokens.shape
    return pl.pallas_call(
        dispatch_kernel,
        out_shape=[jax.ShapeDtypeStruct((CAP, 2 * width), BF16)] * EXPERTS
        + [jax.ShapeDtypeStruct((2, tok), jnp.int32)],
        compiler_params=pltpu.CompilerParams(vmem_limit_bytes=VMEM_LIMIT),
        cost_estimate=pl.CostEstimate(
            flops=4 * EXPERTS * CAP * tok * width, bytes_accessed=4_000_000, transcendentals=0
        ),
        name="dispatch_rows",
    )(ids, probs, tokens, cotangent)


def expert_kernel(parts, first, final, *refs):
    row_refs, (gate_ref, up_ref, down_ref), refs = refs[:parts], refs[parts : parts + 3], refs[parts + 3 :]
    if not first:
        (acc_gate, acc_up, acc_down), refs = refs[:3], refs[3:]
    if final:
        (out_both, out_down, inner_ref), refs = refs[:3], refs[3:]
    else:
        (out_gate, out_up, out_down, inner_ref), refs = refs[:4], refs[4:]
    x_rows, s_rows, x_turned, s_own, total = refs
    width, tile = gate_ref.shape
    quarter = out_down.shape[1]
    step = pl.program_id(0)

    @pl.when(step == 0)
    def _():
        own = pl.multiple_of(lax.axis_index("dp") * quarter, quarter)
        at = 0
        for ref in row_refs:
            count = ref.shape[0]
            x_rows[at : at + count, :] = ref[:, :width]
            s_rows[at : at + count, :] = ref[:, width:]
            at += count
        x_turned[...] = x_rows[:, pl.ds(own, quarter)].T
        s_own[...] = s_rows[:, pl.ds(own, quarter)]
        total[...] = jnp.zeros_like(total)

    x, s = x_rows[...], s_rows[...]
    gate = jnp.dot(x, gate_ref[...], preferred_element_type=F32)
    up = jnp.dot(x, up_ref[...], preferred_element_type=F32)
    grad_hidden = lax.dot_general(
        s, down_ref[...], (((1,), (1,)), ((), ())), preferred_element_type=F32
    )
    sigmoid = 1.0 / (1.0 + jnp.exp(-gate))
    activated = gate * sigmoid
    hidden = (activated * up).astype(BF16)
    grad_gate = (grad_hidden * up * sigmoid * (1.0 + gate * (1.0 - sigmoid))).astype(BF16)
    grad_up = (grad_hidden * activated).astype(BF16)
    total[...] += jnp.sum(hidden.astype(F32) * grad_hidden, axis=1, keepdims=True)
    sum_gate = jnp.dot(x_turned[...], grad_gate, preferred_element_type=F32)
    sum_up = jnp.dot(x_turned[...], grad_up, preferred_element_type=F32)
    sum_down = jnp.dot(hidden.T, s_own[...], preferred_element_type=F32)
    if not first:
        sum_gate, sum_up, sum_down = (
            sum_gate + acc_gate[...],
            sum_up + acc_up[...],
            sum_down + acc_down[...],
        )
    if final:
        at = pl.multiple_of(step * tile, tile)
        half = out_both.shape[1] // 2
        out_both[:, pl.ds(at, tile)] = sum_gate.astype(BF16)
        out_both[:, pl.ds(pl.multiple_of(half + at, tile), tile)] = sum_up.astype(BF16)
    else:
        out_gate[...] = sum_gate
        out_up[...] = sum_up
    out_down[...] = sum_down.astype(out_down.dtype)

    @pl.when(step == pl.num_programs(0) - 1)
    def _():
        inner_ref[...] = total[...]


def expert_rows(rows, weight_gu, weight_down, groups, sums=None, final=False):
    width, both = weight_gu.shape
    half = both // 2
    quarter = width // groups
    tile = 256
    steps = half // tile
    count = sum(part.shape[0] for part in rows)

    def whole(shape):
        return pl.BlockSpec(shape, lambda h: (0, 0))

    sum_specs = [
        pl.BlockSpec((quarter, tile), lambda h: (0, h)),
        pl.BlockSpec((quarter, tile), lambda h: (0, h)),
        pl.BlockSpec((tile, quarter), lambda h: (h, 0)),
    ]
    *sums_out, inner = pl.pallas_call(
        functools.partial(expert_kernel, len(rows), sums is None, final),
        grid=(steps,),
        in_specs=[whole(part.shape) for part in rows]
        + [
            pl.BlockSpec((width, tile), lambda h: (0, h)),
            pl.BlockSpec((width, tile), lambda h: (0, h + steps)),
            pl.BlockSpec((tile, width), lambda h: (h, 0)),
        ]
        + ([] if sums is None else sum_specs),
        out_specs=([whole((quarter, both))] if final else sum_specs[:2])
        + [sum_specs[2], whole((count, 1))],
        out_shape=(
            [jax.ShapeDtypeStruct((quarter, both), BF16)]
            if final
            else [jax.ShapeDtypeStruct((quarter, half), F32)] * 2
        )
        + [
            jax.ShapeDtypeStruct((half, quarter), BF16 if final else F32),
            jax.ShapeDtypeStruct((count, 1), F32),
        ],
        scratch_shapes=[
            pltpu.VMEM((count, width), BF16),
            pltpu.VMEM((count, width), BF16),
            pltpu.VMEM((quarter, count), BF16),
            pltpu.VMEM((count, quarter), BF16),
            pltpu.VMEM((count, 1), F32),
        ],
        compiler_params=pltpu.CompilerParams(vmem_limit_bytes=VMEM_LIMIT),
        cost_estimate=pl.CostEstimate(
            flops=2 * count * (width + quarter) * 3 * half,
            bytes_accessed=2 * width * 3 * half + 2 * 4 * quarter * 3 * half,
            transcendentals=count * half,
        ),
        name="expert_rows",
    )(*rows, weight_gu, weight_gu, weight_down, *(sums or ()))
    return sums_out, inner


def exchange(values, axis, mask):
    size = lax.axis_size(axis)
    return lax.ppermute(values, axis, [(n, n ^ mask) for n in range(size)])


def swap(values):
    return lax.all_to_all(values, "expert", split_axis=0, concat_axis=0, tiled=True)


def plane_body(tokens, cotangent, gate_probs, expert_ids, gate_up, down):
    groups = lax.axis_size("dp")
    group = lax.axis_index("dp")
    me = lax.axis_index("expert")
    ids, probs = expert_ids.T, gate_probs.T
    *local, slots = dispatch_rows(ids, probs, tokens, cotangent)
    arrived = [local[0]] + [exchange(local[k], "expert", k) for k in range(1, EXPERTS)]
    sums, inner = None, [None] * EXPERTS
    chunks = (((0,), (1,)), ((2, 3),), ((4, 5),), ((6,), (7,)))
    for number, chunk in enumerate(chunks):
        rows = []
        for part in chunk:
            values = [arrived[k] for k in part]
            values = values[0] if len(part) == 1 else jnp.concatenate(values, axis=0)
            rows.append(lax.all_gather(values, "dp", tiled=True))
        sums, found = expert_rows(
            rows, gate_up[0], down[0], groups, sums, number == len(chunks) - 1
        )
        at = 0
        for part in chunk:
            size = groups * len(part) * CAP
            own = lax.dynamic_index_in_dim(
                found[at : at + size].reshape(groups, len(part), CAP), group, 0, keepdims=False
            )
            at += size
            for n, k in enumerate(part):
                inner[k] = own[n]
    grad_gu, grad_down = sums
    numbers = jnp.arange(EXPERTS, dtype=jnp.int32)
    mine = (numbers[:, None] == jnp.bitwise_xor(numbers, me)[None, :])[:, :, None]
    sent = jnp.sum(jnp.where(mine, jnp.stack(inner)[None], 0.0), axis=1)
    returned = jnp.sum(jnp.where(mine, swap(sent)[None], 0.0), axis=1).reshape(-1)
    chosen = slots[:, None, :] == jnp.arange(EXPERTS * CAP, dtype=jnp.int32)[None, :, None]
    grad_probs = jnp.sum(jnp.where(chosen, returned[None, :, None], 0.0), axis=1) / probs
    return (grad_probs.T, grad_gu[None], grad_down[None])


def widen(values, slices, expert_count):
    tail = values.shape[1:]
    spread = values.reshape((EXPERTS, 1, CAP) + tail)
    spread = jnp.broadcast_to(spread, (EXPERTS, slices, CAP) + tail)
    return spread.reshape((expert_count, CAP) + tail)


def sliced_body(tokens, cotangent, gate_probs, expert_ids, gate_up, down):
    expert_count = lax.axis_size("expert")
    slices = expert_count // EXPERTS
    tok_count, width = tokens.shape
    choose_count = expert_ids.shape[1]
    half = gate_up.shape[2] // 2
    slot_rows = EXPERTS * CAP
    flat_ids = expert_ids.reshape(-1)
    choose = (flat_ids[:, None] == jnp.arange(EXPERTS, dtype=jnp.int32)[None, :]).astype(jnp.int32)
    earlier = jnp.cumsum(choose, axis=0) - choose
    slot_of = flat_ids * CAP + jnp.sum(earlier * choose, axis=1)
    picked = jnp.arange(slot_rows, dtype=jnp.int32)[:, None] == slot_of[None, :]
    picked_tok = jnp.any(picked.reshape(slot_rows, tok_count, choose_count), axis=2).astype(BF16)
    slot_prob = jnp.sum(jnp.where(picked, gate_probs.reshape(-1)[None, :], 0.0), axis=1)
    local_x = jnp.dot(picked_tok, tokens, preferred_element_type=F32).astype(BF16)
    local_dy = jnp.dot(picked_tok, cotangent, preferred_element_type=F32)
    local_scaled = (slot_prob[:, None] * local_dy).astype(BF16)
    rows_x = swap(widen(local_x, slices, expert_count)).reshape(-1, width)
    rows_s = swap(widen(local_scaled, slices, expert_count)).reshape(-1, width)
    both = jnp.dot(rows_x, gate_up[0], preferred_element_type=F32)
    gate, up = both[:, :half], both[:, half:]
    sigmoid = jax.nn.sigmoid(gate)
    activated = gate * sigmoid
    hidden = (activated * up).astype(BF16)
    grad_hidden = lax.dot_general(
        rows_s, down[0], (((1,), (1,)), ((), ())), preferred_element_type=F32
    )
    inner = jnp.sum(hidden.astype(F32) * grad_hidden, axis=1)
    grad_gate = (grad_hidden * up * sigmoid * (1.0 + gate * (1.0 - sigmoid))).astype(BF16)
    grad_up = (grad_hidden * activated).astype(BF16)
    grad_both = jnp.concatenate([grad_gate, grad_up], axis=1)
    over_rows = (((0,), (0,)), ((), ()))
    grad_gu = lax.dot_general(rows_x, grad_both, over_rows, preferred_element_type=F32)
    grad_down = lax.dot_general(hidden, rows_s, over_rows, preferred_element_type=F32)
    returned = swap(inner.reshape(expert_count, CAP))
    per_slot = jnp.sum(returned.reshape(EXPERTS, slices, CAP), axis=1).reshape(slot_rows)
    grad_probs = jnp.sum(jnp.where(picked, per_slot[:, None], 0.0), axis=0)
    grad_probs = grad_probs.reshape(tok_count, choose_count) / gate_probs
    reduced_gu = lax.psum_scatter(grad_gu.astype(BF16), "dp", scatter_dimension=0, tiled=True)
    reduced_down = lax.psum_scatter(grad_down.astype(BF16), "dp", scatter_dimension=1, tiled=True)
    return (grad_probs, reduced_gu[None], reduced_down[None])


def solution(mesh):
    whole_experts = mesh.shape["expert"] == EXPERTS and mesh.shape["dp"] == 4
    return jax.shard_map(
        plane_body if whole_experts else sliced_body,
        mesh=mesh,
        in_specs=(
            P(("dp", "expert"), None),
            P(("dp", "expert"), None),
            P(("dp", "expert"), None),
            P(("dp", "expert"), None),
            P("expert", None, None),
            P("expert", None, None),
        ),
        out_specs=(P(("dp", "expert"), None), P("expert", "dp", None), P("expert", None, "dp")),
        check_vma=False,
    )
```

```python
import functools

import jax
import jax.numpy as jnp
from jax import lax
from jax.experimental import pallas as pl
from jax.experimental.pallas import tpu as pltpu
from jax.sharding import PartitionSpec as P

EXPERTS = 8
CAP = 40
PAIR = 2 * CAP
TILE = 256
VMEM_LIMIT = 56 * 1024 * 1024
BF16 = jnp.bfloat16
F32 = jnp.float32


def dispatch_kernel(ids_ref, probs_ref, x_ref, dy_ref, *outs):
    row_refs, slot_ref = outs[:-1], outs[-1]
    me = lax.axis_index("expert")
    tok = x_ref.shape[0]
    width = x_ref.shape[1]
    numbers = lax.broadcasted_iota(jnp.int32, (EXPERTS, tok), 0)
    first = jnp.bitwise_xor(ids_ref[0:1, :], me) == numbers
    second = jnp.bitwise_xor(ids_ref[1:2, :], me) == numbers
    either = jnp.where(first | second, 1.0, 0.0)
    prob = jnp.where(first, probs_ref[0:1, :], 0.0) + jnp.where(second, probs_ref[1:2, :], 0.0)
    before = jnp.where(
        lax.broadcasted_iota(jnp.int32, (tok, tok), 0)
        < lax.broadcasted_iota(jnp.int32, (tok, tok), 1),
        1.0,
        0.0,
    )
    position = jnp.dot(either.astype(BF16), before.astype(BF16), preferred_element_type=F32)
    slot = position.astype(jnp.int32) + numbers * CAP
    slot_ref[0:1, :] = jnp.sum(jnp.where(first, slot, 0), axis=0, keepdims=True)
    slot_ref[1:2, :] = jnp.sum(jnp.where(second, slot, 0), axis=0, keepdims=True)
    target = jnp.where(either > 0.5, position, -1.0)
    places = lax.broadcasted_iota(jnp.int32, (CAP, tok), 0).astype(F32)
    picks = [
        jnp.where(places == target[e : e + 1, :], 1.0, 0.0) for e in range(EXPERTS)
    ]
    row_prob = jnp.concatenate(
        [jnp.sum(picks[e] * prob[e : e + 1, :], axis=1, keepdims=True) for e in range(EXPERTS)],
        axis=0,
    )
    pick = jnp.concatenate(picks, axis=0).astype(BF16)
    step = 512
    for at in range(0, width, step):
        rows_x = jnp.dot(pick, x_ref[:, at : at + step], preferred_element_type=F32)
        rows_dy = jnp.dot(pick, dy_ref[:, at : at + step], preferred_element_type=F32)
        scaled = row_prob * rows_dy
        for pair, ref in enumerate(row_refs):
            part = slice(pair * PAIR, (pair + 1) * PAIR)
            ref[:, at : at + step] = rows_x[part].astype(BF16)
            ref[:, width + at : width + at + step] = scaled[part].astype(BF16)


def dispatch_rows(ids, probs, tokens, cotangent):
    tok, width = tokens.shape
    return pl.pallas_call(
        dispatch_kernel,
        out_shape=[jax.ShapeDtypeStruct((PAIR, 2 * width), BF16)] * (EXPERTS // 2)
        + [jax.ShapeDtypeStruct((2, tok), jnp.int32)],
        compiler_params=pltpu.CompilerParams(vmem_limit_bytes=VMEM_LIMIT),
        cost_estimate=pl.CostEstimate(
            flops=4 * EXPERTS * CAP * tok * width, bytes_accessed=4_000_000, transcendentals=0
        ),
        name="dispatch_rows",
    )(ids, probs, tokens, cotangent)


def split_rows(top, half):
    blocks = 3 * half // TILE
    low = PAIR - top
    return blocks, low, (blocks + 4) * top, (blocks + 4) * low


def expert_kernel(top, a_ref, b_ref, gate_ref, up_ref, down_ref, *rest):
    own_ref, to_x, to_y, inner_ref, x_rows, s_rows, total = rest
    width = gate_ref.shape[0]
    steps = pl.num_programs(0)
    half = TILE * 3
    quarter = width // 4
    blocks, low, from_x, from_y = split_rows(top, half)
    step = pl.program_id(0)
    group = lax.axis_index("dp")

    @pl.when(step == 0)
    def _():
        for rows, start in ((x_rows, 0), (s_rows, width)):
            rows[...] = jnp.concatenate(
                [
                    a_ref[:CAP, start : start + width].astype(F32),
                    b_ref[:, start : start + width].astype(F32),
                ],
                axis=0,
            ).astype(BF16)
        for q in range(4):
            rows = (x_rows, s_rows)[q // 2]

            def cut(mask):
                at = jnp.bitwise_xor(group, mask) * quarter + q % 2 * TILE
                return rows[:, pl.ds(pl.multiple_of(at, TILE), TILE)]

            at = blocks + q
            own_ref[at * PAIR : (at + 1) * PAIR] = cut(0)
            far = cut(3)
            to_x[at * top : (at + 1) * top] = far[:top]
            to_y[at * low : (at + 1) * low] = far[top:]
            start = from_x + blocks * low + q * PAIR
            to_x[start : start + PAIR] = cut(1)
            start = from_y + blocks * top + q * PAIR
            to_y[start : start + PAIR] = cut(2)
        total[...] = jnp.zeros_like(total)

    x, s = x_rows[...], s_rows[...]
    gate = jnp.dot(x, gate_ref[...], preferred_element_type=F32)
    up = jnp.dot(x, up_ref[...], preferred_element_type=F32)
    grad_hidden = lax.dot_general(
        s, down_ref[...], (((1,), (1,)), ((), ())), preferred_element_type=F32
    )
    sigmoid = 1.0 / (1.0 + jnp.exp(-gate))
    activated = gate * sigmoid
    hidden = (activated * up).astype(BF16)
    grad_gate = (grad_hidden * up * sigmoid * (1.0 + gate * (1.0 - sigmoid))).astype(BF16)
    grad_up = (grad_hidden * activated).astype(BF16)
    total[...] += jnp.sum(hidden.astype(F32) * grad_hidden, axis=1, keepdims=True)
    for part, values in enumerate((grad_gate, grad_up, hidden)):
        block = part * steps + step

        def rows_at(start, count):
            return pl.ds(pl.multiple_of(start + block * count, 16), count)

        own_ref[rows_at(0, PAIR)] = values
        to_x[rows_at(0, top)] = values[:top]
        to_x[rows_at(from_x, low)] = values[top:]
        to_y[rows_at(0, low)] = values[top:]
        to_y[rows_at(from_y, top)] = values[:top]

    @pl.when(step == steps - 1)
    def _():
        inner_ref[...] = jnp.broadcast_to(total[...], (PAIR, 128)).T[0:1]


def expert_rows(rows_a, rows_b, weight_gu, weight_down, top):
    width, both = weight_gu.shape
    half = both // 2
    steps = half // TILE
    blocks, low, from_x, from_y = split_rows(top, half)
    shapes = [
        ((blocks + 4) * PAIR, TILE),
        (from_x + blocks * low + 4 * PAIR, TILE),
        (from_y + blocks * top + 4 * PAIR, TILE),
    ]

    def whole(shape):
        return pl.BlockSpec(shape, lambda h: (0, 0))

    return pl.pallas_call(
        functools.partial(expert_kernel, top),
        grid=(steps,),
        in_specs=[
            whole(rows_a.shape),
            whole(rows_b.shape),
            pl.BlockSpec((width, TILE), lambda h: (0, h)),
            pl.BlockSpec((width, TILE), lambda h: (0, h + steps)),
            pl.BlockSpec((TILE, width), lambda h: (h, 0)),
        ],
        out_specs=[whole(shape) for shape in shapes] + [whole((1, PAIR))],
        out_shape=[jax.ShapeDtypeStruct(shape, BF16) for shape in shapes]
        + [jax.ShapeDtypeStruct((1, PAIR), F32)],
        scratch_shapes=[
            pltpu.VMEM((PAIR, width), BF16),
            pltpu.VMEM((PAIR, width), BF16),
            pltpu.VMEM((PAIR, 1), F32),
        ],
        compiler_params=pltpu.CompilerParams(vmem_limit_bytes=VMEM_LIMIT),
        cost_estimate=pl.CostEstimate(
            flops=2 * 256 * width * 3 * half * 2,
            bytes_accessed=2 * width * 3 * half,
            transcendentals=PAIR * half,
        ),
        name="expert_rows",
    )(rows_a, rows_b, weight_gu, weight_gu, weight_down)


def gradient_kernel(tops, half, final, *refs):
    groups, refs = [refs[5 * n : 5 * n + 5] for n in range(len(tops))], refs[5 * len(tops) :]
    if final:
        (acc_gu, acc_down), refs = refs[:2], refs[2:]
    out_gu, out_down, turned, s_rows = refs
    both = 2 * half // TILE

    def factor(block):
        parts = []
        for top, (own, got_x, got_y, far_top, far_low) in zip(tops, groups):
            _, low, from_x, from_y = split_rows(top, half)
            parts += [
                own[block * PAIR : (block + 1) * PAIR],
                got_x[block * top : (block + 1) * top],
                got_x[from_x + block * low : from_x + (block + 1) * low],
                got_y[from_y + block * top : from_y + (block + 1) * top],
                got_y[block * low : (block + 1) * low],
                far_top[block * top : (block + 1) * top],
                far_low[block * low : (block + 1) * low],
            ]
        return jnp.concatenate(parts, axis=0)

    def piece(q):
        parts = []
        for top, (own, got_x, got_y, far_top, far_low) in zip(tops, groups):
            blocks, low, from_x, from_y = split_rows(top, half)
            block = blocks + q
            at_x = from_x + blocks * low + q * PAIR
            at_y = from_y + blocks * top + q * PAIR
            parts += [
                own[block * PAIR : (block + 1) * PAIR],
                got_x[at_x : at_x + PAIR],
                got_y[at_y : at_y + PAIR],
                far_top[block * top : (block + 1) * top],
                far_low[block * low : (block + 1) * low],
            ]
        return jnp.concatenate(parts, axis=0)

    for q in range(2):
        turned[q * TILE : (q + 1) * TILE, :] = piece(q).T
        s_rows[:, q * TILE : (q + 1) * TILE] = piece(2 + q)
    for block in range(both):
        at = slice(block * TILE, (block + 1) * TILE)
        grad = jnp.dot(turned[...], factor(block), preferred_element_type=F32)
        if final:
            grad = grad + acc_gu[:, at]
        out_gu[:, at] = grad.astype(out_gu.dtype)
    for block in range(half // TILE):
        at = slice(block * TILE, (block + 1) * TILE)
        grad = jnp.dot(factor(both + block).T, s_rows[...], preferred_element_type=F32)
        if final:
            grad = grad + acc_down[at, :]
        out_down[at, :] = grad.astype(out_down.dtype)


def gradients(tops, pieces, half, quarter, sums=None):
    final = sums is not None
    kept = BF16 if final else F32
    rows = 4 * PAIR * len(tops)
    vmem = pl.BlockSpec(memory_space=pltpu.VMEM)
    return pl.pallas_call(
        functools.partial(gradient_kernel, tops, half, final),
        in_specs=[vmem] * (len(pieces) + (2 if final else 0)),
        out_specs=[vmem] * 2,
        out_shape=[
            jax.ShapeDtypeStruct((quarter, 2 * half), kept),
            jax.ShapeDtypeStruct((half, quarter), kept),
        ],
        scratch_shapes=[pltpu.VMEM((quarter, rows), BF16), pltpu.VMEM((rows, quarter), BF16)],
        compiler_params=pltpu.CompilerParams(vmem_limit_bytes=VMEM_LIMIT),
        cost_estimate=pl.CostEstimate(
            flops=2 * rows * quarter * 3 * half,
            bytes_accessed=2 * rows * (3 * half + 2 * quarter),
            transcendentals=0,
        ),
        name="gradients",
    )(*pieces, *(sums or ()))


def exchange(values, axis, mask):
    size = lax.axis_size(axis)
    return lax.ppermute(values, axis, [(n, n ^ mask) for n in range(size)])


def swap(values):
    return lax.all_to_all(values, "expert", split_axis=0, concat_axis=0, tiled=True)


def after(values, *others):
    return lax.optimization_barrier((values,) + others)[0]


def plane_body(tokens, cotangent, gate_probs, expert_ids, gate_up, down):
    me = lax.axis_index("expert")
    half = gate_up.shape[2] // 2
    quarter = tokens.shape[1] // 4
    ids, probs = expert_ids.T, gate_probs.T
    *local, slots = dispatch_rows(ids, probs, tokens, cotangent)
    chunks = len(local)
    tops = tuple(48 - 16 * (chunk % 2) for chunk in range(chunks))
    arrived = [local[0]]
    for chunk in range(1, chunks):
        sent = local[chunk] if chunk == 1 else after(local[chunk], arrived[-1])
        arrived.append(exchange(sent, "expert", 2 * chunk))
    pieces, inner = [], []
    for chunk, top in enumerate(tops):
        rows = arrived[chunk]
        other = exchange(rows[CAP:], "expert", 1)
        if chunk:
            other = after(other, inner[-1])
        own, to_x, to_y, found = expert_rows(rows, other, gate_up[0], down[0], top)
        inner.append(found)
        _, _, from_x, from_y = split_rows(top, half)
        got_x, got_y = exchange(to_x, "dp", 1), exchange(to_y, "dp", 2)
        far_top, far_low = exchange(got_x[:from_x], "dp", 2), exchange(got_y[:from_y], "dp", 1)
        pieces.append([own, got_x, got_y, far_top, far_low])
    early = [piece for chunk in pieces[:-1] for piece in chunk]
    sums = gradients(tops[:-1], early, half, quarter)
    grad_gu, grad_down = gradients(tops[-1:], pieces[-1], half, quarter, tuple(sums))
    numbers = jnp.arange(EXPERTS, dtype=jnp.int32)
    mine = (numbers[:, None] == jnp.bitwise_xor(numbers, me)[None, :])[:, :, None]
    rows_inner = jnp.concatenate(inner, axis=1).reshape(EXPERTS, CAP)
    sent = jnp.sum(jnp.where(mine, rows_inner[None], 0.0), axis=1)
    returned = jnp.sum(jnp.where(mine, swap(sent)[None], 0.0), axis=1).reshape(-1)
    chosen = slots[:, None, :] == jnp.arange(EXPERTS * CAP, dtype=jnp.int32)[None, :, None]
    grad_probs = jnp.sum(jnp.where(chosen, returned[None, :, None], 0.0), axis=1) / probs
    return (grad_probs.T, grad_gu[None], grad_down[None])


def widen(values, slices, expert_count):
    tail = values.shape[1:]
    spread = values.reshape((EXPERTS, 1, CAP) + tail)
    spread = jnp.broadcast_to(spread, (EXPERTS, slices, CAP) + tail)
    return spread.reshape((expert_count, CAP) + tail)


def sliced_body(tokens, cotangent, gate_probs, expert_ids, gate_up, down):
    expert_count = lax.axis_size("expert")
    slices = expert_count // EXPERTS
    tok_count, width = tokens.shape
    choose_count = expert_ids.shape[1]
    half = gate_up.shape[2] // 2
    slot_rows = EXPERTS * CAP
    flat_ids = expert_ids.reshape(-1)
    choose = (flat_ids[:, None] == jnp.arange(EXPERTS, dtype=jnp.int32)[None, :]).astype(jnp.int32)
    earlier = jnp.cumsum(choose, axis=0) - choose
    slot_of = flat_ids * CAP + jnp.sum(earlier * choose, axis=1)
    picked = jnp.arange(slot_rows, dtype=jnp.int32)[:, None] == slot_of[None, :]
    picked_tok = jnp.any(picked.reshape(slot_rows, tok_count, choose_count), axis=2).astype(BF16)
    slot_prob = jnp.sum(jnp.where(picked, gate_probs.reshape(-1)[None, :], 0.0), axis=1)
    local_x = jnp.dot(picked_tok, tokens, preferred_element_type=F32).astype(BF16)
    local_dy = jnp.dot(picked_tok, cotangent, preferred_element_type=F32)
    local_scaled = (slot_prob[:, None] * local_dy).astype(BF16)
    rows_x = swap(widen(local_x, slices, expert_count)).reshape(-1, width)
    rows_s = swap(widen(local_scaled, slices, expert_count)).reshape(-1, width)
    both = jnp.dot(rows_x, gate_up[0], preferred_element_type=F32)
    gate, up = both[:, :half], both[:, half:]
    sigmoid = jax.nn.sigmoid(gate)
    activated = gate * sigmoid
    hidden = (activated * up).astype(BF16)
    grad_hidden = lax.dot_general(
        rows_s, down[0], (((1,), (1,)), ((), ())), preferred_element_type=F32
    )
    inner = jnp.sum(hidden.astype(F32) * grad_hidden, axis=1)
    grad_gate = (grad_hidden * up * sigmoid * (1.0 + gate * (1.0 - sigmoid))).astype(BF16)
    grad_up = (grad_hidden * activated).astype(BF16)
    grad_both = jnp.concatenate([grad_gate, grad_up], axis=1)
    over_rows = (((0,), (0,)), ((), ()))
    grad_gu = lax.dot_general(rows_x, grad_both, over_rows, preferred_element_type=F32)
    grad_down = lax.dot_general(hidden, rows_s, over_rows, preferred_element_type=F32)
    returned = swap(inner.reshape(expert_count, CAP))
    per_slot = jnp.sum(returned.reshape(EXPERTS, slices, CAP), axis=1).reshape(slot_rows)
    grad_probs = jnp.sum(jnp.where(picked, per_slot[:, None], 0.0), axis=0)
    grad_probs = grad_probs.reshape(tok_count, choose_count) / gate_probs
    reduced_gu = lax.psum_scatter(grad_gu.astype(BF16), "dp", scatter_dimension=0, tiled=True)
    reduced_down = lax.psum_scatter(grad_down.astype(BF16), "dp", scatter_dimension=1, tiled=True)
    return (grad_probs, reduced_gu[None], reduced_down[None])


def solution(mesh):
    whole_experts = mesh.shape["expert"] == EXPERTS and mesh.shape["dp"] == 4
    return jax.shard_map(
        plane_body if whole_experts else sliced_body,
        mesh=mesh,
        in_specs=(
            P(("dp", "expert"), None),
            P(("dp", "expert"), None),
            P(("dp", "expert"), None),
            P(("dp", "expert"), None),
            P("expert", None, None),
            P("expert", None, None),
        ),
        out_specs=(P(("dp", "expert"), None), P("expert", "dp", None), P("expert", None, "dp")),
        check_vma=False,
    )
```

```python
import functools

import jax
import jax.numpy as jnp
from jax import lax
from jax.experimental import pallas as pl
from jax.experimental.pallas import tpu as pltpu
from jax.sharding import PartitionSpec as P

EXPERTS = 8
CAP = 40
PAIR = 2 * CAP
TILE = 256
MIB = 1024 * 1024
BF16 = jnp.bfloat16
F32 = jnp.float32


def dispatch_kernel(ids_ref, probs_ref, x_ref, dy_ref, *outs):
    row_refs, slot_ref = outs[:-1], outs[-1]
    me = lax.axis_index("expert")
    tok = x_ref.shape[0]
    width = x_ref.shape[1]
    numbers = lax.broadcasted_iota(jnp.int32, (EXPERTS, tok), 0)
    first = jnp.bitwise_xor(ids_ref[0:1, :], me) == numbers
    second = jnp.bitwise_xor(ids_ref[1:2, :], me) == numbers
    either = jnp.where(first | second, 1.0, 0.0)
    prob = jnp.where(first, probs_ref[0:1, :], 0.0) + jnp.where(second, probs_ref[1:2, :], 0.0)
    before = jnp.where(
        lax.broadcasted_iota(jnp.int32, (tok, tok), 0)
        < lax.broadcasted_iota(jnp.int32, (tok, tok), 1),
        1.0,
        0.0,
    )
    position = jnp.dot(either.astype(BF16), before.astype(BF16), preferred_element_type=F32)
    slot = position.astype(jnp.int32) + numbers * CAP
    slot_ref[0:1, :] = jnp.sum(jnp.where(first, slot, 0), axis=0, keepdims=True)
    slot_ref[1:2, :] = jnp.sum(jnp.where(second, slot, 0), axis=0, keepdims=True)
    target = jnp.where(either > 0.5, position, -1.0)
    places = lax.broadcasted_iota(jnp.int32, (CAP, tok), 0).astype(F32)
    picks = [
        jnp.where(places == target[e : e + 1, :], 1.0, 0.0) for e in range(EXPERTS)
    ]
    row_prob = jnp.concatenate(
        [jnp.sum(picks[e] * prob[e : e + 1, :], axis=1, keepdims=True) for e in range(EXPERTS)],
        axis=0,
    )
    pick = jnp.concatenate(picks, axis=0).astype(BF16)
    step = 512
    for at in range(0, width, step):
        rows_x = jnp.dot(pick, x_ref[:, at : at + step], preferred_element_type=F32)
        rows_dy = jnp.dot(pick, dy_ref[:, at : at + step], preferred_element_type=F32)
        scaled = row_prob * rows_dy
        for pair, ref in enumerate(row_refs):
            part = slice(pair * PAIR, (pair + 1) * PAIR)
            ref[:, at : at + step] = rows_x[part].astype(BF16)
            ref[:, width + at : width + at + step] = scaled[part].astype(BF16)


def dispatch_rows(ids, probs, tokens, cotangent):
    tok, width = tokens.shape
    return pl.pallas_call(
        dispatch_kernel,
        out_shape=[jax.ShapeDtypeStruct((PAIR, 2 * width), BF16)] * (EXPERTS // 2)
        + [jax.ShapeDtypeStruct((2, tok), jnp.int32)],
        compiler_params=pltpu.CompilerParams(vmem_limit_bytes=16 * MIB),
        cost_estimate=pl.CostEstimate(
            flops=4 * EXPERTS * CAP * tok * width, bytes_accessed=4_000_000, transcendentals=0
        ),
        name="dispatch_rows",
    )(ids, probs, tokens, cotangent)


def split_rows(top, half):
    blocks = 3 * half // TILE
    low = PAIR - top
    return blocks, low, (blocks + 4) * top, (blocks + 4) * low


def expert_kernel(top, a_ref, b_ref, gate_ref, up_ref, down_ref, *rest):
    own_ref, to_x, to_y, inner_ref, x_rows, s_rows, s_turned, total = rest
    width = gate_ref.shape[0]
    steps = pl.num_programs(0)
    half = TILE * 3
    quarter = width // 4
    blocks, low, from_x, from_y = split_rows(top, half)
    step = pl.program_id(0)
    group = lax.axis_index("dp")

    @pl.when(step == 0)
    def _():
        for rows, start in ((x_rows, 0), (s_rows, width)):
            rows[...] = jnp.concatenate(
                [
                    a_ref[:CAP, start : start + width].astype(F32),
                    b_ref[:, start : start + width].astype(F32),
                ],
                axis=0,
            ).astype(BF16)
        for q in range(4):
            rows = (x_rows, s_rows)[q // 2]

            def cut(mask):
                at = jnp.bitwise_xor(group, mask) * quarter + q % 2 * TILE
                return rows[:, pl.ds(pl.multiple_of(at, TILE), TILE)]

            at = blocks + q
            own_ref[at * PAIR : (at + 1) * PAIR] = cut(0)
            far = cut(3)
            to_x[at * top : (at + 1) * top] = far[:top]
            to_y[at * low : (at + 1) * low] = far[top:]
            start = from_x + blocks * low + q * PAIR
            to_x[start : start + PAIR] = cut(1)
            start = from_y + blocks * top + q * PAIR
            to_y[start : start + PAIR] = cut(2)
        s_turned[...] = s_rows[...].T
        total[...] = jnp.zeros_like(total)

    x = x_rows[...]
    gate = jnp.dot(x, gate_ref[...], preferred_element_type=F32)
    up = jnp.dot(x, up_ref[...], preferred_element_type=F32)
    grad_hidden = jnp.dot(down_ref[...], s_turned[...], preferred_element_type=F32).T
    sigmoid = 1.0 / (1.0 + jnp.exp(-gate))
    activated = gate * sigmoid
    hidden = (activated * up).astype(BF16)
    grad_gate = (grad_hidden * up * sigmoid * (1.0 + gate * (1.0 - sigmoid))).astype(BF16)
    grad_up = (grad_hidden * activated).astype(BF16)
    total[...] += jnp.sum(hidden.astype(F32) * grad_hidden, axis=1, keepdims=True)
    for part, values in enumerate((grad_gate, grad_up, hidden)):
        block = part * steps + step

        def rows_at(start, count):
            return pl.ds(pl.multiple_of(start + block * count, 16), count)

        own_ref[rows_at(0, PAIR)] = values
        to_x[rows_at(0, top)] = values[:top]
        to_x[rows_at(from_x, low)] = values[top:]
        to_y[rows_at(0, low)] = values[top:]
        to_y[rows_at(from_y, top)] = values[:top]

    @pl.when(step == steps - 1)
    def _():
        inner_ref[...] = jnp.broadcast_to(total[...], (PAIR, 128)).T[0:1]


def expert_rows(rows_a, rows_b, weight_gu, weight_down, top):
    width, both = weight_gu.shape
    half = both // 2
    steps = half // TILE
    blocks, low, from_x, from_y = split_rows(top, half)
    shapes = [
        ((blocks + 4) * PAIR, TILE),
        (from_x + blocks * low + 4 * PAIR, TILE),
        (from_y + blocks * top + 4 * PAIR, TILE),
    ]

    def whole(shape):
        return pl.BlockSpec(shape, lambda h: (0, 0))

    return pl.pallas_call(
        functools.partial(expert_kernel, top),
        grid=(steps,),
        in_specs=[
            whole(rows_a.shape),
            whole(rows_b.shape),
            pl.BlockSpec((width, TILE), lambda h: (0, h)),
            pl.BlockSpec((width, TILE), lambda h: (0, h + steps)),
            pl.BlockSpec((TILE, width), lambda h: (h, 0)),
        ],
        out_specs=[whole(shape) for shape in shapes] + [whole((1, PAIR))],
        out_shape=[jax.ShapeDtypeStruct(shape, BF16) for shape in shapes]
        + [jax.ShapeDtypeStruct((1, PAIR), F32)],
        scratch_shapes=[
            pltpu.VMEM((PAIR, width), BF16),
            pltpu.VMEM((PAIR, width), BF16),
            pltpu.VMEM((width, PAIR), BF16),
            pltpu.VMEM((PAIR, 1), F32),
        ],
        compiler_params=pltpu.CompilerParams(vmem_limit_bytes=20 * MIB),
        cost_estimate=pl.CostEstimate(flops=1_000_000, bytes_accessed=1_000_000, transcendentals=0),
        name="expert_rows",
    )(rows_a, rows_b, weight_gu, weight_gu, weight_down)


def gradient_kernel(tops, half, adding, *refs):
    groups, refs = [refs[5 * n : 5 * n + 5] for n in range(len(tops))], refs[5 * len(tops) :]
    if adding:
        (acc_gu, acc_down), refs = refs[:2], refs[2:]
    out_gu, out_down, turned, s_rows = refs
    both = 2 * half // TILE

    def factor(block):
        parts = []
        for top, (own, got_x, got_y, far_top, far_low) in zip(tops, groups):
            _, low, from_x, from_y = split_rows(top, half)
            parts += [
                own[block * PAIR : (block + 1) * PAIR],
                got_x[block * top : (block + 1) * top],
                got_x[from_x + block * low : from_x + (block + 1) * low],
                got_y[from_y + block * top : from_y + (block + 1) * top],
                got_y[block * low : (block + 1) * low],
                far_top[block * top : (block + 1) * top],
                far_low[block * low : (block + 1) * low],
            ]
        return jnp.concatenate(parts, axis=0)

    def piece(q):
        parts = []
        for top, (own, got_x, got_y, far_top, far_low) in zip(tops, groups):
            blocks, low, from_x, from_y = split_rows(top, half)
            block = blocks + q
            at_x = from_x + blocks * low + q * PAIR
            at_y = from_y + blocks * top + q * PAIR
            parts += [
                own[block * PAIR : (block + 1) * PAIR],
                got_x[at_x : at_x + PAIR],
                got_y[at_y : at_y + PAIR],
                far_top[block * top : (block + 1) * top],
                far_low[block * low : (block + 1) * low],
            ]
        return jnp.concatenate(parts, axis=0)

    for q in range(2):
        turned[q * TILE : (q + 1) * TILE, :] = piece(q).T
        s_rows[:, q * TILE : (q + 1) * TILE] = piece(2 + q)
    for block in range(both):
        at = slice(block * TILE, (block + 1) * TILE)
        grad = jnp.dot(turned[...], factor(block), preferred_element_type=F32)
        if adding:
            grad = grad + acc_gu[:, at]
        out_gu[:, at] = grad.astype(out_gu.dtype)
    for block in range(half // TILE):
        at = slice(block * TILE, (block + 1) * TILE)
        grad = jnp.dot(factor(both + block).T, s_rows[...], preferred_element_type=F32)
        if adding:
            grad = grad + acc_down[at, :]
        out_down[at, :] = grad.astype(out_down.dtype)


def gradients(tops, pieces, half, quarter, sums=(), final=False):
    kept = BF16 if final else F32
    rows = 4 * PAIR * len(tops)
    vmem = pl.BlockSpec(memory_space=pltpu.VMEM)
    return pl.pallas_call(
        functools.partial(gradient_kernel, tops, half, len(sums)),
        in_specs=[vmem] * (len(pieces) + len(sums)),
        out_specs=[vmem] * 2,
        out_shape=[
            jax.ShapeDtypeStruct((quarter, 2 * half), kept),
            jax.ShapeDtypeStruct((half, quarter), kept),
        ],
        scratch_shapes=[pltpu.VMEM((quarter, rows), BF16), pltpu.VMEM((rows, quarter), BF16)],
        compiler_params=pltpu.CompilerParams(vmem_limit_bytes=24 * MIB),
        cost_estimate=pl.CostEstimate(flops=1_000_000, bytes_accessed=1_000_000, transcendentals=0),
        name="gradients",
    )(*pieces, *sums)


def exchange(values, axis, mask):
    size = lax.axis_size(axis)
    return lax.ppermute(values, axis, [(n, n ^ mask) for n in range(size)])


def swap(values):
    return lax.all_to_all(values, "expert", split_axis=0, concat_axis=0, tiled=True)


def after(values, *others):
    return lax.optimization_barrier((values,) + others)[0]


def plane_body(tokens, cotangent, gate_probs, expert_ids, gate_up, down):
    me = lax.axis_index("expert")
    half = gate_up.shape[2] // 2
    quarter = tokens.shape[1] // 4
    ids, probs = expert_ids.T, gate_probs.T
    *local, slots = dispatch_rows(ids, probs, tokens, cotangent)
    tops = (48, 32, 48, 32)
    inner, pieces = [], []

    def other_core(rows):
        return exchange(rows[CAP:], "expert", 1)

    def compute(rows, other, *others):
        top = tops[len(inner)]
        other = after(other, *others)
        own, to_x, to_y, found = expert_rows(rows, other, gate_up[0], down[0], top)
        inner.append(found)
        _, _, from_x, from_y = split_rows(top, half)
        got_x, got_y = exchange(to_x, "dp", 1), exchange(to_y, "dp", 2)
        forward = (got_x[:from_x], got_y[:from_y])
        far_top, far_low = exchange(forward[0], "dp", 2), exchange(forward[1], "dp", 1)
        pieces.append([own, got_x, got_y, far_top, far_low])

    rows_1 = exchange(local[1], "expert", 2)
    other = other_core(local[0])
    rows_2 = exchange(local[2], "expert", 4)
    compute(local[0], other)
    rows_1 = after(rows_1, inner[0])
    compute(rows_1, other_core(rows_1))
    rows_2 = after(rows_2, inner[1])
    rows_3 = exchange(after(local[3], rows_2), "expert", 6)
    compute(rows_2, other_core(rows_2), *pieces[0])
    rows_3 = after(rows_3, inner[2])
    compute(rows_3, other_core(rows_3), *pieces[1])
    early = after(tuple(pieces[0] + pieces[1]), inner[3])
    sums = gradients(tops[:2], early, half, quarter)
    sums = gradients(tops[2:3], pieces[2], half, quarter, sums)
    grad_gu, grad_down = gradients(tops[3:], pieces[3], half, quarter, sums, True)
    numbers = jnp.arange(EXPERTS, dtype=jnp.int32)
    mine = (numbers[:, None] == jnp.bitwise_xor(numbers, me)[None, :])[:, :, None]
    rows_inner = after(jnp.concatenate(inner, axis=1), *pieces[2]).reshape(EXPERTS, CAP)
    sent = jnp.sum(jnp.where(mine, rows_inner[None], 0.0), axis=1)
    returned = jnp.sum(jnp.where(mine, swap(sent)[None], 0.0), axis=1).reshape(-1)
    chosen = slots[:, None, :] == jnp.arange(EXPERTS * CAP, dtype=jnp.int32)[None, :, None]
    grad_probs = jnp.sum(jnp.where(chosen, returned[None, :, None], 0.0), axis=1) / probs
    return (grad_probs.T, grad_gu[None], grad_down[None])


def widen(values, slices, expert_count):
    tail = values.shape[1:]
    spread = values.reshape((EXPERTS, 1, CAP) + tail)
    spread = jnp.broadcast_to(spread, (EXPERTS, slices, CAP) + tail)
    return spread.reshape((expert_count, CAP) + tail)


def sliced_body(tokens, cotangent, gate_probs, expert_ids, gate_up, down):
    expert_count = lax.axis_size("expert")
    slices = expert_count // EXPERTS
    tok_count, width = tokens.shape
    choose_count = expert_ids.shape[1]
    half = gate_up.shape[2] // 2
    slot_rows = EXPERTS * CAP
    flat_ids = expert_ids.reshape(-1)
    choose = (flat_ids[:, None] == jnp.arange(EXPERTS, dtype=jnp.int32)[None, :]).astype(jnp.int32)
    earlier = jnp.cumsum(choose, axis=0) - choose
    slot_of = flat_ids * CAP + jnp.sum(earlier * choose, axis=1)
    picked = jnp.arange(slot_rows, dtype=jnp.int32)[:, None] == slot_of[None, :]
    picked_tok = jnp.any(picked.reshape(slot_rows, tok_count, choose_count), axis=2).astype(BF16)
    slot_prob = jnp.sum(jnp.where(picked, gate_probs.reshape(-1)[None, :], 0.0), axis=1)
    local_x = jnp.dot(picked_tok, tokens, preferred_element_type=F32).astype(BF16)
    local_dy = jnp.dot(picked_tok, cotangent, preferred_element_type=F32)
    local_scaled = (slot_prob[:, None] * local_dy).astype(BF16)
    rows_x = swap(widen(local_x, slices, expert_count)).reshape(-1, width)
    rows_s = swap(widen(local_scaled, slices, expert_count)).reshape(-1, width)
    both = jnp.dot(rows_x, gate_up[0], preferred_element_type=F32)
    gate, up = both[:, :half], both[:, half:]
    sigmoid = jax.nn.sigmoid(gate)
    activated = gate * sigmoid
    hidden = (activated * up).astype(BF16)
    grad_hidden = lax.dot_general(
        rows_s, down[0], (((1,), (1,)), ((), ())), preferred_element_type=F32
    )
    inner = jnp.sum(hidden.astype(F32) * grad_hidden, axis=1)
    grad_gate = (grad_hidden * up * sigmoid * (1.0 + gate * (1.0 - sigmoid))).astype(BF16)
    grad_up = (grad_hidden * activated).astype(BF16)
    grad_both = jnp.concatenate([grad_gate, grad_up], axis=1)
    over_rows = (((0,), (0,)), ((), ()))
    grad_gu = lax.dot_general(rows_x, grad_both, over_rows, preferred_element_type=F32)
    grad_down = lax.dot_general(hidden, rows_s, over_rows, preferred_element_type=F32)
    returned = swap(inner.reshape(expert_count, CAP))
    per_slot = jnp.sum(returned.reshape(EXPERTS, slices, CAP), axis=1).reshape(slot_rows)
    grad_probs = jnp.sum(jnp.where(picked, per_slot[:, None], 0.0), axis=0)
    grad_probs = grad_probs.reshape(tok_count, choose_count) / gate_probs
    reduced_gu = lax.psum_scatter(grad_gu.astype(BF16), "dp", scatter_dimension=0, tiled=True)
    reduced_down = lax.psum_scatter(grad_down.astype(BF16), "dp", scatter_dimension=1, tiled=True)
    return (grad_probs, reduced_gu[None], reduced_down[None])


def solution(mesh):
    whole_experts = mesh.shape["expert"] == EXPERTS and mesh.shape["dp"] == 4
    return jax.shard_map(
        plane_body if whole_experts else sliced_body,
        mesh=mesh,
        in_specs=(
            P(("dp", "expert"), None),
            P(("dp", "expert"), None),
            P(("dp", "expert"), None),
            P(("dp", "expert"), None),
            P("expert", None, None),
            P("expert", None, None),
        ),
        out_specs=(P(("dp", "expert"), None), P("expert", "dp", None), P("expert", None, "dp")),
        check_vma=False,
    )
```

```python
import functools

import jax
import jax.numpy as jnp
from jax import lax
from jax.experimental import pallas as pl
from jax.experimental.pallas import tpu as pltpu
from jax.sharding import PartitionSpec as P

EXPERTS = 8
CAP = 40
PAIR = 2 * CAP
TILE = 256
MIB = 1024 * 1024
BF16 = jnp.bfloat16
F32 = jnp.float32


def dispatch_kernel(ids_ref, probs_ref, x_ref, dy_ref, *outs):
    row_refs, slot_ref = outs[:-1], outs[-1]
    me = lax.axis_index("expert")
    tok = x_ref.shape[0]
    width = x_ref.shape[1]
    numbers = lax.broadcasted_iota(jnp.int32, (EXPERTS, tok), 0)
    first = jnp.bitwise_xor(ids_ref[0:1, :], me) == numbers
    second = jnp.bitwise_xor(ids_ref[1:2, :], me) == numbers
    either = jnp.where(first | second, 1.0, 0.0)
    prob = jnp.where(first, probs_ref[0:1, :], 0.0) + jnp.where(second, probs_ref[1:2, :], 0.0)
    before = jnp.where(
        lax.broadcasted_iota(jnp.int32, (tok, tok), 0)
        < lax.broadcasted_iota(jnp.int32, (tok, tok), 1),
        1.0,
        0.0,
    )
    position = jnp.dot(either.astype(BF16), before.astype(BF16), preferred_element_type=F32)
    slot = position.astype(jnp.int32) + numbers * CAP
    slot_ref[0:1, :] = jnp.sum(jnp.where(first, slot, 0), axis=0, keepdims=True)
    slot_ref[1:2, :] = jnp.sum(jnp.where(second, slot, 0), axis=0, keepdims=True)
    target = jnp.where(either > 0.5, position, -1.0)
    places = lax.broadcasted_iota(jnp.int32, (CAP, tok), 0).astype(F32)
    picks = [
        jnp.where(places == target[e : e + 1, :], 1.0, 0.0) for e in range(EXPERTS)
    ]
    row_prob = jnp.concatenate(
        [jnp.sum(picks[e] * prob[e : e + 1, :], axis=1, keepdims=True) for e in range(EXPERTS)],
        axis=0,
    )
    pick = jnp.concatenate(picks, axis=0).astype(BF16)
    step = 512
    for at in range(0, width, step):
        rows_x = jnp.dot(pick, x_ref[:, at : at + step], preferred_element_type=F32)
        rows_dy = jnp.dot(pick, dy_ref[:, at : at + step], preferred_element_type=F32)
        scaled = row_prob * rows_dy
        for pair, ref in enumerate(row_refs):
            part = slice(pair * PAIR, (pair + 1) * PAIR)
            ref[:, at : at + step] = rows_x[part].astype(BF16)
            ref[:, width + at : width + at + step] = scaled[part].astype(BF16)


def dispatch_rows(ids, probs, tokens, cotangent):
    tok, width = tokens.shape
    return pl.pallas_call(
        dispatch_kernel,
        out_shape=[jax.ShapeDtypeStruct((PAIR, 2 * width), BF16)] * (EXPERTS // 2)
        + [jax.ShapeDtypeStruct((2, tok), jnp.int32)],
        compiler_params=pltpu.CompilerParams(vmem_limit_bytes=16 * MIB),
        cost_estimate=pl.CostEstimate(
            flops=4 * EXPERTS * CAP * tok * width, bytes_accessed=4_000_000, transcendentals=0
        ),
        name="dispatch_rows",
    )(ids, probs, tokens, cotangent)


def split_rows(top, half):
    blocks = 3 * half // TILE
    low = PAIR - top
    return blocks, low, (blocks + 4) * top, (blocks + 4) * low


def expert_kernel(top, a_ref, b_ref, gate_ref, up_ref, down_ref, *rest):
    own_ref, to_x, to_y, inner_ref, x_rows, s_rows, s_turned, total = rest
    width = gate_ref.shape[0]
    steps = pl.num_programs(0)
    half = TILE * 3
    quarter = width // 4
    blocks, low, from_x, from_y = split_rows(top, half)
    step = pl.program_id(0)
    group = lax.axis_index("dp")

    @pl.when(step == 0)
    def _():
        for rows, start in ((x_rows, 0), (s_rows, width)):
            rows[...] = jnp.concatenate(
                [
                    a_ref[:CAP, start : start + width].astype(F32),
                    b_ref[:, start : start + width].astype(F32),
                ],
                axis=0,
            ).astype(BF16)
        for q in range(4):
            rows = (x_rows, s_rows)[q // 2]

            def cut(mask):
                at = jnp.bitwise_xor(group, mask) * quarter + q % 2 * TILE
                return rows[:, pl.ds(pl.multiple_of(at, TILE), TILE)]

            at = blocks + q
            own_ref[at * PAIR : (at + 1) * PAIR] = cut(0)
            far = cut(3)
            to_x[at * top : (at + 1) * top] = far[:top]
            to_y[at * low : (at + 1) * low] = far[top:]
            start = from_x + blocks * low + q * PAIR
            to_x[start : start + PAIR] = cut(1)
            start = from_y + blocks * top + q * PAIR
            to_y[start : start + PAIR] = cut(2)
        s_turned[...] = s_rows[...].T
        total[...] = jnp.zeros_like(total)

    x = x_rows[...]
    gate = jnp.dot(x, gate_ref[...], preferred_element_type=F32)
    up = jnp.dot(x, up_ref[...], preferred_element_type=F32)
    grad_hidden = jnp.dot(down_ref[...], s_turned[...], preferred_element_type=F32).T
    sigmoid = 1.0 / (1.0 + jnp.exp(-gate))
    activated = gate * sigmoid
    hidden = (activated * up).astype(BF16)
    grad_gate = (grad_hidden * up * sigmoid * (1.0 + gate * (1.0 - sigmoid))).astype(BF16)
    grad_up = (grad_hidden * activated).astype(BF16)
    total[...] += jnp.sum(hidden.astype(F32) * grad_hidden, axis=1, keepdims=True)
    for part, values in enumerate((grad_gate, grad_up, hidden)):
        block = part * steps + step

        def rows_at(start, count):
            return pl.ds(pl.multiple_of(start + block * count, 16), count)

        own_ref[rows_at(0, PAIR)] = values
        to_x[rows_at(0, top)] = values[:top]
        to_x[rows_at(from_x, low)] = values[top:]
        to_y[rows_at(0, low)] = values[top:]
        to_y[rows_at(from_y, top)] = values[:top]

    @pl.when(step == steps - 1)
    def _():
        inner_ref[...] = jnp.broadcast_to(total[...], (PAIR, 128)).T[0:1]


def expert_rows(rows_a, rows_b, weight_gu, weight_down, top):
    width, both = weight_gu.shape
    half = both // 2
    steps = half // TILE
    blocks, low, from_x, from_y = split_rows(top, half)
    shapes = [
        ((blocks + 4) * PAIR, TILE),
        (from_x + blocks * low + 4 * PAIR, TILE),
        (from_y + blocks * top + 4 * PAIR, TILE),
    ]

    def whole(shape):
        return pl.BlockSpec(shape, lambda h: (0, 0))

    return pl.pallas_call(
        functools.partial(expert_kernel, top),
        grid=(steps,),
        in_specs=[
            whole(rows_a.shape),
            whole(rows_b.shape),
            pl.BlockSpec((width, TILE), lambda h: (0, h)),
            pl.BlockSpec((width, TILE), lambda h: (0, h + steps)),
            pl.BlockSpec((TILE, width), lambda h: (h, 0)),
        ],
        out_specs=[whole(shape) for shape in shapes] + [whole((1, PAIR))],
        out_shape=[jax.ShapeDtypeStruct(shape, BF16) for shape in shapes]
        + [jax.ShapeDtypeStruct((1, PAIR), F32)],
        scratch_shapes=[
            pltpu.VMEM((PAIR, width), BF16),
            pltpu.VMEM((PAIR, width), BF16),
            pltpu.VMEM((width, PAIR), BF16),
            pltpu.VMEM((PAIR, 1), F32),
        ],
        compiler_params=pltpu.CompilerParams(vmem_limit_bytes=14 * MIB),
        cost_estimate=pl.CostEstimate(flops=1_000_000, bytes_accessed=1_000_000, transcendentals=0),
        name="expert_rows",
    )(rows_a, rows_b, weight_gu, weight_gu, weight_down)


def gradient_kernel(tops, half, adding, *refs):
    groups, refs = [refs[5 * n : 5 * n + 5] for n in range(len(tops))], refs[5 * len(tops) :]
    if adding:
        (acc_gu, acc_down), refs = refs[:2], refs[2:]
    out_gu, out_down, turned, s_rows = refs
    both = 2 * half // TILE

    def factor(block):
        parts = []
        for top, (own, got_x, got_y, far_top, far_low) in zip(tops, groups):
            _, low, from_x, from_y = split_rows(top, half)
            parts += [
                own[block * PAIR : (block + 1) * PAIR],
                got_x[block * top : (block + 1) * top],
                got_x[from_x + block * low : from_x + (block + 1) * low],
                got_y[from_y + block * top : from_y + (block + 1) * top],
                got_y[block * low : (block + 1) * low],
                far_top[block * top : (block + 1) * top],
                far_low[block * low : (block + 1) * low],
            ]
        return jnp.concatenate(parts, axis=0)

    def piece(q):
        parts = []
        for top, (own, got_x, got_y, far_top, far_low) in zip(tops, groups):
            blocks, low, from_x, from_y = split_rows(top, half)
            block = blocks + q
            at_x = from_x + blocks * low + q * PAIR
            at_y = from_y + blocks * top + q * PAIR
            parts += [
                own[block * PAIR : (block + 1) * PAIR],
                got_x[at_x : at_x + PAIR],
                got_y[at_y : at_y + PAIR],
                far_top[block * top : (block + 1) * top],
                far_low[block * low : (block + 1) * low],
            ]
        return jnp.concatenate(parts, axis=0)

    for q in range(2):
        turned[q * TILE : (q + 1) * TILE, :] = piece(q).T
        s_rows[:, q * TILE : (q + 1) * TILE] = piece(2 + q)
    for block in range(both):
        at = slice(block * TILE, (block + 1) * TILE)
        grad = jnp.dot(turned[...], factor(block), preferred_element_type=F32)
        if adding:
            grad = grad + acc_gu[:, at]
        out_gu[:, at] = grad.astype(out_gu.dtype)
    for block in range(half // TILE):
        at = slice(block * TILE, (block + 1) * TILE)
        grad = jnp.dot(factor(both + block).T, s_rows[...], preferred_element_type=F32)
        if adding:
            grad = grad + acc_down[at, :]
        out_down[at, :] = grad.astype(out_down.dtype)


def gradients(tops, pieces, half, quarter, sums=(), final=False):
    kept = BF16 if final else F32
    rows = 4 * PAIR * len(tops)
    vmem = pl.BlockSpec(memory_space=pltpu.VMEM)
    return pl.pallas_call(
        functools.partial(gradient_kernel, tops, half, len(sums)),
        in_specs=[vmem] * (len(pieces) + len(sums)),
        out_specs=[vmem] * 2,
        out_shape=[
            jax.ShapeDtypeStruct((quarter, 2 * half), kept),
            jax.ShapeDtypeStruct((half, quarter), kept),
        ],
        scratch_shapes=[pltpu.VMEM((quarter, rows), BF16), pltpu.VMEM((rows, quarter), BF16)],
        compiler_params=pltpu.CompilerParams(vmem_limit_bytes=14 * MIB),
        cost_estimate=pl.CostEstimate(flops=1_000_000, bytes_accessed=1_000_000, transcendentals=0),
        name="gradients",
    )(*pieces, *sums)


def exchange(values, axis, mask):
    size = lax.axis_size(axis)
    return lax.ppermute(values, axis, [(n, n ^ mask) for n in range(size)])


def swap(values):
    return lax.all_to_all(values, "expert", split_axis=0, concat_axis=0, tiled=True)


def after(values, *others):
    return lax.optimization_barrier((values,) + others)[0]


def plane_body(tokens, cotangent, gate_probs, expert_ids, gate_up, down):
    me = lax.axis_index("expert")
    half = gate_up.shape[2] // 2
    quarter = tokens.shape[1] // 4
    ids, probs = expert_ids.T, gate_probs.T
    *local, slots = dispatch_rows(ids, probs, tokens, cotangent)
    tops = (48, 32, 48, 32)
    inner, pieces, forwards = [], [], []

    def other_core(rows):
        return exchange(rows[CAP:], "expert", 1)

    def compute(rows):
        top = tops[len(inner)]
        own, to_x, to_y, found = expert_rows(rows, other_core(rows), gate_up[0], down[0], top)
        inner.append(found)
        _, _, from_x, from_y = split_rows(top, half)
        got_x, got_y = exchange(to_x, "dp", 1), exchange(to_y, "dp", 2)
        forward = (got_x[:from_x], got_y[:from_y])
        far_top, far_low = exchange(forward[0], "dp", 2), exchange(forward[1], "dp", 1)
        forwards.append(forward)
        pieces.append([own, got_x, got_y, far_top, far_low])

    def add(chunk, sums=()):
        return gradients(
            tops[chunk : chunk + 1], pieces[chunk], half, quarter, sums, chunk == len(tops) - 1
        )

    rows_2 = exchange(local[2], "expert", 4)
    rows_1 = exchange(local[1], "expert", 2)
    compute(local[0])
    rows_2 = after(rows_2, *forwards[0])
    rows_3 = exchange(after(local[3], rows_2), "expert", 6)
    compute(rows_2)
    compute(after(rows_1, inner[1]))
    sums = add(0)
    compute(after(rows_3, inner[2], *forwards[1], *sums))
    sums = add(1, sums)
    sums = add(2, sums)
    grad_gu, grad_down = add(3, sums)
    numbers = jnp.arange(EXPERTS, dtype=jnp.int32)
    mine = (numbers[:, None] == jnp.bitwise_xor(numbers, me)[None, :])[:, :, None]
    in_order = [inner[0], inner[2], inner[1], inner[3]]
    rows_inner = after(jnp.concatenate(in_order, axis=1), *forwards[2]).reshape(EXPERTS, CAP)
    sent = jnp.sum(jnp.where(mine, rows_inner[None], 0.0), axis=1)
    returned = jnp.sum(jnp.where(mine, swap(sent)[None], 0.0), axis=1).reshape(-1)
    chosen = slots[:, None, :] == jnp.arange(EXPERTS * CAP, dtype=jnp.int32)[None, :, None]
    grad_probs = jnp.sum(jnp.where(chosen, returned[None, :, None], 0.0), axis=1) / probs
    return (grad_probs.T, grad_gu[None], grad_down[None])


def widen(values, slices, expert_count):
    tail = values.shape[1:]
    spread = values.reshape((EXPERTS, 1, CAP) + tail)
    spread = jnp.broadcast_to(spread, (EXPERTS, slices, CAP) + tail)
    return spread.reshape((expert_count, CAP) + tail)


def sliced_body(tokens, cotangent, gate_probs, expert_ids, gate_up, down):
    expert_count = lax.axis_size("expert")
    slices = expert_count // EXPERTS
    tok_count, width = tokens.shape
    choose_count = expert_ids.shape[1]
    half = gate_up.shape[2] // 2
    slot_rows = EXPERTS * CAP
    flat_ids = expert_ids.reshape(-1)
    choose = (flat_ids[:, None] == jnp.arange(EXPERTS, dtype=jnp.int32)[None, :]).astype(jnp.int32)
    earlier = jnp.cumsum(choose, axis=0) - choose
    slot_of = flat_ids * CAP + jnp.sum(earlier * choose, axis=1)
    picked = jnp.arange(slot_rows, dtype=jnp.int32)[:, None] == slot_of[None, :]
    picked_tok = jnp.any(picked.reshape(slot_rows, tok_count, choose_count), axis=2).astype(BF16)
    slot_prob = jnp.sum(jnp.where(picked, gate_probs.reshape(-1)[None, :], 0.0), axis=1)
    local_x = jnp.dot(picked_tok, tokens, preferred_element_type=F32).astype(BF16)
    local_dy = jnp.dot(picked_tok, cotangent, preferred_element_type=F32)
    local_scaled = (slot_prob[:, None] * local_dy).astype(BF16)
    rows_x = swap(widen(local_x, slices, expert_count)).reshape(-1, width)
    rows_s = swap(widen(local_scaled, slices, expert_count)).reshape(-1, width)
    both = jnp.dot(rows_x, gate_up[0], preferred_element_type=F32)
    gate, up = both[:, :half], both[:, half:]
    sigmoid = jax.nn.sigmoid(gate)
    activated = gate * sigmoid
    hidden = (activated * up).astype(BF16)
    grad_hidden = lax.dot_general(
        rows_s, down[0], (((1,), (1,)), ((), ())), preferred_element_type=F32
    )
    inner = jnp.sum(hidden.astype(F32) * grad_hidden, axis=1)
    grad_gate = (grad_hidden * up * sigmoid * (1.0 + gate * (1.0 - sigmoid))).astype(BF16)
    grad_up = (grad_hidden * activated).astype(BF16)
    grad_both = jnp.concatenate([grad_gate, grad_up], axis=1)
    over_rows = (((0,), (0,)), ((), ()))
    grad_gu = lax.dot_general(rows_x, grad_both, over_rows, preferred_element_type=F32)
    grad_down = lax.dot_general(hidden, rows_s, over_rows, preferred_element_type=F32)
    returned = swap(inner.reshape(expert_count, CAP))
    per_slot = jnp.sum(returned.reshape(EXPERTS, slices, CAP), axis=1).reshape(slot_rows)
    grad_probs = jnp.sum(jnp.where(picked, per_slot[:, None], 0.0), axis=0)
    grad_probs = grad_probs.reshape(tok_count, choose_count) / gate_probs
    reduced_gu = lax.psum_scatter(grad_gu.astype(BF16), "dp", scatter_dimension=0, tiled=True)
    reduced_down = lax.psum_scatter(grad_down.astype(BF16), "dp", scatter_dimension=1, tiled=True)
    return (grad_probs, reduced_gu[None], reduced_down[None])


def solution(mesh):
    whole_experts = mesh.shape["expert"] == EXPERTS and mesh.shape["dp"] == 4
    return jax.shard_map(
        plane_body if whole_experts else sliced_body,
        mesh=mesh,
        in_specs=(
            P(("dp", "expert"), None),
            P(("dp", "expert"), None),
            P(("dp", "expert"), None),
            P(("dp", "expert"), None),
            P("expert", None, None),
            P("expert", None, None),
        ),
        out_specs=(P(("dp", "expert"), None), P("expert", "dp", None), P("expert", None, "dp")),
        check_vma=False,
    )
```

```python
import functools

import jax
import jax.numpy as jnp
from jax import lax
from jax.experimental import pallas as pl
from jax.experimental.pallas import tpu as pltpu
from jax.sharding import PartitionSpec as P

EXPERTS = 8
CAP = 40
PAIR = 2 * CAP
TILE = 256
MIB = 1024 * 1024
BF16 = jnp.bfloat16
F32 = jnp.float32


def dispatch_kernel(ids_ref, probs_ref, x_ref, dy_ref, *outs):
    row_refs, slot_ref = outs[:-1], outs[-1]
    me = lax.axis_index("expert")
    tok = x_ref.shape[0]
    width = x_ref.shape[1]
    numbers = lax.broadcasted_iota(jnp.int32, (EXPERTS, tok), 0)
    first = jnp.bitwise_xor(ids_ref[0:1, :], me) == numbers
    second = jnp.bitwise_xor(ids_ref[1:2, :], me) == numbers
    either = jnp.where(first | second, 1.0, 0.0)
    prob = jnp.where(first, probs_ref[0:1, :], 0.0) + jnp.where(second, probs_ref[1:2, :], 0.0)
    before = jnp.where(
        lax.broadcasted_iota(jnp.int32, (tok, tok), 0)
        < lax.broadcasted_iota(jnp.int32, (tok, tok), 1),
        1.0,
        0.0,
    )
    position = jnp.dot(either.astype(BF16), before.astype(BF16), preferred_element_type=F32)
    slot = position.astype(jnp.int32) + numbers * CAP
    slot_ref[0:1, :] = jnp.sum(jnp.where(first, slot, 0), axis=0, keepdims=True)
    slot_ref[1:2, :] = jnp.sum(jnp.where(second, slot, 0), axis=0, keepdims=True)
    target = jnp.where(either > 0.5, position, -1.0)
    places = lax.broadcasted_iota(jnp.int32, (CAP, tok), 0).astype(F32)
    picks = [
        jnp.where(places == target[e : e + 1, :], 1.0, 0.0) for e in range(EXPERTS)
    ]
    row_prob = jnp.concatenate(
        [jnp.sum(picks[e] * prob[e : e + 1, :], axis=1, keepdims=True) for e in range(EXPERTS)],
        axis=0,
    )
    pick = jnp.concatenate(picks, axis=0).astype(BF16)
    step = 512
    for at in range(0, width, step):
        rows_x = jnp.dot(pick, x_ref[:, at : at + step], preferred_element_type=F32)
        rows_dy = jnp.dot(pick, dy_ref[:, at : at + step], preferred_element_type=F32)
        scaled = row_prob * rows_dy
        for pair, ref in enumerate(row_refs):
            part = slice(pair * PAIR, (pair + 1) * PAIR)
            ref[:, at : at + step] = rows_x[part].astype(BF16)
            ref[:, width + at : width + at + step] = scaled[part].astype(BF16)


def dispatch_rows(ids, probs, tokens, cotangent):
    tok, width = tokens.shape
    return pl.pallas_call(
        dispatch_kernel,
        out_shape=[jax.ShapeDtypeStruct((PAIR, 2 * width), BF16)] * (EXPERTS // 2)
        + [jax.ShapeDtypeStruct((2, tok), jnp.int32)],
        compiler_params=pltpu.CompilerParams(vmem_limit_bytes=16 * MIB),
        cost_estimate=pl.CostEstimate(
            flops=4 * EXPERTS * CAP * tok * width, bytes_accessed=4_000_000, transcendentals=0
        ),
        name="dispatch_rows",
    )(ids, probs, tokens, cotangent)


def split_rows(count, top, half):
    blocks = 3 * half // TILE
    low = count - top
    return blocks, low, (blocks + 4) * top, (blocks + 4) * low


def expert_kernel(pairs, top, *refs):
    row_refs, (gate_ref, up_ref, down_ref), rest = (
        refs[: 2 * pairs],
        refs[2 * pairs : 2 * pairs + 3],
        refs[2 * pairs + 3 :],
    )
    own_ref, to_x, to_y, inner_ref, x_rows, s_rows, s_turned, total = rest
    count = pairs * PAIR
    width = gate_ref.shape[0]
    steps = pl.num_programs(0)
    half = TILE * 3
    quarter = width // 4
    blocks, low, from_x, from_y = split_rows(count, top, half)
    step = pl.program_id(0)
    group = lax.axis_index("dp")

    @pl.when(step == 0)
    def _():
        for rows, start in ((x_rows, 0), (s_rows, width)):
            rows[...] = jnp.concatenate(
                [ref[:CAP, start : start + width].astype(F32) for ref in row_refs],
                axis=0,
            ).astype(BF16)
        for q in range(4):
            rows = (x_rows, s_rows)[q // 2]

            def cut(mask):
                at = jnp.bitwise_xor(group, mask) * quarter + q % 2 * TILE
                return rows[:, pl.ds(pl.multiple_of(at, TILE), TILE)]

            at = blocks + q
            own_ref[at * count : (at + 1) * count] = cut(0)
            far = cut(3)
            to_x[at * top : (at + 1) * top] = far[:top]
            to_y[at * low : (at + 1) * low] = far[top:]
            start = from_x + blocks * low + q * count
            to_x[start : start + count] = cut(1)
            start = from_y + blocks * top + q * count
            to_y[start : start + count] = cut(2)
        s_turned[...] = s_rows[...].T
        total[...] = jnp.zeros_like(total)

    x = x_rows[...]
    gate = jnp.dot(x, gate_ref[...], preferred_element_type=F32)
    up = jnp.dot(x, up_ref[...], preferred_element_type=F32)
    grad_hidden = jnp.dot(down_ref[...], s_turned[...], preferred_element_type=F32).T
    sigmoid = 1.0 / (1.0 + jnp.exp(-gate))
    activated = gate * sigmoid
    hidden = (activated * up).astype(BF16)
    grad_gate = (grad_hidden * up * sigmoid * (1.0 + gate * (1.0 - sigmoid))).astype(BF16)
    grad_up = (grad_hidden * activated).astype(BF16)
    total[...] += jnp.sum(hidden.astype(F32) * grad_hidden, axis=1, keepdims=True)
    for part, values in enumerate((grad_gate, grad_up, hidden)):
        block = part * steps + step

        def rows_at(start, count):
            return pl.ds(pl.multiple_of(start + block * count, 16), count)

        own_ref[rows_at(0, count)] = values
        to_x[rows_at(0, top)] = values[:top]
        to_x[rows_at(from_x, low)] = values[top:]
        to_y[rows_at(0, low)] = values[top:]
        to_y[rows_at(from_y, top)] = values[:top]

    @pl.when(step == steps - 1)
    def _():
        inner_ref[...] = jnp.broadcast_to(total[...], (count, 128)).T[0:1]


def expert_rows(rows, weight_gu, weight_down, top):
    count = len(rows) // 2 * PAIR
    width, both = weight_gu.shape
    half = both // 2
    steps = half // TILE
    blocks, low, from_x, from_y = split_rows(count, top, half)
    shapes = [
        ((blocks + 4) * count, TILE),
        (from_x + blocks * low + 4 * count, TILE),
        (from_y + blocks * top + 4 * count, TILE),
    ]

    def whole(shape):
        return pl.BlockSpec(shape, lambda h: (0, 0))

    return pl.pallas_call(
        functools.partial(expert_kernel, len(rows) // 2, top),
        grid=(steps,),
        in_specs=[
            *[whole(part.shape) for part in rows],
            pl.BlockSpec((width, TILE), lambda h: (0, h)),
            pl.BlockSpec((width, TILE), lambda h: (0, h + steps)),
            pl.BlockSpec((TILE, width), lambda h: (h, 0)),
        ],
        out_specs=[whole(shape) for shape in shapes] + [whole((1, count))],
        out_shape=[jax.ShapeDtypeStruct(shape, BF16) for shape in shapes]
        + [jax.ShapeDtypeStruct((1, count), F32)],
        scratch_shapes=[
            pltpu.VMEM((count, width), BF16),
            pltpu.VMEM((count, width), BF16),
            pltpu.VMEM((width, count), BF16),
            pltpu.VMEM((count, 1), F32),
        ],
        compiler_params=pltpu.CompilerParams(vmem_limit_bytes=20 * MIB),
        cost_estimate=pl.CostEstimate(flops=1_000, bytes_accessed=1_000, transcendentals=0),
        name="expert_rows",
    )(*rows, weight_gu, weight_gu, weight_down)


def gradient_kernel(top, half, adding, *refs):
    (own, got_x, got_y, far_top, far_low), refs = refs[:5], refs[5:]
    count = own.shape[0] // (3 * half // TILE + 4)
    blocks, low, from_x, from_y = split_rows(count, top, half)
    if adding:
        (acc_gu, acc_down), refs = refs[:2], refs[2:]
    out_gu, out_down, turned, s_rows = refs
    both = 2 * half // TILE

    def factor(block):
        return jnp.concatenate(
            [
                own[block * count : (block + 1) * count],
                got_x[block * top : (block + 1) * top],
                got_x[from_x + block * low : from_x + (block + 1) * low],
                got_y[from_y + block * top : from_y + (block + 1) * top],
                got_y[block * low : (block + 1) * low],
                far_top[block * top : (block + 1) * top],
                far_low[block * low : (block + 1) * low],
            ],
            axis=0,
        )

    def piece(q):
        block = blocks + q
        at_x = from_x + blocks * low + q * count
        at_y = from_y + blocks * top + q * count
        return jnp.concatenate(
            [
                own[block * count : (block + 1) * count],
                got_x[at_x : at_x + count],
                got_y[at_y : at_y + count],
                far_top[block * top : (block + 1) * top],
                far_low[block * low : (block + 1) * low],
            ],
            axis=0,
        )

    for q in range(2):
        turned[q * TILE : (q + 1) * TILE, :] = piece(q).T
        s_rows[:, q * TILE : (q + 1) * TILE] = piece(2 + q)
    for block in range(both):
        at = slice(block * TILE, (block + 1) * TILE)
        grad = jnp.dot(turned[...], factor(block), preferred_element_type=F32)
        if adding:
            grad = grad + acc_gu[:, at]
        out_gu[:, at] = grad.astype(out_gu.dtype)
    for block in range(half // TILE):
        at = slice(block * TILE, (block + 1) * TILE)
        grad = jnp.dot(factor(both + block).T, s_rows[...], preferred_element_type=F32)
        if adding:
            grad = grad + acc_down[at, :]
        out_down[at, :] = grad.astype(out_down.dtype)


def gradients(top, pieces, half, quarter, sums=(), final=False):
    kept = BF16 if final else F32
    rows = 4 * pieces[0].shape[0] // (3 * half // TILE + 4)
    vmem = pl.BlockSpec(memory_space=pltpu.VMEM)
    return pl.pallas_call(
        functools.partial(gradient_kernel, top, half, len(sums)),
        in_specs=[vmem] * (len(pieces) + len(sums)),
        out_specs=[vmem] * 2,
        out_shape=[
            jax.ShapeDtypeStruct((quarter, 2 * half), kept),
            jax.ShapeDtypeStruct((half, quarter), kept),
        ],
        input_output_aliases={} if final or not sums else {len(pieces): 0, len(pieces) + 1: 1},
        scratch_shapes=[pltpu.VMEM((quarter, rows), BF16), pltpu.VMEM((rows, quarter), BF16)],
        compiler_params=pltpu.CompilerParams(vmem_limit_bytes=14 * MIB),
        cost_estimate=pl.CostEstimate(flops=1_000, bytes_accessed=1_000, transcendentals=0),
        name="gradients",
    )(*pieces, *sums)


def exchange(values, axis, mask):
    size = lax.axis_size(axis)
    return lax.ppermute(values, axis, [(n, n ^ mask) for n in range(size)])


def swap(values):
    return lax.all_to_all(values, "expert", split_axis=0, concat_axis=0, tiled=True)


def after(values, *others):
    return lax.optimization_barrier((values,) + others)[0]


def plane_body(tokens, cotangent, gate_probs, expert_ids, gate_up, down):
    me = lax.axis_index("expert")
    half = gate_up.shape[2] // 2
    quarter = tokens.shape[1] // 4
    ids, probs = expert_ids.T, gate_probs.T
    *local, slots = dispatch_rows(ids, probs, tokens, cotangent)
    tops = (48, PAIR, 32)
    inner, pieces, forwards = [], [], []

    def other_core(rows):
        return exchange(rows[CAP:], "expert", 1)

    def compute(*rows):
        top = tops[len(inner)]
        own, to_x, to_y, found = expert_rows(rows, gate_up[0], down[0], top)
        inner.append(found)
        _, _, from_x, from_y = split_rows(len(rows) // 2 * PAIR, top, half)
        got_x, got_y = exchange(to_x, "dp", 1), exchange(to_y, "dp", 2)
        forward = (got_x[:from_x], got_y[:from_y])
        far_top, far_low = exchange(forward[0], "dp", 2), exchange(forward[1], "dp", 1)
        forwards.append(forward)
        pieces.append([own, got_x, got_y, far_top, far_low])

    def add(chunk, sums=()):
        return gradients(tops[chunk], pieces[chunk], half, quarter, sums, chunk == len(tops) - 1)

    rows_1 = exchange(local[1], "expert", 2)
    rows_2 = exchange(local[2], "expert", 4)
    compute(local[0], other_core(local[0]))
    rows_1 = after(rows_1, inner[0])
    other_1 = other_core(rows_1)
    rows_3 = exchange(after(local[3], rows_2), "expert", 6)
    rows_2 = after(rows_2, *forwards[0])
    compute(rows_1, other_1, rows_2, other_core(rows_2))
    sums = add(0)
    rows_3 = after(rows_3, inner[1], *sums)
    compute(rows_3, after(other_core(rows_3), *forwards[1]))
    sums = add(1, sums)
    grad_gu, grad_down = add(2, sums)
    numbers = jnp.arange(EXPERTS, dtype=jnp.int32)
    mine = (numbers[:, None] == jnp.bitwise_xor(numbers, me)[None, :])[:, :, None]
    rows_inner = after(jnp.concatenate(inner, axis=1), *forwards[2]).reshape(EXPERTS, CAP)
    sent = jnp.sum(jnp.where(mine, rows_inner[None], 0.0), axis=1)
    returned = jnp.sum(jnp.where(mine, swap(sent)[None], 0.0), axis=1).reshape(-1)
    chosen = slots[:, None, :] == jnp.arange(EXPERTS * CAP, dtype=jnp.int32)[None, :, None]
    grad_probs = jnp.sum(jnp.where(chosen, returned[None, :, None], 0.0), axis=1) / probs
    return (grad_probs.T, grad_gu[None], grad_down[None])


def widen(values, slices, expert_count):
    tail = values.shape[1:]
    spread = values.reshape((EXPERTS, 1, CAP) + tail)
    spread = jnp.broadcast_to(spread, (EXPERTS, slices, CAP) + tail)
    return spread.reshape((expert_count, CAP) + tail)


def sliced_body(tokens, cotangent, gate_probs, expert_ids, gate_up, down):
    expert_count = lax.axis_size("expert")
    slices = expert_count // EXPERTS
    tok_count, width = tokens.shape
    choose_count = expert_ids.shape[1]
    half = gate_up.shape[2] // 2
    slot_rows = EXPERTS * CAP
    flat_ids = expert_ids.reshape(-1)
    choose = (flat_ids[:, None] == jnp.arange(EXPERTS, dtype=jnp.int32)[None, :]).astype(jnp.int32)
    earlier = jnp.cumsum(choose, axis=0) - choose
    slot_of = flat_ids * CAP + jnp.sum(earlier * choose, axis=1)
    picked = jnp.arange(slot_rows, dtype=jnp.int32)[:, None] == slot_of[None, :]
    picked_tok = jnp.any(picked.reshape(slot_rows, tok_count, choose_count), axis=2).astype(BF16)
    slot_prob = jnp.sum(jnp.where(picked, gate_probs.reshape(-1)[None, :], 0.0), axis=1)
    local_x = jnp.dot(picked_tok, tokens, preferred_element_type=F32).astype(BF16)
    local_dy = jnp.dot(picked_tok, cotangent, preferred_element_type=F32)
    local_scaled = (slot_prob[:, None] * local_dy).astype(BF16)
    rows_x = swap(widen(local_x, slices, expert_count)).reshape(-1, width)
    rows_s = swap(widen(local_scaled, slices, expert_count)).reshape(-1, width)
    both = jnp.dot(rows_x, gate_up[0], preferred_element_type=F32)
    gate, up = both[:, :half], both[:, half:]
    sigmoid = jax.nn.sigmoid(gate)
    activated = gate * sigmoid
    hidden = (activated * up).astype(BF16)
    grad_hidden = lax.dot_general(
        rows_s, down[0], (((1,), (1,)), ((), ())), preferred_element_type=F32
    )
    inner = jnp.sum(hidden.astype(F32) * grad_hidden, axis=1)
    grad_gate = (grad_hidden * up * sigmoid * (1.0 + gate * (1.0 - sigmoid))).astype(BF16)
    grad_up = (grad_hidden * activated).astype(BF16)
    grad_both = jnp.concatenate([grad_gate, grad_up], axis=1)
    over_rows = (((0,), (0,)), ((), ()))
    grad_gu = lax.dot_general(rows_x, grad_both, over_rows, preferred_element_type=F32)
    grad_down = lax.dot_general(hidden, rows_s, over_rows, preferred_element_type=F32)
    returned = swap(inner.reshape(expert_count, CAP))
    per_slot = jnp.sum(returned.reshape(EXPERTS, slices, CAP), axis=1).reshape(slot_rows)
    grad_probs = jnp.sum(jnp.where(picked, per_slot[:, None], 0.0), axis=0)
    grad_probs = grad_probs.reshape(tok_count, choose_count) / gate_probs
    reduced_gu = lax.psum_scatter(grad_gu.astype(BF16), "dp", scatter_dimension=0, tiled=True)
    reduced_down = lax.psum_scatter(grad_down.astype(BF16), "dp", scatter_dimension=1, tiled=True)
    return (grad_probs, reduced_gu[None], reduced_down[None])


def solution(mesh):
    whole_experts = mesh.shape["expert"] == EXPERTS and mesh.shape["dp"] == 4
    return jax.shard_map(
        plane_body if whole_experts else sliced_body,
        mesh=mesh,
        in_specs=(
            P(("dp", "expert"), None),
            P(("dp", "expert"), None),
            P(("dp", "expert"), None),
            P(("dp", "expert"), None),
            P("expert", None, None),
            P("expert", None, None),
        ),
        out_specs=(P(("dp", "expert"), None), P("expert", "dp", None), P("expert", None, "dp")),
        check_vma=False,
    )
```

```python
import functools

import jax
import jax.numpy as jnp
from jax import lax
from jax.experimental import pallas as pl
from jax.experimental.pallas import tpu as pltpu
from jax.sharding import PartitionSpec as P

EXPERTS = 8
CAP = 40
PAIR = 2 * CAP
TILE = 256
MIB = 1024 * 1024
BF16 = jnp.bfloat16
F32 = jnp.float32


def dispatch_kernel(ids_ref, probs_ref, x_ref, dy_ref, *outs):
    row_refs, slot_ref = outs[:-1], outs[-1]
    me = lax.axis_index("expert")
    tok = x_ref.shape[0]
    width = x_ref.shape[1]
    numbers = lax.broadcasted_iota(jnp.int32, (EXPERTS, tok), 0)
    first = jnp.bitwise_xor(ids_ref[0:1, :], me) == numbers
    second = jnp.bitwise_xor(ids_ref[1:2, :], me) == numbers
    either = jnp.where(first | second, 1.0, 0.0)
    prob = jnp.where(first, probs_ref[0:1, :], 0.0) + jnp.where(second, probs_ref[1:2, :], 0.0)
    before = jnp.where(
        lax.broadcasted_iota(jnp.int32, (tok, tok), 0)
        < lax.broadcasted_iota(jnp.int32, (tok, tok), 1),
        1.0,
        0.0,
    )
    position = jnp.dot(either.astype(BF16), before.astype(BF16), preferred_element_type=F32)
    slot = position.astype(jnp.int32) + numbers * CAP
    slot_ref[0:1, :] = jnp.sum(jnp.where(first, slot, 0), axis=0, keepdims=True)
    slot_ref[1:2, :] = jnp.sum(jnp.where(second, slot, 0), axis=0, keepdims=True)
    target = jnp.where(either > 0.5, position, -1.0)
    places = lax.broadcasted_iota(jnp.int32, (CAP, tok), 0).astype(F32)
    picks = [
        jnp.where(places == target[e : e + 1, :], 1.0, 0.0) for e in range(EXPERTS)
    ]
    row_prob = jnp.concatenate(
        [jnp.sum(picks[e] * prob[e : e + 1, :], axis=1, keepdims=True) for e in range(EXPERTS)],
        axis=0,
    )
    pick = jnp.concatenate(picks, axis=0).astype(BF16)
    step = 512
    for at in range(0, width, step):
        rows_x = jnp.dot(pick, x_ref[:, at : at + step], preferred_element_type=F32)
        rows_dy = jnp.dot(pick, dy_ref[:, at : at + step], preferred_element_type=F32)
        scaled = row_prob * rows_dy
        for pair, ref in enumerate(row_refs):
            part = slice(pair * PAIR, (pair + 1) * PAIR)
            ref[:, at : at + step] = rows_x[part].astype(BF16)
            ref[:, width + at : width + at + step] = scaled[part].astype(BF16)


def dispatch_rows(ids, probs, tokens, cotangent):
    tok, width = tokens.shape
    return pl.pallas_call(
        dispatch_kernel,
        out_shape=[jax.ShapeDtypeStruct((PAIR, 2 * width), BF16)] * (EXPERTS // 2)
        + [jax.ShapeDtypeStruct((2, tok), jnp.int32)],
        compiler_params=pltpu.CompilerParams(vmem_limit_bytes=16 * MIB),
        cost_estimate=pl.CostEstimate(
            flops=4 * EXPERTS * CAP * tok * width, bytes_accessed=4_000_000, transcendentals=0
        ),
        name="dispatch_rows",
    )(ids, probs, tokens, cotangent)


def split_rows(count, top, half):
    blocks = 3 * half // TILE
    low = count - top
    from_x, from_y = (blocks + 4) * top, (blocks + 4) * low
    sizes = (from_x + blocks * low + 4 * count, from_y + blocks * top + 4 * count)
    return blocks, low, from_x, from_y, sizes


def expert_kernel(pairs, top, relays, *refs):
    row_refs, refs = refs[: 2 * pairs], refs[2 * pairs :]
    (gu_hbm, down_hbm), refs = refs[:2], refs[2:]
    relay_refs, refs = refs[: len(relays)], refs[len(relays) :]
    own_ref, to_x, to_y, inner_ref, gu_tiles, down_tiles, x_rows, s_turned, sems = refs
    count = pairs * PAIR
    width, both = gu_hbm.shape
    half = both // 2
    quarter = width // 4
    steps = half // TILE
    blocks, low, from_x, from_y, sizes = split_rows(count, top, half)
    group = lax.axis_index("dp")
    copies = []
    for step in range(steps):
        for n, at in enumerate((step * TILE, half + step * TILE)):
            copies.append(
                pltpu.make_async_copy(
                    gu_hbm.at[:, at : at + TILE], gu_tiles.at[2 * step + n], sems.at[3 * step + n]
                )
            )
        copies.append(
            pltpu.make_async_copy(
                down_hbm.at[step * TILE : (step + 1) * TILE, :],
                down_tiles.at[step],
                sems.at[3 * step + 2],
            )
        )
    for copy in copies:
        copy.start()
    for ref, relay, rows, at in zip((to_x, to_y), relay_refs, relays, sizes):
        ref[at : at + rows] = relay[:rows]

    for n, start in enumerate((0, width)):
        x_rows[n] = jnp.concatenate(
            [ref[:CAP, start : start + width].astype(F32) for ref in row_refs], axis=0
        ).astype(BF16)
    s_turned[...] = x_rows[1].T
    for q in range(4):

        def cut(mask):
            at = jnp.bitwise_xor(group, mask) * quarter + q % 2 * TILE
            return x_rows[q // 2, :, pl.ds(pl.multiple_of(at, TILE), TILE)]

        at = blocks + q
        own_ref[at * count : (at + 1) * count] = cut(0)
        far = cut(3)
        to_x[at * top : (at + 1) * top] = far[:top]
        to_y[at * low : (at + 1) * low] = far[top:]
        start = from_x + blocks * low + q * count
        to_x[start : start + count] = cut(1)
        start = from_y + blocks * top + q * count
        to_y[start : start + count] = cut(2)

    total = jnp.zeros((count, 1), F32)
    for step in range(steps):
        for copy in copies[3 * step : 3 * step + 3]:
            copy.wait()
        x = x_rows[0]
        gate = jnp.dot(x, gu_tiles[2 * step], preferred_element_type=F32)
        up = jnp.dot(x, gu_tiles[2 * step + 1], preferred_element_type=F32)
        grad_hidden = jnp.dot(down_tiles[step], s_turned[...], preferred_element_type=F32).T
        sigmoid = 1.0 / (1.0 + jnp.exp(-gate))
        activated = gate * sigmoid
        hidden = (activated * up).astype(BF16)
        grad_gate = (grad_hidden * up * sigmoid * (1.0 + gate * (1.0 - sigmoid))).astype(BF16)
        grad_up = (grad_hidden * activated).astype(BF16)
        total += jnp.sum(hidden.astype(F32) * grad_hidden, axis=1, keepdims=True)
        for part, values in enumerate((grad_gate, grad_up, hidden)):
            block = part * steps + step
            own_ref[block * count : (block + 1) * count] = values
            to_x[block * top : (block + 1) * top] = values[:top]
            to_x[from_x + block * low : from_x + (block + 1) * low] = values[top:]
            to_y[block * low : (block + 1) * low] = values[top:]
            to_y[from_y + block * top : from_y + (block + 1) * top] = values[:top]
    inner_ref[...] = jnp.broadcast_to(total, (count, 128)).T[0:1]


def expert_rows(rows, weight_gu, weight_down, top, relay=(), relays=(), room=26):
    pairs = len(rows) // 2
    count = pairs * PAIR
    width, both = weight_gu.shape
    half = both // 2
    steps = half // TILE
    blocks, _, _, _, sizes = split_rows(count, top, half)
    sizes = [(blocks + 4) * count] + [
        size + extra for size, extra in zip(sizes, relays or (0, 0))
    ]
    vmem = pl.BlockSpec(memory_space=pltpu.VMEM)
    hbm = pl.BlockSpec(memory_space=pl.ANY)
    return pl.pallas_call(
        functools.partial(expert_kernel, pairs, top, tuple(relays)),
        in_specs=[vmem] * len(rows) + [hbm] * 2 + [vmem] * len(relay),
        out_specs=[vmem] * 4,
        out_shape=[jax.ShapeDtypeStruct((size, TILE), BF16) for size in sizes]
        + [jax.ShapeDtypeStruct((1, count), F32)],
        scratch_shapes=[
            pltpu.VMEM((2 * steps, width, TILE), BF16),
            pltpu.VMEM((steps, TILE, width), BF16),
            pltpu.VMEM((2, count, width), BF16),
            pltpu.VMEM((width, count), BF16),
            pltpu.SemaphoreType.DMA((3 * steps,)),
        ],
        compiler_params=pltpu.CompilerParams(vmem_limit_bytes=room * MIB),
        cost_estimate=pl.CostEstimate(flops=1_000, bytes_accessed=1_000, transcendentals=0),
        name="expert_rows",
    )(*rows, weight_gu, weight_down, *relay)


def gradient_kernel(chunks, half, adding, *refs):
    groups, refs = (
        [refs[5 * n : 5 * n + 5] for n in range(len(chunks))],
        refs[5 * len(chunks) :],
    )
    if adding:
        (acc_gu, acc_down), refs = refs[:2], refs[2:]
    out_gu, out_down, turned, s_rows = refs
    both = 2 * half // TILE

    def far_parts(block, top, low, at_top, at_low, far_top, far_low):
        return [
            far_top[at_top + block * top : at_top + (block + 1) * top],
            far_low[at_low + block * low : at_low + (block + 1) * low],
        ]

    def factor(block):
        parts = []
        for (count, top, at_top, at_low), group in zip(chunks, groups):
            own, got_x, got_y, *far = group
            _, low, from_x, from_y, _ = split_rows(count, top, half)
            parts += [
                own[block * count : (block + 1) * count],
                got_x[block * top : (block + 1) * top],
                got_x[from_x + block * low : from_x + (block + 1) * low],
                got_y[from_y + block * top : from_y + (block + 1) * top],
                got_y[block * low : (block + 1) * low],
            ] + far_parts(block, top, low, at_top, at_low, *far)
        return jnp.concatenate(parts, axis=0)

    def piece(q):
        parts = []
        for (count, top, at_top, at_low), group in zip(chunks, groups):
            own, got_x, got_y, *far = group
            blocks, low, from_x, from_y, _ = split_rows(count, top, half)
            block = blocks + q
            at_x = from_x + blocks * low + q * count
            at_y = from_y + blocks * top + q * count
            parts += [
                own[block * count : (block + 1) * count],
                got_x[at_x : at_x + count],
                got_y[at_y : at_y + count],
            ] + far_parts(block, top, low, at_top, at_low, *far)
        return jnp.concatenate(parts, axis=0)

    for q in range(2):
        turned[q * TILE : (q + 1) * TILE, :] = piece(q).T
        s_rows[:, q * TILE : (q + 1) * TILE] = piece(2 + q)
    for block in range(both):
        at = slice(block * TILE, (block + 1) * TILE)
        grad = jnp.dot(turned[...], factor(block), preferred_element_type=F32)
        if adding:
            grad = grad + acc_gu[:, at]
        out_gu[:, at] = grad.astype(out_gu.dtype)
    for block in range(half // TILE):
        at = slice(block * TILE, (block + 1) * TILE)
        grad = jnp.dot(factor(both + block).T, s_rows[...], preferred_element_type=F32)
        if adding:
            grad = grad + acc_down[at, :]
        out_down[at, :] = grad.astype(out_down.dtype)


def gradients(chunks, pieces, half, quarter, sums=(), final=False):
    kept = BF16 if final else F32
    rows = 4 * sum(chunk[0] for chunk in chunks)
    vmem = pl.BlockSpec(memory_space=pltpu.VMEM)
    return pl.pallas_call(
        functools.partial(gradient_kernel, chunks, half, len(sums)),
        in_specs=[vmem] * (len(pieces) + len(sums)),
        out_specs=[vmem] * 2,
        out_shape=[
            jax.ShapeDtypeStruct((quarter, 2 * half), kept),
            jax.ShapeDtypeStruct((half, quarter), kept),
        ],
        scratch_shapes=[pltpu.VMEM((quarter, rows), BF16), pltpu.VMEM((rows, quarter), BF16)],
        compiler_params=pltpu.CompilerParams(vmem_limit_bytes=20 * MIB),
        cost_estimate=pl.CostEstimate(flops=1_000, bytes_accessed=1_000, transcendentals=0),
        name="gradients",
    )(*pieces, *sums)


def exchange(values, axis, mask):
    size = lax.axis_size(axis)
    return lax.ppermute(values, axis, [(n, n ^ mask) for n in range(size)])


def swap(values):
    return lax.all_to_all(values, "expert", split_axis=0, concat_axis=0, tiled=True)


def after(values, *others):
    return lax.optimization_barrier((values,) + others)[0]


def plane_body(tokens, cotangent, gate_probs, expert_ids, gate_up, down):
    me = lax.axis_index("expert")
    half = gate_up.shape[2] // 2
    quarter = tokens.shape[1] // 4
    ids, probs = expert_ids.T, gate_probs.T
    *local, slots = dispatch_rows(ids, probs, tokens, cotangent)
    weights = (gate_up[0], down[0])
    _, _, cut_x0, cut_y0, _ = split_rows(PAIR, 48, half)
    _, _, cut_x1, cut_y1, sizes = split_rows(2 * PAIR, PAIR, half)
    _, _, cut_x2, cut_y2, _ = split_rows(PAIR, 32, half)

    def other_core(rows):
        return exchange(rows[CAP:], "expert", 1)

    def to_plane(to_x, to_y):
        return exchange(to_x, "dp", 1), exchange(to_y, "dp", 2)

    rows_1 = exchange(local[1], "expert", 2)
    rows_2 = exchange(local[2], "expert", 4)
    own_0, to_x, to_y, inner_0 = expert_rows(
        (local[0], other_core(local[0])), *weights, 48, room=58
    )
    got_x0, got_y0 = to_plane(to_x, to_y)
    rows_1 = after(rows_1, inner_0)
    rows_3 = exchange(after(local[3], rows_2), "expert", 6)
    rows_2 = after(rows_2, inner_0)
    own_1, to_x, to_y, inner_1 = expert_rows(
        (rows_1, other_core(rows_1), rows_2, other_core(rows_2)),
        *weights,
        PAIR,
        (got_y0, got_x0),
        (cut_y0, cut_x0),
    )
    got_x1, got_y1 = to_plane(to_x, to_y)
    rows_3 = after(rows_3, inner_1)
    own_2, to_x, to_y, inner_2 = expert_rows((rows_3, other_core(rows_3)), *weights, 32)
    got_x2, got_y2 = to_plane(to_x, to_y)
    got_x1, got_y1 = after((got_x1, got_y1), inner_2)
    turn_1 = (got_y1[:cut_y1], got_x1[:cut_x1])
    low_1, top_1 = to_plane(*turn_1)
    sums = gradients(
        ((PAIR, 48, sizes[1], sizes[0]),),
        (own_0, got_x0, got_y0, got_y1, got_x1),
        half,
        quarter,
    )
    numbers = jnp.arange(EXPERTS, dtype=jnp.int32)
    mine = (numbers[:, None] == jnp.bitwise_xor(numbers, me)[None, :])[:, :, None]
    inner = jnp.concatenate([inner_0, inner_1, inner_2], axis=1)
    rows_inner = after(inner, *turn_1).reshape(EXPERTS, CAP)
    returned = swap(jnp.sum(jnp.where(mine, rows_inner[None], 0.0), axis=1))
    got_x2, got_y2 = after((got_x2, got_y2), returned, *sums)
    low_2, top_2 = to_plane(got_y2[:cut_y2], got_x2[:cut_x2])
    grad_gu, grad_down = gradients(
        ((2 * PAIR, PAIR, 0, 0), (PAIR, 32, 0, 0)),
        (own_1, got_x1, got_y1, top_1, low_1, own_2, got_x2, got_y2, top_2, low_2),
        half,
        quarter,
        sums,
        True,
    )
    returned = jnp.sum(jnp.where(mine, returned[None], 0.0), axis=1).reshape(-1)
    chosen = slots[:, None, :] == jnp.arange(EXPERTS * CAP, dtype=jnp.int32)[None, :, None]
    grad_probs = jnp.sum(jnp.where(chosen, returned[None, :, None], 0.0), axis=1) / probs
    return (grad_probs.T, grad_gu[None], grad_down[None])


def widen(values, slices, expert_count):
    tail = values.shape[1:]
    spread = values.reshape((EXPERTS, 1, CAP) + tail)
    spread = jnp.broadcast_to(spread, (EXPERTS, slices, CAP) + tail)
    return spread.reshape((expert_count, CAP) + tail)


def sliced_body(tokens, cotangent, gate_probs, expert_ids, gate_up, down):
    expert_count = lax.axis_size("expert")
    slices = expert_count // EXPERTS
    tok_count, width = tokens.shape
    choose_count = expert_ids.shape[1]
    half = gate_up.shape[2] // 2
    slot_rows = EXPERTS * CAP
    flat_ids = expert_ids.reshape(-1)
    choose = (flat_ids[:, None] == jnp.arange(EXPERTS, dtype=jnp.int32)[None, :]).astype(jnp.int32)
    earlier = jnp.cumsum(choose, axis=0) - choose
    slot_of = flat_ids * CAP + jnp.sum(earlier * choose, axis=1)
    picked = jnp.arange(slot_rows, dtype=jnp.int32)[:, None] == slot_of[None, :]
    picked_tok = jnp.any(picked.reshape(slot_rows, tok_count, choose_count), axis=2).astype(BF16)
    slot_prob = jnp.sum(jnp.where(picked, gate_probs.reshape(-1)[None, :], 0.0), axis=1)
    local_x = jnp.dot(picked_tok, tokens, preferred_element_type=F32).astype(BF16)
    local_dy = jnp.dot(picked_tok, cotangent, preferred_element_type=F32)
    local_scaled = (slot_prob[:, None] * local_dy).astype(BF16)
    rows_x = swap(widen(local_x, slices, expert_count)).reshape(-1, width)
    rows_s = swap(widen(local_scaled, slices, expert_count)).reshape(-1, width)
    both = jnp.dot(rows_x, gate_up[0], preferred_element_type=F32)
    gate, up = both[:, :half], both[:, half:]
    sigmoid = jax.nn.sigmoid(gate)
    activated = gate * sigmoid
    hidden = (activated * up).astype(BF16)
    grad_hidden = lax.dot_general(
        rows_s, down[0], (((1,), (1,)), ((), ())), preferred_element_type=F32
    )
    inner = jnp.sum(hidden.astype(F32) * grad_hidden, axis=1)
    grad_gate = (grad_hidden * up * sigmoid * (1.0 + gate * (1.0 - sigmoid))).astype(BF16)
    grad_up = (grad_hidden * activated).astype(BF16)
    grad_both = jnp.concatenate([grad_gate, grad_up], axis=1)
    over_rows = (((0,), (0,)), ((), ()))
    grad_gu = lax.dot_general(rows_x, grad_both, over_rows, preferred_element_type=F32)
    grad_down = lax.dot_general(hidden, rows_s, over_rows, preferred_element_type=F32)
    returned = swap(inner.reshape(expert_count, CAP))
    per_slot = jnp.sum(returned.reshape(EXPERTS, slices, CAP), axis=1).reshape(slot_rows)
    grad_probs = jnp.sum(jnp.where(picked, per_slot[:, None], 0.0), axis=0)
    grad_probs = grad_probs.reshape(tok_count, choose_count) / gate_probs
    reduced_gu = lax.psum_scatter(grad_gu.astype(BF16), "dp", scatter_dimension=0, tiled=True)
    reduced_down = lax.psum_scatter(grad_down.astype(BF16), "dp", scatter_dimension=1, tiled=True)
    return (grad_probs, reduced_gu[None], reduced_down[None])


def solution(mesh):
    whole_experts = mesh.shape["expert"] == EXPERTS and mesh.shape["dp"] == 4
    return jax.shard_map(
        plane_body if whole_experts else sliced_body,
        mesh=mesh,
        in_specs=(
            P(("dp", "expert"), None),
            P(("dp", "expert"), None),
            P(("dp", "expert"), None),
            P(("dp", "expert"), None),
            P("expert", None, None),
            P("expert", None, None),
        ),
        out_specs=(P(("dp", "expert"), None), P("expert", "dp", None), P("expert", None, "dp")),
        check_vma=False,
    )
```

```python
import functools

import jax
import jax.numpy as jnp
from jax import lax
from jax.experimental import pallas as pl
from jax.experimental.pallas import tpu as pltpu
from jax.sharding import PartitionSpec as P

EXPERTS = 8
CAP = 40
PAIR = 2 * CAP
LANES = 128
TILE = 256
MIB = 1024 * 1024
BF16 = jnp.bfloat16
F32 = jnp.float32


def dispatch_kernel(ids_ref, probs_ref, x_ref, dy_ref, *outs):
    row_refs, slot_ref = outs[:-1], outs[-1]
    me = lax.axis_index("expert")
    tok = x_ref.shape[0]
    width = x_ref.shape[1]
    numbers = lax.broadcasted_iota(jnp.int32, (EXPERTS, tok), 0)
    first = jnp.bitwise_xor(ids_ref[0:1, :], me) == numbers
    second = jnp.bitwise_xor(ids_ref[1:2, :], me) == numbers
    either = jnp.where(first | second, 1.0, 0.0)
    prob = jnp.where(first, probs_ref[0:1, :], 0.0) + jnp.where(second, probs_ref[1:2, :], 0.0)
    before = jnp.where(
        lax.broadcasted_iota(jnp.int32, (tok, tok), 0)
        < lax.broadcasted_iota(jnp.int32, (tok, tok), 1),
        1.0,
        0.0,
    )
    position = jnp.dot(either.astype(BF16), before.astype(BF16), preferred_element_type=F32)
    slot = position.astype(jnp.int32) + numbers * CAP
    slot_ref[0:1, :] = jnp.sum(jnp.where(first, slot, 0), axis=0, keepdims=True)
    slot_ref[1:2, :] = jnp.sum(jnp.where(second, slot, 0), axis=0, keepdims=True)
    target = jnp.where(either > 0.5, position, -1.0)
    places = lax.broadcasted_iota(jnp.int32, (CAP, tok), 0).astype(F32)
    picks = [
        jnp.where(places == target[e : e + 1, :], 1.0, 0.0) for e in range(EXPERTS)
    ]
    row_prob = jnp.concatenate(
        [jnp.sum(picks[e] * prob[e : e + 1, :], axis=1, keepdims=True) for e in range(EXPERTS)],
        axis=0,
    )
    pick = jnp.concatenate(picks, axis=0).astype(BF16)
    step = 512
    for at in range(0, width, step):
        rows_x = jnp.dot(pick, x_ref[:, at : at + step], preferred_element_type=F32)
        rows_dy = jnp.dot(pick, dy_ref[:, at : at + step], preferred_element_type=F32)
        scaled = row_prob * rows_dy
        for pair, ref in enumerate(row_refs):
            part = slice(pair * PAIR, (pair + 1) * PAIR)
            ref[:, at : at + step] = rows_x[part].astype(BF16)
            ref[:, width + at : width + at + step] = scaled[part].astype(BF16)


def dispatch_rows(ids, probs, tokens, cotangent):
    tok, width = tokens.shape
    return pl.pallas_call(
        dispatch_kernel,
        out_shape=[jax.ShapeDtypeStruct((PAIR, 2 * width), BF16)] * (EXPERTS // 2)
        + [jax.ShapeDtypeStruct((2, tok), jnp.int32)],
        compiler_params=pltpu.CompilerParams(vmem_limit_bytes=16 * MIB),
        cost_estimate=pl.CostEstimate(
            flops=4 * EXPERTS * CAP * tok * width, bytes_accessed=4_000_000, transcendentals=0
        ),
        name="dispatch_rows",
    )(ids, probs, tokens, cotangent)


def split_rows(count, top, half):
    blocks = 3 * half // TILE
    low = count - top
    from_x, from_y = (blocks + 4) * top, (blocks + 4) * low
    sizes = (from_x + blocks * low + 4 * count, from_y + blocks * top + 4 * count)
    return blocks, low, from_x, from_y, sizes


def expert_kernel(pairs, top, relays, *refs):
    row_refs, (gate_ref, up_ref, down_ref), rest = (
        refs[: 2 * pairs],
        refs[2 * pairs : 2 * pairs + 3],
        refs[2 * pairs + 3 :],
    )
    relay_refs, rest = rest[: len(relays)], rest[len(relays) :]
    own_ref, to_x, to_y, *inner_refs, x_rows, s_rows, s_turned, total = rest
    count = pairs * PAIR
    width = gate_ref.shape[0]
    steps = pl.num_programs(0)
    half = TILE * 3
    quarter = width // 4
    blocks, low, from_x, from_y, sizes = split_rows(count, top, half)
    step = pl.program_id(0)
    group = lax.axis_index("dp")

    @pl.when(step == 0)
    def _():
        for ref, relay, size, at in zip((to_x, to_y), relay_refs, relays, sizes):
            ref[at : at + size] = relay[:size]
        for rows, start in ((x_rows, 0), (s_rows, width)):
            rows[...] = jnp.concatenate(
                [ref[:CAP, start : start + width].astype(F32) for ref in row_refs],
                axis=0,
            ).astype(BF16)
        for q in range(4):
            rows = (x_rows, s_rows)[q // 2]

            def cut(mask):
                at = jnp.bitwise_xor(group, mask) * quarter + q % 2 * TILE
                return rows[:, pl.ds(pl.multiple_of(at, TILE), TILE)]

            at = blocks + q
            own_ref[at * count : (at + 1) * count] = cut(0)
            far = cut(3)
            to_x[at * top : (at + 1) * top] = far[:top]
            to_y[at * low : (at + 1) * low] = far[top:]
            start = from_x + blocks * low + q * count
            to_x[start : start + count] = cut(1)
            start = from_y + blocks * top + q * count
            to_y[start : start + count] = cut(2)
        s_turned[...] = s_rows[...].T
        total[...] = jnp.zeros_like(total)

    x = x_rows[...]
    gate = jnp.dot(x, gate_ref[...], preferred_element_type=F32)
    up = jnp.dot(x, up_ref[...], preferred_element_type=F32)
    grad_hidden = jnp.dot(down_ref[...], s_turned[...], preferred_element_type=F32).T
    sigmoid = 1.0 / (1.0 + jnp.exp(-gate))
    activated = gate * sigmoid
    hidden = (activated * up).astype(BF16)
    grad_gate = (grad_hidden * up * sigmoid * (1.0 + gate * (1.0 - sigmoid))).astype(BF16)
    grad_up = (grad_hidden * activated).astype(BF16)
    total[...] += jnp.sum(hidden.astype(F32) * grad_hidden, axis=1, keepdims=True)
    for part, values in enumerate((grad_gate, grad_up, hidden)):
        block = part * steps + step

        def rows_at(start, count):
            return pl.ds(pl.multiple_of(start + block * count, 16), count)

        own_ref[rows_at(0, count)] = values
        to_x[rows_at(0, top)] = values[:top]
        to_x[rows_at(from_x, low)] = values[top:]
        to_y[rows_at(0, low)] = values[top:]
        to_y[rows_at(from_y, top)] = values[:top]

    @pl.when(step == steps - 1)
    def _():
        for pair, ref in enumerate(inner_refs):
            part = total[pair * PAIR : (pair + 1) * PAIR]
            ref[...] = jnp.broadcast_to(part, ref.shape)


def expert_rows(rows, weight_gu, weight_down, top, relay=(), relays=()):
    pairs = len(rows) // 2
    count = pairs * PAIR
    width, both = weight_gu.shape
    half = both // 2
    steps = half // TILE
    blocks, _, _, _, sizes = split_rows(count, top, half)
    sizes = [(blocks + 4) * count] + [
        size + extra for size, extra in zip(sizes, relays or (0, 0))
    ]
    shapes = [(size, TILE) for size in sizes]

    def whole(shape):
        return pl.BlockSpec(shape, lambda h: (0, 0))

    return pl.pallas_call(
        functools.partial(expert_kernel, pairs, top, tuple(relays)),
        grid=(steps,),
        in_specs=[
            *[whole(part.shape) for part in rows],
            pl.BlockSpec((width, TILE), lambda h: (0, h)),
            pl.BlockSpec((width, TILE), lambda h: (0, h + steps)),
            pl.BlockSpec((TILE, width), lambda h: (h, 0)),
            *[whole(part.shape) for part in relay],
        ],
        out_specs=[whole(shape) for shape in shapes] + [whole((PAIR, LANES))] * pairs,
        out_shape=[jax.ShapeDtypeStruct(shape, BF16) for shape in shapes]
        + [jax.ShapeDtypeStruct((PAIR, LANES), F32)] * pairs,
        scratch_shapes=[
            pltpu.VMEM((count, width), BF16),
            pltpu.VMEM((count, width), BF16),
            pltpu.VMEM((width, count), BF16),
            pltpu.VMEM((count, 1), F32),
        ],
        compiler_params=pltpu.CompilerParams(vmem_limit_bytes=20 * MIB),
        cost_estimate=pl.CostEstimate(flops=1_000, bytes_accessed=1_000, transcendentals=0),
        name="expert_rows",
    )(*rows, weight_gu, weight_gu, weight_down, *relay)


def gradient_kernel(chunks, half, adding, *refs):
    groups, refs = (
        [refs[5 * n : 5 * n + 5] for n in range(len(chunks))],
        refs[5 * len(chunks) :],
    )
    if adding:
        (acc_gu, acc_down), refs = refs[:2], refs[2:]
    out_gu, out_down, turned, s_rows = refs
    both = 2 * half // TILE

    def far_parts(block, top, low, at_top, at_low, far_top, far_low):
        return [
            far_top[at_top + block * top : at_top + (block + 1) * top],
            far_low[at_low + block * low : at_low + (block + 1) * low],
        ]

    def factor(block):
        parts = []
        for (count, top, at_top, at_low), group in zip(chunks, groups):
            own, got_x, got_y, *far = group
            _, low, from_x, from_y, _ = split_rows(count, top, half)
            parts += [
                own[block * count : (block + 1) * count],
                got_x[block * top : (block + 1) * top],
                got_x[from_x + block * low : from_x + (block + 1) * low],
                got_y[from_y + block * top : from_y + (block + 1) * top],
                got_y[block * low : (block + 1) * low],
            ] + far_parts(block, top, low, at_top, at_low, *far)
        return jnp.concatenate(parts, axis=0)

    def piece(q):
        parts = []
        for (count, top, at_top, at_low), group in zip(chunks, groups):
            own, got_x, got_y, *far = group
            blocks, low, from_x, from_y, _ = split_rows(count, top, half)
            block = blocks + q
            at_x = from_x + blocks * low + q * count
            at_y = from_y + blocks * top + q * count
            parts += [
                own[block * count : (block + 1) * count],
                got_x[at_x : at_x + count],
                got_y[at_y : at_y + count],
            ] + far_parts(block, top, low, at_top, at_low, *far)
        return jnp.concatenate(parts, axis=0)

    for q in range(2):
        turned[q * TILE : (q + 1) * TILE, :] = piece(q).T
        s_rows[:, q * TILE : (q + 1) * TILE] = piece(2 + q)
    for block in range(both):
        at = slice(block * TILE, (block + 1) * TILE)
        grad = jnp.dot(turned[...], factor(block), preferred_element_type=F32)
        if adding:
            grad = grad + acc_gu[:, at]
        out_gu[:, at] = grad.astype(out_gu.dtype)
    for block in range(half // TILE):
        at = slice(block * TILE, (block + 1) * TILE)
        grad = jnp.dot(factor(both + block).T, s_rows[...], preferred_element_type=F32)
        if adding:
            grad = grad + acc_down[at, :]
        out_down[at, :] = grad.astype(out_down.dtype)


def gradients(chunks, pieces, half, quarter, sums=(), final=False):
    kept = BF16 if final else F32
    rows = 4 * sum(chunk[0] for chunk in chunks)
    vmem = pl.BlockSpec(memory_space=pltpu.VMEM)
    return pl.pallas_call(
        functools.partial(gradient_kernel, chunks, half, len(sums)),
        in_specs=[vmem] * (len(pieces) + len(sums)),
        out_specs=[vmem] * 2,
        out_shape=[
            jax.ShapeDtypeStruct((quarter, 2 * half), kept),
            jax.ShapeDtypeStruct((half, quarter), kept),
        ],
        scratch_shapes=[pltpu.VMEM((quarter, rows), BF16), pltpu.VMEM((rows, quarter), BF16)],
        compiler_params=pltpu.CompilerParams(vmem_limit_bytes=20 * MIB),
        cost_estimate=pl.CostEstimate(flops=1_000, bytes_accessed=1_000, transcendentals=0),
        name="gradients",
    )(*pieces, *sums)


def prob_kernel(own_0, own_1, own_2, own_3, other_ref, slot_ref, prob_ref, out_ref):
    owns = (own_0, own_1, own_2, own_3)
    tok = slot_ref.shape[1]
    places = lax.broadcasted_iota(jnp.int32, (CAP, tok), 0)
    for choice in range(2):
        slot = slot_ref[choice : choice + 1, :]
        grad = jnp.zeros((CAP, tok), F32)
        for e in range(EXPERTS):
            chunk = e // 2
            if e % 2 == 0:
                values = owns[chunk][:CAP, :]
            else:
                values = other_ref[chunk * CAP : (chunk + 1) * CAP, :]
            grad += jnp.where(places + e * CAP == slot, values, 0.0)
        grad = jnp.sum(grad, axis=0, keepdims=True)
        out_ref[choice : choice + 1, :] = grad / prob_ref[choice : choice + 1, :]


def prob_gradients(owns, other, slots, probs):
    return pl.pallas_call(
        prob_kernel,
        out_shape=jax.ShapeDtypeStruct(probs.shape, F32),
        compiler_params=pltpu.CompilerParams(vmem_limit_bytes=4 * MIB),
        cost_estimate=pl.CostEstimate(flops=1_000, bytes_accessed=1_000, transcendentals=0),
        name="prob_gradients",
    )(*owns, other, slots, probs)


def exchange(values, axis, mask):
    size = lax.axis_size(axis)
    return lax.ppermute(values, axis, [(n, n ^ mask) for n in range(size)])


def swap(values):
    return lax.all_to_all(values, "expert", split_axis=0, concat_axis=0, tiled=True)


def after(values, *others):
    return lax.optimization_barrier((values,) + others)[0]


def plane_body(tokens, cotangent, gate_probs, expert_ids, gate_up, down):
    half = gate_up.shape[2] // 2
    quarter = tokens.shape[1] // 4
    ids, probs = expert_ids.T, gate_probs.T
    *local, slots = dispatch_rows(ids, probs, tokens, cotangent)
    weights = (gate_up[0], down[0])
    _, _, cut_x0, cut_y0, _ = split_rows(PAIR, 48, half)
    _, _, cut_x1, cut_y1, sizes = split_rows(2 * PAIR, PAIR, half)
    _, _, cut_x2, cut_y2, _ = split_rows(PAIR, 32, half)

    def other_core(rows):
        return exchange(rows[CAP:], "expert", 1)

    def to_plane(to_x, to_y):
        return exchange(to_x, "dp", 1), exchange(to_y, "dp", 2)

    rows_1 = exchange(local[1], "expert", 2)
    rows_2 = exchange(local[2], "expert", 4)
    own_0, to_x, to_y, inner_0 = expert_rows((local[0], other_core(local[0])), *weights, 48)
    got_x0, got_y0 = to_plane(to_x, to_y)
    rows_1 = after(rows_1, inner_0)
    rows_3 = exchange(after(local[3], rows_2), "expert", 6)
    rows_2 = after(rows_2, inner_0)
    own_1, to_x, to_y, inner_1, inner_2 = expert_rows(
        (rows_1, other_core(rows_1), rows_2, other_core(rows_2)),
        *weights,
        PAIR,
        (got_y0, got_x0),
        (cut_y0, cut_x0),
    )
    got_x1, got_y1 = to_plane(to_x, to_y)
    rows_3 = after(rows_3, inner_1)
    own_2, to_x, to_y, inner_3 = expert_rows((rows_3, other_core(rows_3)), *weights, 32)
    got_x2, got_y2 = to_plane(to_x, to_y)
    returned = [inner_0] + [
        exchange(part, "expert", 2 * n + 2)
        for n, part in enumerate((inner_1, inner_2, inner_3))
    ]
    other = exchange(
        jnp.concatenate([part[CAP:] for part in returned], axis=0), "expert", 1
    )
    got_x1, got_y1 = after((got_x1, got_y1), inner_3, other)
    turn_1 = (got_y1[:cut_y1], got_x1[:cut_x1])
    low_1, top_1 = to_plane(*turn_1)
    sums = gradients(
        ((PAIR, 48, sizes[1], sizes[0]),),
        (own_0, got_x0, got_y0, got_y1, got_x1),
        half,
        quarter,
    )
    grad_probs = prob_gradients(returned, other, slots, probs)
    got_x2, got_y2 = after((got_x2, got_y2), *sums)
    low_2, top_2 = to_plane(got_y2[:cut_y2], got_x2[:cut_x2])
    grad_gu, grad_down = gradients(
        ((2 * PAIR, PAIR, 0, 0), (PAIR, 32, 0, 0)),
        (own_1, got_x1, got_y1, top_1, low_1, own_2, got_x2, got_y2, top_2, low_2),
        half,
        quarter,
        sums,
        True,
    )
    return (grad_probs.T, grad_gu[None], grad_down[None])


def widen(values, slices, expert_count):
    tail = values.shape[1:]
    spread = values.reshape((EXPERTS, 1, CAP) + tail)
    spread = jnp.broadcast_to(spread, (EXPERTS, slices, CAP) + tail)
    return spread.reshape((expert_count, CAP) + tail)


def sliced_body(tokens, cotangent, gate_probs, expert_ids, gate_up, down):
    expert_count = lax.axis_size("expert")
    slices = expert_count // EXPERTS
    tok_count, width = tokens.shape
    choose_count = expert_ids.shape[1]
    half = gate_up.shape[2] // 2
    slot_rows = EXPERTS * CAP
    flat_ids = expert_ids.reshape(-1)
    choose = (flat_ids[:, None] == jnp.arange(EXPERTS, dtype=jnp.int32)[None, :]).astype(jnp.int32)
    earlier = jnp.cumsum(choose, axis=0) - choose
    slot_of = flat_ids * CAP + jnp.sum(earlier * choose, axis=1)
    picked = jnp.arange(slot_rows, dtype=jnp.int32)[:, None] == slot_of[None, :]
    picked_tok = jnp.any(picked.reshape(slot_rows, tok_count, choose_count), axis=2).astype(BF16)
    slot_prob = jnp.sum(jnp.where(picked, gate_probs.reshape(-1)[None, :], 0.0), axis=1)
    local_x = jnp.dot(picked_tok, tokens, preferred_element_type=F32).astype(BF16)
    local_dy = jnp.dot(picked_tok, cotangent, preferred_element_type=F32)
    local_scaled = (slot_prob[:, None] * local_dy).astype(BF16)
    rows_x = swap(widen(local_x, slices, expert_count)).reshape(-1, width)
    rows_s = swap(widen(local_scaled, slices, expert_count)).reshape(-1, width)
    both = jnp.dot(rows_x, gate_up[0], preferred_element_type=F32)
    gate, up = both[:, :half], both[:, half:]
    sigmoid = jax.nn.sigmoid(gate)
    activated = gate * sigmoid
    hidden = (activated * up).astype(BF16)
    grad_hidden = lax.dot_general(
        rows_s, down[0], (((1,), (1,)), ((), ())), preferred_element_type=F32
    )
    inner = jnp.sum(hidden.astype(F32) * grad_hidden, axis=1)
    grad_gate = (grad_hidden * up * sigmoid * (1.0 + gate * (1.0 - sigmoid))).astype(BF16)
    grad_up = (grad_hidden * activated).astype(BF16)
    grad_both = jnp.concatenate([grad_gate, grad_up], axis=1)
    over_rows = (((0,), (0,)), ((), ()))
    grad_gu = lax.dot_general(rows_x, grad_both, over_rows, preferred_element_type=F32)
    grad_down = lax.dot_general(hidden, rows_s, over_rows, preferred_element_type=F32)
    returned = swap(inner.reshape(expert_count, CAP))
    per_slot = jnp.sum(returned.reshape(EXPERTS, slices, CAP), axis=1).reshape(slot_rows)
    grad_probs = jnp.sum(jnp.where(picked, per_slot[:, None], 0.0), axis=0)
    grad_probs = grad_probs.reshape(tok_count, choose_count) / gate_probs
    reduced_gu = lax.psum_scatter(grad_gu.astype(BF16), "dp", scatter_dimension=0, tiled=True)
    reduced_down = lax.psum_scatter(grad_down.astype(BF16), "dp", scatter_dimension=1, tiled=True)
    return (grad_probs, reduced_gu[None], reduced_down[None])


def solution(mesh):
    whole_experts = mesh.shape["expert"] == EXPERTS and mesh.shape["dp"] == 4
    return jax.shard_map(
        plane_body if whole_experts else sliced_body,
        mesh=mesh,
        in_specs=(
            P(("dp", "expert"), None),
            P(("dp", "expert"), None),
            P(("dp", "expert"), None),
            P(("dp", "expert"), None),
            P("expert", None, None),
            P("expert", None, None),
        ),
        out_specs=(P(("dp", "expert"), None), P("expert", "dp", None), P("expert", None, "dp")),
        check_vma=False,
    )
```

```python
import functools

import jax
import jax.numpy as jnp
from jax import lax
from jax.experimental import pallas as pl
from jax.experimental.pallas import tpu as pltpu
from jax.sharding import PartitionSpec as P

EXPERTS = 8
CAP = 40
PAIR = 2 * CAP
LANES = 128
TILE = 256
MIB = 1024 * 1024
BF16 = jnp.bfloat16
F32 = jnp.float32


def dispatch_kernel(ids_ref, probs_ref, x_ref, dy_ref, *outs):
    row_refs, slot_ref = outs[:-1], outs[-1]
    me = lax.axis_index("expert")
    tok = x_ref.shape[0]
    width = x_ref.shape[1]
    numbers = lax.broadcasted_iota(jnp.int32, (EXPERTS, tok), 0)
    first = jnp.bitwise_xor(ids_ref[0:1, :], me) == numbers
    second = jnp.bitwise_xor(ids_ref[1:2, :], me) == numbers
    either = jnp.where(first | second, 1.0, 0.0)
    prob = jnp.where(first, probs_ref[0:1, :], 0.0) + jnp.where(second, probs_ref[1:2, :], 0.0)
    before = jnp.where(
        lax.broadcasted_iota(jnp.int32, (tok, tok), 0)
        < lax.broadcasted_iota(jnp.int32, (tok, tok), 1),
        1.0,
        0.0,
    )
    position = jnp.dot(either.astype(BF16), before.astype(BF16), preferred_element_type=F32)
    slot = position.astype(jnp.int32) + numbers * CAP
    slot_ref[0:1, :] = jnp.sum(jnp.where(first, slot, 0), axis=0, keepdims=True)
    slot_ref[1:2, :] = jnp.sum(jnp.where(second, slot, 0), axis=0, keepdims=True)
    target = jnp.where(either > 0.5, position, -1.0)
    places = lax.broadcasted_iota(jnp.int32, (CAP, tok), 0).astype(F32)
    picks = [
        jnp.where(places == target[e : e + 1, :], 1.0, 0.0) for e in range(EXPERTS)
    ]
    row_prob = jnp.concatenate(
        [jnp.sum(picks[e] * prob[e : e + 1, :], axis=1, keepdims=True) for e in range(EXPERTS)],
        axis=0,
    )
    pick = jnp.concatenate(picks, axis=0).astype(BF16)
    step = 512
    for at in range(0, width, step):
        rows_x = jnp.dot(pick, x_ref[:, at : at + step], preferred_element_type=F32)
        rows_dy = jnp.dot(pick, dy_ref[:, at : at + step], preferred_element_type=F32)
        scaled = row_prob * rows_dy
        for pair, ref in enumerate(row_refs):
            part = slice(pair * PAIR, (pair + 1) * PAIR)
            ref[:, at : at + step] = rows_x[part].astype(BF16)
            ref[:, width + at : width + at + step] = scaled[part].astype(BF16)


def dispatch_rows(ids, probs, tokens, cotangent):
    tok, width = tokens.shape
    return pl.pallas_call(
        dispatch_kernel,
        out_shape=[jax.ShapeDtypeStruct((PAIR, 2 * width), BF16)] * (EXPERTS // 2)
        + [jax.ShapeDtypeStruct((2, tok), jnp.int32)],
        compiler_params=pltpu.CompilerParams(vmem_limit_bytes=16 * MIB),
        cost_estimate=pl.CostEstimate(
            flops=4 * EXPERTS * CAP * tok * width, bytes_accessed=4_000_000, transcendentals=0
        ),
        name="dispatch_rows",
    )(ids, probs, tokens, cotangent)


def split_rows(count, top, half):
    blocks = 3 * half // TILE
    low = count - top
    from_x, from_y = (blocks + 4) * top, (blocks + 4) * low
    sizes = (from_x + blocks * low + 4 * count, from_y + blocks * top + 4 * count)
    return blocks, low, from_x, from_y, sizes


def expert_kernel(pairs, top, relays, *refs):
    row_refs, (gate_ref, up_ref, down_ref), rest = (
        refs[: 2 * pairs],
        refs[2 * pairs : 2 * pairs + 3],
        refs[2 * pairs + 3 :],
    )
    relay_refs, rest = rest[: len(relays)], rest[len(relays) :]
    own_ref, to_x, to_y, *inner_refs, x_rows, s_rows, s_turned, total = rest
    count = pairs * PAIR
    width = gate_ref.shape[0]
    steps = pl.num_programs(0)
    half = TILE * 3
    quarter = width // 4
    blocks, low, from_x, from_y, sizes = split_rows(count, top, half)
    step = pl.program_id(0)
    group = lax.axis_index("dp")

    @pl.when(step == 0)
    def _():
        for ref, relay, size, at in zip((to_x, to_y), relay_refs, relays, sizes):
            ref[at : at + size] = relay[:size]
        for rows, start in ((x_rows, 0), (s_rows, width)):
            rows[...] = jnp.concatenate(
                [ref[:CAP, start : start + width].astype(F32) for ref in row_refs],
                axis=0,
            ).astype(BF16)
        for q in range(4):
            rows = (x_rows, s_rows)[q // 2]

            def cut(mask):
                at = jnp.bitwise_xor(group, mask) * quarter + q % 2 * TILE
                return rows[:, pl.ds(pl.multiple_of(at, TILE), TILE)]

            at = blocks + q
            own_ref[at * count : (at + 1) * count] = cut(0)
            far = cut(3)
            to_x[at * top : (at + 1) * top] = far[:top]
            to_y[at * low : (at + 1) * low] = far[top:]
            start = from_x + blocks * low + q * count
            to_x[start : start + count] = cut(1)
            start = from_y + blocks * top + q * count
            to_y[start : start + count] = cut(2)
        s_turned[...] = s_rows[...].T
        total[...] = jnp.zeros_like(total)

    x = x_rows[...]
    gate = jnp.dot(x, gate_ref[...], preferred_element_type=F32)
    up = jnp.dot(x, up_ref[...], preferred_element_type=F32)
    grad_hidden = jnp.dot(down_ref[...], s_turned[...], preferred_element_type=F32).T
    sigmoid = 1.0 / (1.0 + jnp.exp(-gate))
    activated = gate * sigmoid
    hidden = (activated * up).astype(BF16)
    grad_gate = (grad_hidden * up * sigmoid * (1.0 + gate * (1.0 - sigmoid))).astype(BF16)
    grad_up = (grad_hidden * activated).astype(BF16)
    total[...] += jnp.sum(hidden.astype(F32) * grad_hidden, axis=1, keepdims=True)
    for part, values in enumerate((grad_gate, grad_up, hidden)):
        block = part * steps + step

        def rows_at(start, count):
            return pl.ds(pl.multiple_of(start + block * count, 16), count)

        own_ref[rows_at(0, count)] = values
        to_x[rows_at(0, top)] = values[:top]
        to_x[rows_at(from_x, low)] = values[top:]
        to_y[rows_at(0, low)] = values[top:]
        to_y[rows_at(from_y, top)] = values[:top]

    @pl.when(step == steps - 1)
    def _():
        for pair, ref in enumerate(inner_refs):
            part = total[pair * PAIR : (pair + 1) * PAIR]
            ref[...] = jnp.broadcast_to(part, ref.shape)


def expert_rows(rows, weight_gu, weight_down, top, relay=(), relays=()):
    pairs = len(rows) // 2
    count = pairs * PAIR
    width, both = weight_gu.shape
    half = both // 2
    steps = half // TILE
    blocks, _, _, _, sizes = split_rows(count, top, half)
    sizes = [(blocks + 4) * count] + [
        size + extra for size, extra in zip(sizes, relays or (0, 0))
    ]
    shapes = [(size, TILE) for size in sizes]

    def whole(shape):
        return pl.BlockSpec(shape, lambda h: (0, 0))

    return pl.pallas_call(
        functools.partial(expert_kernel, pairs, top, tuple(relays)),
        grid=(steps,),
        in_specs=[
            *[whole(part.shape) for part in rows],
            pl.BlockSpec((width, TILE), lambda h: (0, h)),
            pl.BlockSpec((width, TILE), lambda h: (0, h + steps)),
            pl.BlockSpec((TILE, width), lambda h: (h, 0)),
            *[whole(part.shape) for part in relay],
        ],
        out_specs=[whole(shape) for shape in shapes] + [whole((PAIR, LANES))] * pairs,
        out_shape=[jax.ShapeDtypeStruct(shape, BF16) for shape in shapes]
        + [jax.ShapeDtypeStruct((PAIR, LANES), F32)] * pairs,
        scratch_shapes=[
            pltpu.VMEM((count, width), BF16),
            pltpu.VMEM((count, width), BF16),
            pltpu.VMEM((width, count), BF16),
            pltpu.VMEM((count, 1), F32),
        ],
        compiler_params=pltpu.CompilerParams(vmem_limit_bytes=20 * MIB),
        cost_estimate=pl.CostEstimate(flops=1_000, bytes_accessed=1_000, transcendentals=0),
        name="expert_rows",
    )(*rows, weight_gu, weight_gu, weight_down, *relay)


def gradient_kernel(chunks, half, adding, *refs):
    groups, refs = (
        [refs[5 * n : 5 * n + 5] for n in range(len(chunks))],
        refs[5 * len(chunks) :],
    )
    if adding:
        (acc_gu, acc_down), refs = refs[:2], refs[2:]
    out_gu, out_down, turned, s_rows = refs
    both = 2 * half // TILE

    def far_parts(block, top, low, at_top, at_low, far_top, far_low):
        return [
            far_top[at_top + block * top : at_top + (block + 1) * top],
            far_low[at_low + block * low : at_low + (block + 1) * low],
        ]

    def factor(block):
        parts = []
        for (count, top, at_top, at_low), group in zip(chunks, groups):
            own, got_x, got_y, *far = group
            _, low, from_x, from_y, _ = split_rows(count, top, half)
            parts += [
                own[block * count : (block + 1) * count],
                got_x[block * top : (block + 1) * top],
                got_x[from_x + block * low : from_x + (block + 1) * low],
                got_y[from_y + block * top : from_y + (block + 1) * top],
                got_y[block * low : (block + 1) * low],
            ] + far_parts(block, top, low, at_top, at_low, *far)
        return jnp.concatenate(parts, axis=0)

    def piece(q):
        parts = []
        for (count, top, at_top, at_low), group in zip(chunks, groups):
            own, got_x, got_y, *far = group
            blocks, low, from_x, from_y, _ = split_rows(count, top, half)
            block = blocks + q
            at_x = from_x + blocks * low + q * count
            at_y = from_y + blocks * top + q * count
            parts += [
                own[block * count : (block + 1) * count],
                got_x[at_x : at_x + count],
                got_y[at_y : at_y + count],
            ] + far_parts(block, top, low, at_top, at_low, *far)
        return jnp.concatenate(parts, axis=0)

    for q in range(2):
        turned[q * TILE : (q + 1) * TILE, :] = piece(q).T
        s_rows[:, q * TILE : (q + 1) * TILE] = piece(2 + q)
    for block in range(both):
        at = slice(block * TILE, (block + 1) * TILE)
        grad = jnp.dot(turned[...], factor(block), preferred_element_type=F32)
        if adding:
            grad = grad + acc_gu[:, at]
        out_gu[:, at] = grad.astype(out_gu.dtype)
    for block in range(half // TILE):
        at = slice(block * TILE, (block + 1) * TILE)
        grad = jnp.dot(factor(both + block).T, s_rows[...], preferred_element_type=F32)
        if adding:
            grad = grad + acc_down[at, :]
        out_down[at, :] = grad.astype(out_down.dtype)


def gradients(chunks, pieces, half, quarter, sums=(), final=False):
    kept = BF16 if final else F32
    rows = 4 * sum(chunk[0] for chunk in chunks)
    vmem = pl.BlockSpec(memory_space=pltpu.VMEM)
    return pl.pallas_call(
        functools.partial(gradient_kernel, chunks, half, len(sums)),
        in_specs=[vmem] * (len(pieces) + len(sums)),
        out_specs=[vmem] * 2,
        out_shape=[
            jax.ShapeDtypeStruct((quarter, 2 * half), kept),
            jax.ShapeDtypeStruct((half, quarter), kept),
        ],
        scratch_shapes=[pltpu.VMEM((quarter, rows), BF16), pltpu.VMEM((rows, quarter), BF16)],
        compiler_params=pltpu.CompilerParams(vmem_limit_bytes=20 * MIB),
        cost_estimate=pl.CostEstimate(flops=1_000, bytes_accessed=1_000, transcendentals=0),
        name="gradients",
    )(*pieces, *sums)


def prob_kernel(own_0, own_1, own_2, own_3, other_ref, slot_ref, prob_ref, out_ref):
    owns = (own_0, own_1, own_2, own_3)
    tok = slot_ref.shape[1]
    places = lax.broadcasted_iota(jnp.int32, (CAP, tok), 0)
    for choice in range(2):
        slot = slot_ref[choice : choice + 1, :]
        grad = jnp.zeros((CAP, tok), F32)
        for e in range(EXPERTS):
            chunk = e // 2
            if e % 2 == 0:
                values = owns[chunk][:CAP, :]
            else:
                values = other_ref[chunk * CAP : (chunk + 1) * CAP, :]
            grad += jnp.where(places + e * CAP == slot, values, 0.0)
        grad = jnp.sum(grad, axis=0, keepdims=True)
        out_ref[choice : choice + 1, :] = grad / prob_ref[choice : choice + 1, :]


def prob_gradients(owns, other, slots, probs):
    return pl.pallas_call(
        prob_kernel,
        out_shape=jax.ShapeDtypeStruct(probs.shape, F32),
        compiler_params=pltpu.CompilerParams(vmem_limit_bytes=4 * MIB),
        cost_estimate=pl.CostEstimate(flops=1_000, bytes_accessed=1_000, transcendentals=0),
        name="prob_gradients",
    )(*owns, other, slots, probs)


def exchange(values, axis, mask):
    size = lax.axis_size(axis)
    return lax.ppermute(values, axis, [(n, n ^ mask) for n in range(size)])


def swap(values):
    return lax.all_to_all(values, "expert", split_axis=0, concat_axis=0, tiled=True)


def after(values, *others):
    return lax.optimization_barrier((values,) + others)[0]


def plane_body(tokens, cotangent, gate_probs, expert_ids, gate_up, down):
    half = gate_up.shape[2] // 2
    quarter = tokens.shape[1] // 4
    ids, probs = expert_ids.T, gate_probs.T
    *local, slots = dispatch_rows(ids, probs, tokens, cotangent)
    weights = (gate_up[0], down[0])
    _, _, cut_x0, cut_y0, _ = split_rows(PAIR, 48, half)
    _, _, cut_x1, cut_y1, _ = split_rows(2 * PAIR, PAIR, half)
    _, _, cut_x2, cut_y2, sizes = split_rows(PAIR, 32, half)

    def other_core(rows):
        return exchange(rows, "expert", 1)

    def to_plane(to_x, to_y):
        return exchange(to_x, "dp", 1), exchange(to_y, "dp", 2)

    rows_1 = exchange(local[1], "expert", 2)
    rows_3 = exchange(local[3], "expert", 6)
    own_0, to_x, to_y, inner_0 = expert_rows(
        (local[0], other_core(local[0][CAP:])), *weights, 48
    )
    got_x0, got_y0 = to_plane(to_x, to_y)
    rows_2 = exchange(after(local[2], inner_0), "expert", 4)
    rows_1, rows_3 = after((rows_1, rows_3), inner_0)
    own_1, to_x, to_y, inner_1, inner_3 = expert_rows(
        (rows_1, other_core(rows_1[CAP:]), rows_3, other_core(rows_3[CAP:])), *weights, PAIR
    )
    got_x1, got_y1 = to_plane(to_x, to_y)
    back_1, back_3 = after((inner_1, inner_3), got_x0, got_y0)
    inner_1, inner_3 = exchange(back_1, "expert", 2), exchange(back_3, "expert", 6)
    rows_2 = after(rows_2, inner_1, inner_3)
    own_2, to_x, to_y, inner_2 = expert_rows(
        (rows_2, other_core(rows_2[CAP:])),
        *weights,
        32,
        (got_y0, got_x0),
        (cut_y0, cut_x0),
    )
    got_x2, got_y2 = to_plane(to_x, to_y)
    got_x1, got_y1 = after((got_x1, got_y1), inner_2)
    low_1, top_1 = to_plane(got_y1[:cut_y1], got_x1[:cut_x1])
    returned = (inner_0, inner_1, exchange(inner_2, "expert", 4), inner_3)
    other = other_core(jnp.concatenate([part[CAP:] for part in returned], axis=0))
    grad_probs = prob_gradients(returned, other, slots, probs)
    got_x2, got_y2 = after((got_x2, got_y2), other)
    low_2, top_2 = to_plane(got_y2[:cut_y2], got_x2[:cut_x2])
    sums = gradients(
        ((PAIR, 48, sizes[1], sizes[0]),),
        (own_0, got_x0, got_y0, got_y2, got_x2),
        half,
        quarter,
    )
    grad_gu, grad_down = gradients(
        ((2 * PAIR, PAIR, 0, 0), (PAIR, 32, 0, 0)),
        (own_1, got_x1, got_y1, top_1, low_1, own_2, got_x2, got_y2, top_2, low_2),
        half,
        quarter,
        sums,
        True,
    )
    return (grad_probs.T, grad_gu[None], grad_down[None])


def widen(values, slices, expert_count):
    tail = values.shape[1:]
    spread = values.reshape((EXPERTS, 1, CAP) + tail)
    spread = jnp.broadcast_to(spread, (EXPERTS, slices, CAP) + tail)
    return spread.reshape((expert_count, CAP) + tail)


def sliced_body(tokens, cotangent, gate_probs, expert_ids, gate_up, down):
    expert_count = lax.axis_size("expert")
    slices = expert_count // EXPERTS
    tok_count, width = tokens.shape
    choose_count = expert_ids.shape[1]
    half = gate_up.shape[2] // 2
    slot_rows = EXPERTS * CAP
    flat_ids = expert_ids.reshape(-1)
    choose = (flat_ids[:, None] == jnp.arange(EXPERTS, dtype=jnp.int32)[None, :]).astype(jnp.int32)
    earlier = jnp.cumsum(choose, axis=0) - choose
    slot_of = flat_ids * CAP + jnp.sum(earlier * choose, axis=1)
    picked = jnp.arange(slot_rows, dtype=jnp.int32)[:, None] == slot_of[None, :]
    picked_tok = jnp.any(picked.reshape(slot_rows, tok_count, choose_count), axis=2).astype(BF16)
    slot_prob = jnp.sum(jnp.where(picked, gate_probs.reshape(-1)[None, :], 0.0), axis=1)
    local_x = jnp.dot(picked_tok, tokens, preferred_element_type=F32).astype(BF16)
    local_dy = jnp.dot(picked_tok, cotangent, preferred_element_type=F32)
    local_scaled = (slot_prob[:, None] * local_dy).astype(BF16)
    rows_x = swap(widen(local_x, slices, expert_count)).reshape(-1, width)
    rows_s = swap(widen(local_scaled, slices, expert_count)).reshape(-1, width)
    both = jnp.dot(rows_x, gate_up[0], preferred_element_type=F32)
    gate, up = both[:, :half], both[:, half:]
    sigmoid = jax.nn.sigmoid(gate)
    activated = gate * sigmoid
    hidden = (activated * up).astype(BF16)
    grad_hidden = lax.dot_general(
        rows_s, down[0], (((1,), (1,)), ((), ())), preferred_element_type=F32
    )
    inner = jnp.sum(hidden.astype(F32) * grad_hidden, axis=1)
    grad_gate = (grad_hidden * up * sigmoid * (1.0 + gate * (1.0 - sigmoid))).astype(BF16)
    grad_up = (grad_hidden * activated).astype(BF16)
    grad_both = jnp.concatenate([grad_gate, grad_up], axis=1)
    over_rows = (((0,), (0,)), ((), ()))
    grad_gu = lax.dot_general(rows_x, grad_both, over_rows, preferred_element_type=F32)
    grad_down = lax.dot_general(hidden, rows_s, over_rows, preferred_element_type=F32)
    returned = swap(inner.reshape(expert_count, CAP))
    per_slot = jnp.sum(returned.reshape(EXPERTS, slices, CAP), axis=1).reshape(slot_rows)
    grad_probs = jnp.sum(jnp.where(picked, per_slot[:, None], 0.0), axis=0)
    grad_probs = grad_probs.reshape(tok_count, choose_count) / gate_probs
    reduced_gu = lax.psum_scatter(grad_gu.astype(BF16), "dp", scatter_dimension=0, tiled=True)
    reduced_down = lax.psum_scatter(grad_down.astype(BF16), "dp", scatter_dimension=1, tiled=True)
    return (grad_probs, reduced_gu[None], reduced_down[None])


def solution(mesh):
    whole_experts = mesh.shape["expert"] == EXPERTS and mesh.shape["dp"] == 4
    return jax.shard_map(
        plane_body if whole_experts else sliced_body,
        mesh=mesh,
        in_specs=(
            P(("dp", "expert"), None),
            P(("dp", "expert"), None),
            P(("dp", "expert"), None),
            P(("dp", "expert"), None),
            P("expert", None, None),
            P("expert", None, None),
        ),
        out_specs=(P(("dp", "expert"), None), P("expert", "dp", None), P("expert", None, "dp")),
        check_vma=False,
    )
```

```python
import functools

import jax
import jax.numpy as jnp
from jax import lax
from jax.experimental import pallas as pl
from jax.experimental.pallas import tpu as pltpu
from jax.sharding import PartitionSpec as P

EXPERTS = 8
CAP = 40
PAIR = 2 * CAP
LANES = 128
TILE = 256
MIB = 1024 * 1024
BF16 = jnp.bfloat16
F32 = jnp.float32


def dispatch_kernel(ids_ref, probs_ref, x_ref, dy_ref, *outs):
    row_refs, slot_ref = outs[:-1], outs[-1]
    me = lax.axis_index("expert")
    tok = x_ref.shape[0]
    width = x_ref.shape[1]
    numbers = lax.broadcasted_iota(jnp.int32, (EXPERTS, tok), 0)
    first = jnp.bitwise_xor(ids_ref[0:1, :], me) == numbers
    second = jnp.bitwise_xor(ids_ref[1:2, :], me) == numbers
    either = jnp.where(first | second, 1.0, 0.0)
    prob = jnp.where(first, probs_ref[0:1, :], 0.0) + jnp.where(second, probs_ref[1:2, :], 0.0)
    before = jnp.where(
        lax.broadcasted_iota(jnp.int32, (tok, tok), 0)
        < lax.broadcasted_iota(jnp.int32, (tok, tok), 1),
        1.0,
        0.0,
    )
    position = jnp.dot(either.astype(BF16), before.astype(BF16), preferred_element_type=F32)
    slot = position.astype(jnp.int32) + numbers * CAP
    slot_ref[0:1, :] = jnp.sum(jnp.where(first, slot, 0), axis=0, keepdims=True)
    slot_ref[1:2, :] = jnp.sum(jnp.where(second, slot, 0), axis=0, keepdims=True)
    target = jnp.where(either > 0.5, position, -1.0)
    places = lax.broadcasted_iota(jnp.int32, (CAP, tok), 0).astype(F32)
    picks = [
        jnp.where(places == target[e : e + 1, :], 1.0, 0.0) for e in range(EXPERTS)
    ]
    row_prob = jnp.concatenate(
        [jnp.sum(picks[e] * prob[e : e + 1, :], axis=1, keepdims=True) for e in range(EXPERTS)],
        axis=0,
    )
    pick = jnp.concatenate(picks, axis=0).astype(BF16)
    step = 512
    for at in range(0, width, step):
        rows_x = jnp.dot(pick, x_ref[:, at : at + step], preferred_element_type=F32)
        rows_dy = jnp.dot(pick, dy_ref[:, at : at + step], preferred_element_type=F32)
        scaled = row_prob * rows_dy
        for pair, ref in enumerate(row_refs):
            part = slice(pair * PAIR, (pair + 1) * PAIR)
            ref[:, at : at + step] = rows_x[part].astype(BF16)
            ref[:, width + at : width + at + step] = scaled[part].astype(BF16)


def dispatch_rows(ids, probs, tokens, cotangent):
    tok, width = tokens.shape
    return pl.pallas_call(
        dispatch_kernel,
        out_shape=[jax.ShapeDtypeStruct((PAIR, 2 * width), BF16)] * (EXPERTS // 2)
        + [jax.ShapeDtypeStruct((2, tok), jnp.int32)],
        compiler_params=pltpu.CompilerParams(vmem_limit_bytes=16 * MIB),
        cost_estimate=pl.CostEstimate(
            flops=4 * EXPERTS * CAP * tok * width, bytes_accessed=4_000_000, transcendentals=0
        ),
        name="dispatch_rows",
    )(ids, probs, tokens, cotangent)


def split_rows(count, top, half):
    blocks = 3 * half // TILE
    low = count - top
    from_x, from_y = (blocks + 4) * top, (blocks + 4) * low
    sizes = (from_x + blocks * low + 4 * count, from_y + blocks * top + 4 * count)
    return blocks, low, from_x, from_y, sizes


def expert_kernel(pairs, top, relays, *refs):
    row_refs, (gate_ref, up_ref, down_ref), rest = (
        refs[: 2 * pairs],
        refs[2 * pairs : 2 * pairs + 3],
        refs[2 * pairs + 3 :],
    )
    relay_refs, rest = rest[: len(relays)], rest[len(relays) :]
    own_ref, to_x, to_y, *inner_refs, x_rows, s_rows, s_turned, total = rest
    count = pairs * PAIR
    width = gate_ref.shape[0]
    steps = pl.num_programs(0)
    half = TILE * 3
    quarter = width // 4
    blocks, low, from_x, from_y, sizes = split_rows(count, top, half)
    step = pl.program_id(0)
    group = lax.axis_index("dp")

    @pl.when(step == 0)
    def _():
        for ref, relay, size, at in zip((to_x, to_y), relay_refs, relays, sizes):
            ref[at : at + size] = relay[:size]
        for rows, start in ((x_rows, 0), (s_rows, width)):
            rows[...] = jnp.concatenate(
                [ref[:CAP, start : start + width].astype(F32) for ref in row_refs],
                axis=0,
            ).astype(BF16)
        for q in range(4):
            rows = (x_rows, s_rows)[q // 2]

            def cut(mask):
                at = jnp.bitwise_xor(group, mask) * quarter + q % 2 * TILE
                return rows[:, pl.ds(pl.multiple_of(at, TILE), TILE)]

            at = blocks + q
            own_ref[at * count : (at + 1) * count] = cut(0)
            far = cut(3)
            to_x[at * top : (at + 1) * top] = far[:top]
            to_y[at * low : (at + 1) * low] = far[top:]
            start = from_x + blocks * low + q * count
            to_x[start : start + count] = cut(1)
            start = from_y + blocks * top + q * count
            to_y[start : start + count] = cut(2)
        s_turned[...] = s_rows[...].T
        total[...] = jnp.zeros_like(total)

    x = x_rows[...]
    gate = jnp.dot(x, gate_ref[...], preferred_element_type=F32)
    up = jnp.dot(x, up_ref[...], preferred_element_type=F32)
    grad_hidden = jnp.dot(down_ref[...], s_turned[...], preferred_element_type=F32).T
    sigmoid = 1.0 / (1.0 + jnp.exp(-gate))
    activated = gate * sigmoid
    hidden = (activated * up).astype(BF16)
    grad_gate = (grad_hidden * up * sigmoid * (1.0 + gate * (1.0 - sigmoid))).astype(BF16)
    grad_up = (grad_hidden * activated).astype(BF16)
    total[...] += jnp.sum(hidden.astype(F32) * grad_hidden, axis=1, keepdims=True)
    for part, values in enumerate((grad_gate, grad_up, hidden)):
        block = part * steps + step

        def rows_at(start, count):
            return pl.ds(pl.multiple_of(start + block * count, 16), count)

        own_ref[rows_at(0, count)] = values
        to_x[rows_at(0, top)] = values[:top]
        to_x[rows_at(from_x, low)] = values[top:]
        to_y[rows_at(0, low)] = values[top:]
        to_y[rows_at(from_y, top)] = values[:top]

    @pl.when(step == steps - 1)
    def _():
        for pair, ref in enumerate(inner_refs):
            part = total[pair * PAIR : (pair + 1) * PAIR]
            ref[...] = jnp.broadcast_to(part, ref.shape)


def expert_rows(rows, weight_gu, weight_down, top, relay=(), relays=()):
    pairs = len(rows) // 2
    count = pairs * PAIR
    width, both = weight_gu.shape
    half = both // 2
    steps = half // TILE
    blocks, _, _, _, sizes = split_rows(count, top, half)
    sizes = [(blocks + 4) * count] + [
        size + extra for size, extra in zip(sizes, relays or (0, 0))
    ]
    shapes = [(size, TILE) for size in sizes]

    def whole(shape):
        return pl.BlockSpec(shape, lambda h: (0, 0))

    return pl.pallas_call(
        functools.partial(expert_kernel, pairs, top, tuple(relays)),
        grid=(steps,),
        in_specs=[
            *[whole(part.shape) for part in rows],
            pl.BlockSpec((width, TILE), lambda h: (0, h)),
            pl.BlockSpec((width, TILE), lambda h: (0, h + steps)),
            pl.BlockSpec((TILE, width), lambda h: (h, 0)),
            *[whole(part.shape) for part in relay],
        ],
        out_specs=[whole(shape) for shape in shapes] + [whole((PAIR, LANES))] * pairs,
        out_shape=[jax.ShapeDtypeStruct(shape, BF16) for shape in shapes]
        + [jax.ShapeDtypeStruct((PAIR, LANES), F32)] * pairs,
        scratch_shapes=[
            pltpu.VMEM((count, width), BF16),
            pltpu.VMEM((count, width), BF16),
            pltpu.VMEM((width, count), BF16),
            pltpu.VMEM((count, 1), F32),
        ],
        compiler_params=pltpu.CompilerParams(vmem_limit_bytes=20 * MIB),
        cost_estimate=pl.CostEstimate(flops=1_000, bytes_accessed=1_000, transcendentals=0),
        name="expert_rows",
    )(*rows, weight_gu, weight_gu, weight_down, *relay)


def gradient_kernel(chunks, half, adding, *refs):
    groups, refs = (
        [refs[5 * n : 5 * n + 5] for n in range(len(chunks))],
        refs[5 * len(chunks) :],
    )
    if adding:
        (acc_gu, acc_down), refs = refs[:2], refs[2:]
    out_gu, out_down, turned, s_rows = refs
    both = 2 * half // TILE

    def far_parts(block, top, low, at_top, at_low, far_top, far_low):
        return [
            far_top[at_top + block * top : at_top + (block + 1) * top],
            far_low[at_low + block * low : at_low + (block + 1) * low],
        ]

    def factor(block):
        parts = []
        for (count, top, at_top, at_low), group in zip(chunks, groups):
            own, got_x, got_y, *far = group
            _, low, from_x, from_y, _ = split_rows(count, top, half)
            parts += [
                own[block * count : (block + 1) * count],
                got_x[block * top : (block + 1) * top],
                got_x[from_x + block * low : from_x + (block + 1) * low],
                got_y[from_y + block * top : from_y + (block + 1) * top],
                got_y[block * low : (block + 1) * low],
            ] + far_parts(block, top, low, at_top, at_low, *far)
        return jnp.concatenate(parts, axis=0)

    def piece(q):
        parts = []
        for (count, top, at_top, at_low), group in zip(chunks, groups):
            own, got_x, got_y, *far = group
            blocks, low, from_x, from_y, _ = split_rows(count, top, half)
            block = blocks + q
            at_x = from_x + blocks * low + q * count
            at_y = from_y + blocks * top + q * count
            parts += [
                own[block * count : (block + 1) * count],
                got_x[at_x : at_x + count],
                got_y[at_y : at_y + count],
            ] + far_parts(block, top, low, at_top, at_low, *far)
        return jnp.concatenate(parts, axis=0)

    for q in range(2):
        turned[q * TILE : (q + 1) * TILE, :] = piece(q).T
        s_rows[:, q * TILE : (q + 1) * TILE] = piece(2 + q)
    for block in range(both):
        at = slice(block * TILE, (block + 1) * TILE)
        grad = jnp.dot(turned[...], factor(block), preferred_element_type=F32)
        if adding:
            grad = grad + acc_gu[:, at]
        out_gu[:, at] = grad.astype(out_gu.dtype)
    for block in range(half // TILE):
        at = slice(block * TILE, (block + 1) * TILE)
        grad = jnp.dot(factor(both + block).T, s_rows[...], preferred_element_type=F32)
        if adding:
            grad = grad + acc_down[at, :]
        out_down[at, :] = grad.astype(out_down.dtype)


def gradients(chunks, pieces, half, quarter, sums=(), final=False):
    kept = BF16 if final else F32
    rows = 4 * sum(chunk[0] for chunk in chunks)
    vmem = pl.BlockSpec(memory_space=pltpu.VMEM)
    return pl.pallas_call(
        functools.partial(gradient_kernel, chunks, half, len(sums)),
        in_specs=[vmem] * (len(pieces) + len(sums)),
        out_specs=[vmem] * 2,
        out_shape=[
            jax.ShapeDtypeStruct((quarter, 2 * half), kept),
            jax.ShapeDtypeStruct((half, quarter), kept),
        ],
        scratch_shapes=[pltpu.VMEM((quarter, rows), BF16), pltpu.VMEM((rows, quarter), BF16)],
        compiler_params=pltpu.CompilerParams(vmem_limit_bytes=20 * MIB),
        cost_estimate=pl.CostEstimate(flops=1_000, bytes_accessed=1_000, transcendentals=0),
        name="gradients",
    )(*pieces, *sums)


def prob_kernel(own_0, own_1, own_2, own_3, other_ref, slot_ref, prob_ref, out_ref):
    owns = (own_0, own_1, own_2, own_3)
    tok = slot_ref.shape[1]
    places = lax.broadcasted_iota(jnp.int32, (CAP, tok), 0)
    for choice in range(2):
        slot = slot_ref[choice : choice + 1, :]
        grad = jnp.zeros((CAP, tok), F32)
        for e in range(EXPERTS):
            chunk = e // 2
            if e % 2 == 0:
                values = owns[chunk][:CAP, :]
            else:
                values = other_ref[chunk * CAP : (chunk + 1) * CAP, :]
            grad += jnp.where(places + e * CAP == slot, values, 0.0)
        grad = jnp.sum(grad, axis=0, keepdims=True)
        out_ref[choice : choice + 1, :] = grad / prob_ref[choice : choice + 1, :]


def prob_gradients(owns, other, slots, probs):
    return pl.pallas_call(
        prob_kernel,
        out_shape=jax.ShapeDtypeStruct(probs.shape, F32),
        compiler_params=pltpu.CompilerParams(vmem_limit_bytes=4 * MIB),
        cost_estimate=pl.CostEstimate(flops=1_000, bytes_accessed=1_000, transcendentals=0),
        name="prob_gradients",
    )(*owns, other, slots, probs)


def exchange(values, axis, mask):
    size = lax.axis_size(axis)
    return lax.ppermute(values, axis, [(n, n ^ mask) for n in range(size)])


def swap(values):
    return lax.all_to_all(values, "expert", split_axis=0, concat_axis=0, tiled=True)


def after(values, *others):
    return lax.optimization_barrier((values,) + others)[0]


def plane_body(tokens, cotangent, gate_probs, expert_ids, gate_up, down):
    half = gate_up.shape[2] // 2
    quarter = tokens.shape[1] // 4
    ids, probs = expert_ids.T, gate_probs.T
    *local, slots = dispatch_rows(ids, probs, tokens, cotangent)
    weights = (gate_up[0], down[0])
    _, _, cut_x0, cut_y0, _ = split_rows(PAIR, 48, half)
    _, _, cut_x1, cut_y1, _ = split_rows(2 * PAIR, PAIR, half)
    _, _, cut_x2, cut_y2, _ = split_rows(PAIR, 32, half)

    def other_core(rows):
        return exchange(rows, "expert", 1)

    def to_plane(to_x, to_y):
        return exchange(to_x, "dp", 1), exchange(to_y, "dp", 2)

    rows_1 = exchange(local[1], "expert", 2)
    rows_2 = exchange(local[2], "expert", 4)
    own_0, to_x, to_y, inner_0 = expert_rows(
        (local[0], other_core(local[0][CAP:])), *weights, 48
    )
    got_x0, got_y0 = to_plane(to_x, to_y)
    low_0, top_0 = to_plane(got_y0[:cut_y0], got_x0[:cut_x0])
    rows_1, rows_2 = after((rows_1, rows_2), inner_0)
    other_1, other_2 = other_core(rows_1[CAP:]), other_core(rows_2[CAP:])
    rows_3 = exchange(after(local[3], rows_2), "expert", 6)
    own_1, to_x, to_y, inner_1, inner_2 = expert_rows(
        (rows_1, other_1, rows_2, other_2), *weights, PAIR
    )
    got_x1, got_y1 = to_plane(*after((to_x, to_y), low_0, top_0))
    sums = gradients(
        ((PAIR, 48, 0, 0),), (own_0, got_x0, got_y0, top_0, low_0), half, quarter
    )
    back_1, back_2 = after((inner_1, inner_2), *sums)
    inner_1, inner_2 = exchange(back_1, "expert", 2), exchange(back_2, "expert", 4)
    rows_3 = after(rows_3, inner_1, inner_2)
    own_2, to_x, to_y, inner_3 = expert_rows(
        (rows_3, other_core(rows_3[CAP:])), *weights, 32
    )
    got_x2, got_y2 = to_plane(to_x, to_y)
    got_x1, got_y1 = after((got_x1, got_y1), inner_3)
    low_1, top_1 = to_plane(got_y1[:cut_y1], got_x1[:cut_x1])
    returned = (inner_0, inner_1, inner_2, exchange(inner_3, "expert", 6))
    other = other_core(jnp.concatenate([part[CAP:] for part in returned], axis=0))
    grad_probs = prob_gradients(returned, other, slots, probs)
    got_x2, got_y2 = after((got_x2, got_y2), other)
    low_2, top_2 = to_plane(got_y2[:cut_y2], got_x2[:cut_x2])
    grad_gu, grad_down = gradients(
        ((2 * PAIR, PAIR, 0, 0), (PAIR, 32, 0, 0)),
        (own_1, got_x1, got_y1, top_1, low_1, own_2, got_x2, got_y2, top_2, low_2),
        half,
        quarter,
        sums,
        True,
    )
    return (grad_probs.T, grad_gu[None], grad_down[None])


def widen(values, slices, expert_count):
    tail = values.shape[1:]
    spread = values.reshape((EXPERTS, 1, CAP) + tail)
    spread = jnp.broadcast_to(spread, (EXPERTS, slices, CAP) + tail)
    return spread.reshape((expert_count, CAP) + tail)


def sliced_body(tokens, cotangent, gate_probs, expert_ids, gate_up, down):
    expert_count = lax.axis_size("expert")
    slices = expert_count // EXPERTS
    tok_count, width = tokens.shape
    choose_count = expert_ids.shape[1]
    half = gate_up.shape[2] // 2
    slot_rows = EXPERTS * CAP
    flat_ids = expert_ids.reshape(-1)
    choose = (flat_ids[:, None] == jnp.arange(EXPERTS, dtype=jnp.int32)[None, :]).astype(jnp.int32)
    earlier = jnp.cumsum(choose, axis=0) - choose
    slot_of = flat_ids * CAP + jnp.sum(earlier * choose, axis=1)
    picked = jnp.arange(slot_rows, dtype=jnp.int32)[:, None] == slot_of[None, :]
    picked_tok = jnp.any(picked.reshape(slot_rows, tok_count, choose_count), axis=2).astype(BF16)
    slot_prob = jnp.sum(jnp.where(picked, gate_probs.reshape(-1)[None, :], 0.0), axis=1)
    local_x = jnp.dot(picked_tok, tokens, preferred_element_type=F32).astype(BF16)
    local_dy = jnp.dot(picked_tok, cotangent, preferred_element_type=F32)
    local_scaled = (slot_prob[:, None] * local_dy).astype(BF16)
    rows_x = swap(widen(local_x, slices, expert_count)).reshape(-1, width)
    rows_s = swap(widen(local_scaled, slices, expert_count)).reshape(-1, width)
    both = jnp.dot(rows_x, gate_up[0], preferred_element_type=F32)
    gate, up = both[:, :half], both[:, half:]
    sigmoid = jax.nn.sigmoid(gate)
    activated = gate * sigmoid
    hidden = (activated * up).astype(BF16)
    grad_hidden = lax.dot_general(
        rows_s, down[0], (((1,), (1,)), ((), ())), preferred_element_type=F32
    )
    inner = jnp.sum(hidden.astype(F32) * grad_hidden, axis=1)
    grad_gate = (grad_hidden * up * sigmoid * (1.0 + gate * (1.0 - sigmoid))).astype(BF16)
    grad_up = (grad_hidden * activated).astype(BF16)
    grad_both = jnp.concatenate([grad_gate, grad_up], axis=1)
    over_rows = (((0,), (0,)), ((), ()))
    grad_gu = lax.dot_general(rows_x, grad_both, over_rows, preferred_element_type=F32)
    grad_down = lax.dot_general(hidden, rows_s, over_rows, preferred_element_type=F32)
    returned = swap(inner.reshape(expert_count, CAP))
    per_slot = jnp.sum(returned.reshape(EXPERTS, slices, CAP), axis=1).reshape(slot_rows)
    grad_probs = jnp.sum(jnp.where(picked, per_slot[:, None], 0.0), axis=0)
    grad_probs = grad_probs.reshape(tok_count, choose_count) / gate_probs
    reduced_gu = lax.psum_scatter(grad_gu.astype(BF16), "dp", scatter_dimension=0, tiled=True)
    reduced_down = lax.psum_scatter(grad_down.astype(BF16), "dp", scatter_dimension=1, tiled=True)
    return (grad_probs, reduced_gu[None], reduced_down[None])


def solution(mesh):
    whole_experts = mesh.shape["expert"] == EXPERTS and mesh.shape["dp"] == 4
    return jax.shard_map(
        plane_body if whole_experts else sliced_body,
        mesh=mesh,
        in_specs=(
            P(("dp", "expert"), None),
            P(("dp", "expert"), None),
            P(("dp", "expert"), None),
            P(("dp", "expert"), None),
            P("expert", None, None),
            P("expert", None, None),
        ),
        out_specs=(P(("dp", "expert"), None), P("expert", "dp", None), P("expert", None, "dp")),
        check_vma=False,
    )
```

```python
import functools

import jax
import jax.numpy as jnp
from jax import lax
from jax.experimental import pallas as pl
from jax.experimental.pallas import tpu as pltpu
from jax.sharding import PartitionSpec as P

EXPERTS = 8
CAP = 40
PAIR = 2 * CAP
LANES = 128
TILE = 256
MIB = 1024 * 1024
BF16 = jnp.bfloat16
F32 = jnp.float32


def dispatch_kernel(ids_ref, probs_ref, x_ref, dy_ref, *outs):
    row_refs, slot_ref = outs[:-1], outs[-1]
    me = lax.axis_index("expert")
    tok = x_ref.shape[0]
    width = x_ref.shape[1]
    numbers = lax.broadcasted_iota(jnp.int32, (EXPERTS, tok), 0)
    first = jnp.bitwise_xor(ids_ref[0:1, :], me) == numbers
    second = jnp.bitwise_xor(ids_ref[1:2, :], me) == numbers
    either = jnp.where(first | second, 1.0, 0.0)
    prob = jnp.where(first, probs_ref[0:1, :], 0.0) + jnp.where(second, probs_ref[1:2, :], 0.0)
    before = jnp.where(
        lax.broadcasted_iota(jnp.int32, (tok, tok), 0)
        < lax.broadcasted_iota(jnp.int32, (tok, tok), 1),
        1.0,
        0.0,
    )
    position = jnp.dot(either.astype(BF16), before.astype(BF16), preferred_element_type=F32)
    slot = position.astype(jnp.int32) + numbers * CAP
    slot_ref[0:1, :] = jnp.sum(jnp.where(first, slot, 0), axis=0, keepdims=True)
    slot_ref[1:2, :] = jnp.sum(jnp.where(second, slot, 0), axis=0, keepdims=True)
    target = jnp.where(either > 0.5, position, -1.0)
    places = lax.broadcasted_iota(jnp.int32, (CAP, tok), 0).astype(F32)
    picks = [
        jnp.where(places == target[e : e + 1, :], 1.0, 0.0) for e in range(EXPERTS)
    ]
    row_prob = jnp.concatenate(
        [jnp.sum(picks[e] * prob[e : e + 1, :], axis=1, keepdims=True) for e in range(EXPERTS)],
        axis=0,
    )
    pick = jnp.concatenate(picks, axis=0).astype(BF16)
    step = 512
    for at in range(0, width, step):
        rows_x = jnp.dot(pick, x_ref[:, at : at + step], preferred_element_type=F32)
        rows_dy = jnp.dot(pick, dy_ref[:, at : at + step], preferred_element_type=F32)
        scaled = row_prob * rows_dy
        for pair, ref in enumerate(row_refs):
            part = slice(pair * PAIR, (pair + 1) * PAIR)
            ref[:, at : at + step] = rows_x[part].astype(BF16)
            ref[:, width + at : width + at + step] = scaled[part].astype(BF16)


def dispatch_rows(ids, probs, tokens, cotangent):
    tok, width = tokens.shape
    return pl.pallas_call(
        dispatch_kernel,
        out_shape=[jax.ShapeDtypeStruct((PAIR, 2 * width), BF16)] * (EXPERTS // 2)
        + [jax.ShapeDtypeStruct((2, tok), jnp.int32)],
        compiler_params=pltpu.CompilerParams(vmem_limit_bytes=16 * MIB),
        cost_estimate=pl.CostEstimate(
            flops=4 * EXPERTS * CAP * tok * width, bytes_accessed=4_000_000, transcendentals=0
        ),
        name="dispatch_rows",
    )(ids, probs, tokens, cotangent)


def split_rows(count, top, half):
    blocks = 3 * half // TILE
    low = count - top
    from_x, from_y = (blocks + 4) * top, (blocks + 4) * low
    sizes = (from_x + blocks * low + 4 * count, from_y + blocks * top + 4 * count)
    return blocks, low, from_x, from_y, sizes


def expert_kernel(pairs, top, relays, *refs):
    row_refs, (gate_ref, up_ref, down_ref), rest = (
        refs[: 2 * pairs],
        refs[2 * pairs : 2 * pairs + 3],
        refs[2 * pairs + 3 :],
    )
    relay_refs, rest = rest[: len(relays)], rest[len(relays) :]
    own_ref, to_x, to_y, *inner_refs, x_rows, s_rows, s_turned, total = rest
    count = pairs * PAIR
    width = gate_ref.shape[0]
    steps = pl.num_programs(0)
    half = TILE * 3
    quarter = width // 4
    blocks, low, from_x, from_y, sizes = split_rows(count, top, half)
    step = pl.program_id(0)
    group = lax.axis_index("dp")

    @pl.when(step == 0)
    def _():
        for ref, relay, size, at in zip((to_x, to_y), relay_refs, relays, sizes):
            ref[at : at + size] = relay[:size]
        for rows, start in ((x_rows, 0), (s_rows, width)):
            rows[...] = jnp.concatenate(
                [ref[:CAP, start : start + width].astype(F32) for ref in row_refs],
                axis=0,
            ).astype(BF16)
        for q in range(4):
            rows = (x_rows, s_rows)[q // 2]

            def cut(mask):
                at = jnp.bitwise_xor(group, mask) * quarter + q % 2 * TILE
                return rows[:, pl.ds(pl.multiple_of(at, TILE), TILE)]

            at = blocks + q
            own_ref[at * count : (at + 1) * count] = cut(0)
            far = cut(3)
            to_x[at * top : (at + 1) * top] = far[:top]
            to_y[at * low : (at + 1) * low] = far[top:]
            start = from_x + blocks * low + q * count
            to_x[start : start + count] = cut(1)
            start = from_y + blocks * top + q * count
            to_y[start : start + count] = cut(2)
        s_turned[...] = s_rows[...].T
        total[...] = jnp.zeros_like(total)

    x = x_rows[...]
    gate = jnp.dot(x, gate_ref[...], preferred_element_type=F32)
    up = jnp.dot(x, up_ref[...], preferred_element_type=F32)
    grad_hidden = jnp.dot(down_ref[...], s_turned[...], preferred_element_type=F32).T
    sigmoid = 1.0 / (1.0 + jnp.exp(-gate))
    activated = gate * sigmoid
    hidden = (activated * up).astype(BF16)
    grad_gate = (grad_hidden * up * sigmoid * (1.0 + gate * (1.0 - sigmoid))).astype(BF16)
    grad_up = (grad_hidden * activated).astype(BF16)
    total[...] += jnp.sum(hidden.astype(F32) * grad_hidden, axis=1, keepdims=True)
    for part, values in enumerate((grad_gate, grad_up, hidden)):
        block = part * steps + step

        def rows_at(start, count):
            return pl.ds(pl.multiple_of(start + block * count, 16), count)

        own_ref[rows_at(0, count)] = values
        to_x[rows_at(0, top)] = values[:top]
        to_x[rows_at(from_x, low)] = values[top:]
        to_y[rows_at(0, low)] = values[top:]
        to_y[rows_at(from_y, top)] = values[:top]

    @pl.when(step == steps - 1)
    def _():
        for pair, ref in enumerate(inner_refs):
            part = total[pair * PAIR : (pair + 1) * PAIR]
            ref[...] = jnp.broadcast_to(part, ref.shape)


def expert_rows(rows, weight_gu, weight_down, top, relay=(), relays=()):
    pairs = len(rows) // 2
    count = pairs * PAIR
    width, both = weight_gu.shape
    half = both // 2
    steps = half // TILE
    blocks, _, _, _, sizes = split_rows(count, top, half)
    sizes = [(blocks + 4) * count] + [
        size + extra for size, extra in zip(sizes, relays or (0, 0))
    ]
    shapes = [(size, TILE) for size in sizes]

    def whole(shape):
        return pl.BlockSpec(shape, lambda h: (0, 0))

    return pl.pallas_call(
        functools.partial(expert_kernel, pairs, top, tuple(relays)),
        grid=(steps,),
        in_specs=[
            *[whole(part.shape) for part in rows],
            pl.BlockSpec((width, TILE), lambda h: (0, h)),
            pl.BlockSpec((width, TILE), lambda h: (0, h + steps)),
            pl.BlockSpec((TILE, width), lambda h: (h, 0)),
            *[whole(part.shape) for part in relay],
        ],
        out_specs=[whole(shape) for shape in shapes] + [whole((PAIR, LANES))] * pairs,
        out_shape=[jax.ShapeDtypeStruct(shape, BF16) for shape in shapes]
        + [jax.ShapeDtypeStruct((PAIR, LANES), F32)] * pairs,
        scratch_shapes=[
            pltpu.VMEM((count, width), BF16),
            pltpu.VMEM((count, width), BF16),
            pltpu.VMEM((width, count), BF16),
            pltpu.VMEM((count, 1), F32),
        ],
        compiler_params=pltpu.CompilerParams(vmem_limit_bytes=20 * MIB),
        cost_estimate=pl.CostEstimate(flops=1_000, bytes_accessed=1_000, transcendentals=0),
        name="expert_rows",
    )(*rows, weight_gu, weight_gu, weight_down, *relay)


def gradient_kernel(chunks, half, adding, *refs):
    groups, refs = (
        [refs[5 * n : 5 * n + 5] for n in range(len(chunks))],
        refs[5 * len(chunks) :],
    )
    if adding:
        (acc_gu, acc_down), refs = refs[:2], refs[2:]
    out_gu, out_down, turned, s_rows = refs
    both = 2 * half // TILE

    def far_parts(block, top, low, at_top, at_low, far_top, far_low):
        return [
            far_top[at_top + block * top : at_top + (block + 1) * top],
            far_low[at_low + block * low : at_low + (block + 1) * low],
        ]

    def factor(block):
        parts = []
        for (count, top, at_top, at_low), group in zip(chunks, groups):
            own, got_x, got_y, *far = group
            _, low, from_x, from_y, _ = split_rows(count, top, half)
            parts += [
                own[block * count : (block + 1) * count],
                got_x[block * top : (block + 1) * top],
                got_x[from_x + block * low : from_x + (block + 1) * low],
                got_y[from_y + block * top : from_y + (block + 1) * top],
                got_y[block * low : (block + 1) * low],
            ] + far_parts(block, top, low, at_top, at_low, *far)
        return jnp.concatenate(parts, axis=0)

    def piece(q):
        parts = []
        for (count, top, at_top, at_low), group in zip(chunks, groups):
            own, got_x, got_y, *far = group
            blocks, low, from_x, from_y, _ = split_rows(count, top, half)
            block = blocks + q
            at_x = from_x + blocks * low + q * count
            at_y = from_y + blocks * top + q * count
            parts += [
                own[block * count : (block + 1) * count],
                got_x[at_x : at_x + count],
                got_y[at_y : at_y + count],
            ] + far_parts(block, top, low, at_top, at_low, *far)
        return jnp.concatenate(parts, axis=0)

    for q in range(2):
        turned[q * TILE : (q + 1) * TILE, :] = piece(q).T
        s_rows[:, q * TILE : (q + 1) * TILE] = piece(2 + q)
    for block in range(both):
        at = slice(block * TILE, (block + 1) * TILE)
        grad = jnp.dot(turned[...], factor(block), preferred_element_type=F32)
        if adding:
            grad = grad + acc_gu[:, at]
        out_gu[:, at] = grad.astype(out_gu.dtype)
    for block in range(half // TILE):
        at = slice(block * TILE, (block + 1) * TILE)
        grad = jnp.dot(factor(both + block).T, s_rows[...], preferred_element_type=F32)
        if adding:
            grad = grad + acc_down[at, :]
        out_down[at, :] = grad.astype(out_down.dtype)


def gradients(chunks, pieces, half, quarter, sums=(), final=False):
    kept = BF16 if final else F32
    rows = 4 * sum(chunk[0] for chunk in chunks)
    vmem = pl.BlockSpec(memory_space=pltpu.VMEM)
    return pl.pallas_call(
        functools.partial(gradient_kernel, chunks, half, len(sums)),
        in_specs=[vmem] * (len(pieces) + len(sums)),
        out_specs=[vmem] * 2,
        out_shape=[
            jax.ShapeDtypeStruct((quarter, 2 * half), kept),
            jax.ShapeDtypeStruct((half, quarter), kept),
        ],
        scratch_shapes=[pltpu.VMEM((quarter, rows), BF16), pltpu.VMEM((rows, quarter), BF16)],
        compiler_params=pltpu.CompilerParams(vmem_limit_bytes=20 * MIB),
        cost_estimate=pl.CostEstimate(flops=1_000, bytes_accessed=1_000, transcendentals=0),
        name="gradients",
    )(*pieces, *sums)


def prob_kernel(own_0, own_1, own_2, own_3, other_ref, slot_ref, prob_ref, out_ref):
    owns = (own_0, own_1, own_2, own_3)
    tok = slot_ref.shape[1]
    places = lax.broadcasted_iota(jnp.int32, (CAP, tok), 0)
    for choice in range(2):
        slot = slot_ref[choice : choice + 1, :]
        grad = jnp.zeros((CAP, tok), F32)
        for e in range(EXPERTS):
            chunk = e // 2
            if e % 2 == 0:
                values = owns[chunk][:CAP, :]
            else:
                values = other_ref[chunk * CAP : (chunk + 1) * CAP, :]
            grad += jnp.where(places + e * CAP == slot, values, 0.0)
        grad = jnp.sum(grad, axis=0, keepdims=True)
        out_ref[choice : choice + 1, :] = grad / prob_ref[choice : choice + 1, :]


def prob_gradients(owns, other, slots, probs):
    return pl.pallas_call(
        prob_kernel,
        out_shape=jax.ShapeDtypeStruct(probs.shape, F32),
        compiler_params=pltpu.CompilerParams(vmem_limit_bytes=4 * MIB),
        cost_estimate=pl.CostEstimate(flops=1_000, bytes_accessed=1_000, transcendentals=0),
        name="prob_gradients",
    )(*owns, other, slots, probs)


def exchange(values, axis, mask):
    size = lax.axis_size(axis)
    return lax.ppermute(values, axis, [(n, n ^ mask) for n in range(size)])


def swap(values):
    return lax.all_to_all(values, "expert", split_axis=0, concat_axis=0, tiled=True)


def after(values, *others):
    return lax.optimization_barrier((values,) + others)[0]


def plane_body(tokens, cotangent, gate_probs, expert_ids, gate_up, down):
    half = gate_up.shape[2] // 2
    quarter = tokens.shape[1] // 4
    ids, probs = expert_ids.T, gate_probs.T
    *local, slots = dispatch_rows(ids, probs, tokens, cotangent)
    weights = (gate_up[0], down[0])
    _, _, cut_x0, cut_y0, _ = split_rows(PAIR, 48, half)
    _, _, cut_x1, cut_y1, _ = split_rows(2 * PAIR, PAIR, half)
    _, _, cut_x2, cut_y2, _ = split_rows(PAIR, 32, half)

    def other_core(rows):
        return exchange(rows, "expert", 1)

    def to_plane(to_x, to_y):
        return exchange(to_x, "dp", 1), exchange(to_y, "dp", 2)

    rows_2 = exchange(local[2], "expert", 4)
    rows_1 = exchange(local[1], "expert", 2)
    own_0, to_x, to_y, inner_0 = expert_rows(
        (local[0], other_core(local[0][CAP:])), *weights, 48
    )
    got_x0, got_y0 = to_plane(to_x, to_y)
    low_0, top_0 = to_plane(got_y0[:cut_y0], got_x0[:cut_x0])
    rows_2, rows_1 = after((rows_2, rows_1), inner_0)
    other_2, other_1 = other_core(rows_2[CAP:]), other_core(rows_1[CAP:])
    rows_3 = exchange(after(local[3], rows_2), "expert", 6)
    own_1, to_x, to_y, inner_1, inner_2 = expert_rows(
        (rows_1, other_1, rows_2, other_2), *weights, PAIR
    )
    got_x1, got_y1 = to_plane(*after((to_x, to_y), low_0, top_0))
    sums = gradients(
        ((PAIR, 48, 0, 0),), (own_0, got_x0, got_y0, top_0, low_0), half, quarter
    )
    back_1, back_2 = after((inner_1, inner_2), *sums)
    inner_1, inner_2 = exchange(back_1, "expert", 2), exchange(back_2, "expert", 4)
    rows_3 = after(rows_3, inner_1, inner_2)
    own_2, to_x, to_y, inner_3 = expert_rows(
        (rows_3, other_core(rows_3[CAP:])), *weights, 32
    )
    got_x2, got_y2 = to_plane(to_x, to_y)
    got_x1, got_y1 = after((got_x1, got_y1), inner_3)
    low_1, top_1 = to_plane(got_y1[:cut_y1], got_x1[:cut_x1])
    returned = (inner_0, inner_1, inner_2, exchange(inner_3, "expert", 6))
    other = other_core(jnp.concatenate([part[CAP:] for part in returned], axis=0))
    grad_probs = prob_gradients(returned, other, slots, probs)
    got_x2, got_y2 = after((got_x2, got_y2), other)
    low_2, top_2 = to_plane(got_y2[:cut_y2], got_x2[:cut_x2])
    sums = gradients(
        ((2 * PAIR, PAIR, 0, 0),), (own_1, got_x1, got_y1, top_1, low_1), half, quarter, sums
    )
    grad_gu, grad_down = gradients(
        ((PAIR, 32, 0, 0),), (own_2, got_x2, got_y2, top_2, low_2), half, quarter, sums, True
    )
    return (grad_probs.T, grad_gu[None], grad_down[None])


def widen(values, slices, expert_count):
    tail = values.shape[1:]
    spread = values.reshape((EXPERTS, 1, CAP) + tail)
    spread = jnp.broadcast_to(spread, (EXPERTS, slices, CAP) + tail)
    return spread.reshape((expert_count, CAP) + tail)


def sliced_body(tokens, cotangent, gate_probs, expert_ids, gate_up, down):
    expert_count = lax.axis_size("expert")
    slices = expert_count // EXPERTS
    tok_count, width = tokens.shape
    choose_count = expert_ids.shape[1]
    half = gate_up.shape[2] // 2
    slot_rows = EXPERTS * CAP
    flat_ids = expert_ids.reshape(-1)
    choose = (flat_ids[:, None] == jnp.arange(EXPERTS, dtype=jnp.int32)[None, :]).astype(jnp.int32)
    earlier = jnp.cumsum(choose, axis=0) - choose
    slot_of = flat_ids * CAP + jnp.sum(earlier * choose, axis=1)
    picked = jnp.arange(slot_rows, dtype=jnp.int32)[:, None] == slot_of[None, :]
    picked_tok = jnp.any(picked.reshape(slot_rows, tok_count, choose_count), axis=2).astype(BF16)
    slot_prob = jnp.sum(jnp.where(picked, gate_probs.reshape(-1)[None, :], 0.0), axis=1)
    local_x = jnp.dot(picked_tok, tokens, preferred_element_type=F32).astype(BF16)
    local_dy = jnp.dot(picked_tok, cotangent, preferred_element_type=F32)
    local_scaled = (slot_prob[:, None] * local_dy).astype(BF16)
    rows_x = swap(widen(local_x, slices, expert_count)).reshape(-1, width)
    rows_s = swap(widen(local_scaled, slices, expert_count)).reshape(-1, width)
    both = jnp.dot(rows_x, gate_up[0], preferred_element_type=F32)
    gate, up = both[:, :half], both[:, half:]
    sigmoid = jax.nn.sigmoid(gate)
    activated = gate * sigmoid
    hidden = (activated * up).astype(BF16)
    grad_hidden = lax.dot_general(
        rows_s, down[0], (((1,), (1,)), ((), ())), preferred_element_type=F32
    )
    inner = jnp.sum(hidden.astype(F32) * grad_hidden, axis=1)
    grad_gate = (grad_hidden * up * sigmoid * (1.0 + gate * (1.0 - sigmoid))).astype(BF16)
    grad_up = (grad_hidden * activated).astype(BF16)
    grad_both = jnp.concatenate([grad_gate, grad_up], axis=1)
    over_rows = (((0,), (0,)), ((), ()))
    grad_gu = lax.dot_general(rows_x, grad_both, over_rows, preferred_element_type=F32)
    grad_down = lax.dot_general(hidden, rows_s, over_rows, preferred_element_type=F32)
    returned = swap(inner.reshape(expert_count, CAP))
    per_slot = jnp.sum(returned.reshape(EXPERTS, slices, CAP), axis=1).reshape(slot_rows)
    grad_probs = jnp.sum(jnp.where(picked, per_slot[:, None], 0.0), axis=0)
    grad_probs = grad_probs.reshape(tok_count, choose_count) / gate_probs
    reduced_gu = lax.psum_scatter(grad_gu.astype(BF16), "dp", scatter_dimension=0, tiled=True)
    reduced_down = lax.psum_scatter(grad_down.astype(BF16), "dp", scatter_dimension=1, tiled=True)
    return (grad_probs, reduced_gu[None], reduced_down[None])


def solution(mesh):
    whole_experts = mesh.shape["expert"] == EXPERTS and mesh.shape["dp"] == 4
    return jax.shard_map(
        plane_body if whole_experts else sliced_body,
        mesh=mesh,
        in_specs=(
            P(("dp", "expert"), None),
            P(("dp", "expert"), None),
            P(("dp", "expert"), None),
            P(("dp", "expert"), None),
            P("expert", None, None),
            P("expert", None, None),
        ),
        out_specs=(P(("dp", "expert"), None), P("expert", "dp", None), P("expert", None, "dp")),
        check_vma=False,
    )
```

```python
import functools

import jax
import jax.numpy as jnp
from jax import lax
from jax.experimental import pallas as pl
from jax.experimental.pallas import tpu as pltpu
from jax.sharding import PartitionSpec as P

EXPERTS = 8
CAP = 40
PAIR = 2 * CAP
LANES = 128
TILE = 256
MIB = 1024 * 1024
BF16 = jnp.bfloat16
F32 = jnp.float32


def dispatch_kernel(ids_ref, probs_ref, x_ref, dy_ref, *outs):
    row_refs, slot_ref = outs[:-1], outs[-1]
    me = lax.axis_index("expert")
    tok = x_ref.shape[0]
    width = x_ref.shape[1]
    numbers = lax.broadcasted_iota(jnp.int32, (EXPERTS, tok), 0)
    first = jnp.bitwise_xor(ids_ref[0:1, :], me) == numbers
    second = jnp.bitwise_xor(ids_ref[1:2, :], me) == numbers
    either = jnp.where(first | second, 1.0, 0.0)
    prob = jnp.where(first, probs_ref[0:1, :], 0.0) + jnp.where(second, probs_ref[1:2, :], 0.0)
    before = jnp.where(
        lax.broadcasted_iota(jnp.int32, (tok, tok), 0)
        < lax.broadcasted_iota(jnp.int32, (tok, tok), 1),
        1.0,
        0.0,
    )
    position = jnp.dot(either.astype(BF16), before.astype(BF16), preferred_element_type=F32)
    slot = position.astype(jnp.int32) + numbers * CAP
    slot_ref[0:1, :] = jnp.sum(jnp.where(first, slot, 0), axis=0, keepdims=True)
    slot_ref[1:2, :] = jnp.sum(jnp.where(second, slot, 0), axis=0, keepdims=True)
    target = jnp.where(either > 0.5, position, -1.0)
    places = lax.broadcasted_iota(jnp.int32, (CAP, tok), 0).astype(F32)
    picks = [
        jnp.where(places == target[e : e + 1, :], 1.0, 0.0) for e in range(EXPERTS)
    ]
    row_prob = jnp.concatenate(
        [jnp.sum(picks[e] * prob[e : e + 1, :], axis=1, keepdims=True) for e in range(EXPERTS)],
        axis=0,
    )
    pick = jnp.concatenate(picks, axis=0).astype(BF16)
    step = 512
    for at in range(0, width, step):
        rows_x = jnp.dot(pick, x_ref[:, at : at + step], preferred_element_type=F32)
        rows_dy = jnp.dot(pick, dy_ref[:, at : at + step], preferred_element_type=F32)
        scaled = row_prob * rows_dy
        for pair, ref in enumerate(row_refs):
            part = slice(pair * PAIR, (pair + 1) * PAIR)
            ref[:, at : at + step] = rows_x[part].astype(BF16)
            ref[:, width + at : width + at + step] = scaled[part].astype(BF16)


def dispatch_rows(ids, probs, tokens, cotangent):
    tok, width = tokens.shape
    return pl.pallas_call(
        dispatch_kernel,
        out_shape=[jax.ShapeDtypeStruct((PAIR, 2 * width), BF16)] * (EXPERTS // 2)
        + [jax.ShapeDtypeStruct((2, tok), jnp.int32)],
        compiler_params=pltpu.CompilerParams(vmem_limit_bytes=16 * MIB),
        cost_estimate=pl.CostEstimate(
            flops=4 * EXPERTS * CAP * tok * width, bytes_accessed=4_000_000, transcendentals=0
        ),
        name="dispatch_rows",
    )(ids, probs, tokens, cotangent)


def split_rows(count, top, half):
    blocks = 3 * half // TILE
    low = count - top
    from_x, from_y = (blocks + 4) * top, (blocks + 4) * low
    sizes = (from_x + blocks * low + 4 * count, from_y + blocks * top + 4 * count)
    return blocks, low, from_x, from_y, sizes


def expert_kernel(pairs, top, relays, *refs):
    row_refs, (gate_ref, up_ref, down_ref), rest = (
        refs[: 2 * pairs],
        refs[2 * pairs : 2 * pairs + 3],
        refs[2 * pairs + 3 :],
    )
    relay_refs, rest = rest[: len(relays)], rest[len(relays) :]
    *out_refs, x_rows, s_rows, s_turned, total = rest
    direct = top is None
    if direct:
        plane_refs, inner_refs = out_refs[:4], out_refs[4:]
        own_ref, to_x, to_y = plane_refs[:3]
    else:
        (own_ref, to_x, to_y), inner_refs = out_refs[:3], out_refs[3:]
    count = pairs * PAIR
    width = gate_ref.shape[0]
    steps = pl.num_programs(0)
    half = TILE * 3
    quarter = width // 4
    blocks, low, from_x, from_y, sizes = split_rows(count, top or 0, half)
    step = pl.program_id(0)
    group = lax.axis_index("dp")

    @pl.when(step == 0)
    def _():
        for ref, relay, size, at in zip((to_x, to_y), relay_refs, relays, sizes):
            ref[at : at + size] = relay[:size]
        for rows, start in ((x_rows, 0), (s_rows, width)):
            rows[...] = jnp.concatenate(
                [ref[:CAP, start : start + width].astype(F32) for ref in row_refs],
                axis=0,
            ).astype(BF16)
        for q in range(4):
            rows = (x_rows, s_rows)[q // 2]

            def cut(mask):
                at = jnp.bitwise_xor(group, mask) * quarter + q % 2 * TILE
                return rows[:, pl.ds(pl.multiple_of(at, TILE), TILE)]

            at = blocks + q
            if direct:
                for mask, ref in enumerate(plane_refs):
                    ref[at * count : (at + 1) * count] = cut(mask)
                continue
            own_ref[at * count : (at + 1) * count] = cut(0)
            far = cut(3)
            to_x[at * top : (at + 1) * top] = far[:top]
            to_y[at * low : (at + 1) * low] = far[top:]
            start = from_x + blocks * low + q * count
            to_x[start : start + count] = cut(1)
            start = from_y + blocks * top + q * count
            to_y[start : start + count] = cut(2)
        s_turned[...] = s_rows[...].T
        total[...] = jnp.zeros_like(total)

    x = x_rows[...]
    gate = jnp.dot(x, gate_ref[...], preferred_element_type=F32)
    up = jnp.dot(x, up_ref[...], preferred_element_type=F32)
    grad_hidden = jnp.dot(down_ref[...], s_turned[...], preferred_element_type=F32).T
    sigmoid = 1.0 / (1.0 + jnp.exp(-gate))
    activated = gate * sigmoid
    hidden = (activated * up).astype(BF16)
    grad_gate = (grad_hidden * up * sigmoid * (1.0 + gate * (1.0 - sigmoid))).astype(BF16)
    grad_up = (grad_hidden * activated).astype(BF16)
    total[...] += jnp.sum(hidden.astype(F32) * grad_hidden, axis=1, keepdims=True)
    for part, values in enumerate((grad_gate, grad_up, hidden)):
        block = part * steps + step

        def rows_at(start, count):
            return pl.ds(pl.multiple_of(start + block * count, 16), count)

        if direct:
            for ref in plane_refs:
                ref[rows_at(0, count)] = values
            continue
        own_ref[rows_at(0, count)] = values
        to_x[rows_at(0, top)] = values[:top]
        to_x[rows_at(from_x, low)] = values[top:]
        to_y[rows_at(0, low)] = values[top:]
        to_y[rows_at(from_y, top)] = values[:top]

    @pl.when(step == steps - 1)
    def _():
        for pair, ref in enumerate(inner_refs):
            part = total[pair * PAIR : (pair + 1) * PAIR]
            ref[...] = jnp.broadcast_to(part, ref.shape)


def expert_rows(rows, weight_gu, weight_down, top, relay=(), relays=()):
    pairs = len(rows) // 2
    count = pairs * PAIR
    width, both = weight_gu.shape
    half = both // 2
    steps = half // TILE
    blocks, _, _, _, sizes = split_rows(count, top or 0, half)
    whole_rows = (blocks + 4) * count
    if top is None:
        sizes = [whole_rows] * 4
    else:
        sizes = [whole_rows] + [size + extra for size, extra in zip(sizes, relays or (0, 0))]
    shapes = [(size, TILE) for size in sizes]

    def whole(shape):
        return pl.BlockSpec(shape, lambda h: (0, 0))

    return pl.pallas_call(
        functools.partial(expert_kernel, pairs, top, tuple(relays)),
        grid=(steps,),
        in_specs=[
            *[whole(part.shape) for part in rows],
            pl.BlockSpec((width, TILE), lambda h: (0, h)),
            pl.BlockSpec((width, TILE), lambda h: (0, h + steps)),
            pl.BlockSpec((TILE, width), lambda h: (h, 0)),
            *[whole(part.shape) for part in relay],
        ],
        out_specs=[whole(shape) for shape in shapes] + [whole((PAIR, LANES))] * pairs,
        out_shape=[jax.ShapeDtypeStruct(shape, BF16) for shape in shapes]
        + [jax.ShapeDtypeStruct((PAIR, LANES), F32)] * pairs,
        scratch_shapes=[
            pltpu.VMEM((count, width), BF16),
            pltpu.VMEM((count, width), BF16),
            pltpu.VMEM((width, count), BF16),
            pltpu.VMEM((count, 1), F32),
        ],
        compiler_params=pltpu.CompilerParams(vmem_limit_bytes=20 * MIB),
        cost_estimate=pl.CostEstimate(flops=1_000, bytes_accessed=1_000, transcendentals=0),
        name="expert_rows",
    )(*rows, weight_gu, weight_gu, weight_down, *relay)


def gradient_kernel(chunks, half, adding, *refs):
    groups = []
    for chunk in chunks:
        size = 4 if chunk[1] is None else 5
        groups.append(refs[:size])
        refs = refs[size:]
    if adding:
        (acc_gu, acc_down), refs = refs[:2], refs[2:]
    out_gu, out_down, turned, s_rows = refs
    both = 2 * half // TILE

    def far_parts(block, top, low, at_top, at_low, far_top, far_low):
        return [
            far_top[at_top + block * top : at_top + (block + 1) * top],
            far_low[at_low + block * low : at_low + (block + 1) * low],
        ]

    def factor(block):
        parts = []
        for (count, top, at_top, at_low), group in zip(chunks, groups):
            if top is None:
                parts += [ref[block * count : (block + 1) * count] for ref in group]
                continue
            own, got_x, got_y, *far = group
            _, low, from_x, from_y, _ = split_rows(count, top, half)
            parts += [
                own[block * count : (block + 1) * count],
                got_x[block * top : (block + 1) * top],
                got_x[from_x + block * low : from_x + (block + 1) * low],
                got_y[from_y + block * top : from_y + (block + 1) * top],
                got_y[block * low : (block + 1) * low],
            ] + far_parts(block, top, low, at_top, at_low, *far)
        return jnp.concatenate(parts, axis=0)

    def piece(q):
        parts = []
        for (count, top, at_top, at_low), group in zip(chunks, groups):
            if top is None:
                block = 3 * half // TILE + q
                parts += [ref[block * count : (block + 1) * count] for ref in group]
                continue
            own, got_x, got_y, *far = group
            blocks, low, from_x, from_y, _ = split_rows(count, top, half)
            block = blocks + q
            at_x = from_x + blocks * low + q * count
            at_y = from_y + blocks * top + q * count
            parts += [
                own[block * count : (block + 1) * count],
                got_x[at_x : at_x + count],
                got_y[at_y : at_y + count],
            ] + far_parts(block, top, low, at_top, at_low, *far)
        return jnp.concatenate(parts, axis=0)

    for q in range(2):
        turned[q * TILE : (q + 1) * TILE, :] = piece(q).T
        s_rows[:, q * TILE : (q + 1) * TILE] = piece(2 + q)
    for block in range(both):
        at = slice(block * TILE, (block + 1) * TILE)
        grad = jnp.dot(turned[...], factor(block), preferred_element_type=F32)
        if adding:
            grad = grad + acc_gu[:, at]
        out_gu[:, at] = grad.astype(out_gu.dtype)
    for block in range(half // TILE):
        at = slice(block * TILE, (block + 1) * TILE)
        grad = jnp.dot(factor(both + block).T, s_rows[...], preferred_element_type=F32)
        if adding:
            grad = grad + acc_down[at, :]
        out_down[at, :] = grad.astype(out_down.dtype)


def gradients(chunks, pieces, half, quarter, sums=(), final=False):
    kept = BF16 if final else F32
    rows = 4 * sum(chunk[0] for chunk in chunks)
    vmem = pl.BlockSpec(memory_space=pltpu.VMEM)
    return pl.pallas_call(
        functools.partial(gradient_kernel, chunks, half, len(sums)),
        in_specs=[vmem] * (len(pieces) + len(sums)),
        out_specs=[vmem] * 2,
        out_shape=[
            jax.ShapeDtypeStruct((quarter, 2 * half), kept),
            jax.ShapeDtypeStruct((half, quarter), kept),
        ],
        scratch_shapes=[pltpu.VMEM((quarter, rows), BF16), pltpu.VMEM((rows, quarter), BF16)],
        compiler_params=pltpu.CompilerParams(vmem_limit_bytes=20 * MIB),
        cost_estimate=pl.CostEstimate(flops=1_000, bytes_accessed=1_000, transcendentals=0),
        name="gradients",
    )(*pieces, *sums)


def prob_kernel(own_0, own_1, own_2, own_3, other_ref, slot_ref, prob_ref, out_ref):
    owns = (own_0, own_1, own_2, own_3)
    tok = slot_ref.shape[1]
    places = lax.broadcasted_iota(jnp.int32, (CAP, tok), 0)
    for choice in range(2):
        slot = slot_ref[choice : choice + 1, :]
        grad = jnp.zeros((CAP, tok), F32)
        for e in range(EXPERTS):
            chunk = e // 2
            if e % 2 == 0:
                values = owns[chunk][:CAP, :]
            else:
                values = other_ref[chunk * CAP : (chunk + 1) * CAP, :]
            grad += jnp.where(places + e * CAP == slot, values, 0.0)
        grad = jnp.sum(grad, axis=0, keepdims=True)
        out_ref[choice : choice + 1, :] = grad / prob_ref[choice : choice + 1, :]


def prob_gradients(owns, other, slots, probs):
    return pl.pallas_call(
        prob_kernel,
        out_shape=jax.ShapeDtypeStruct(probs.shape, F32),
        compiler_params=pltpu.CompilerParams(vmem_limit_bytes=4 * MIB),
        cost_estimate=pl.CostEstimate(flops=1_000, bytes_accessed=1_000, transcendentals=0),
        name="prob_gradients",
    )(*owns, other, slots, probs)


def exchange(values, axis, mask):
    size = lax.axis_size(axis)
    return lax.ppermute(values, axis, [(n, n ^ mask) for n in range(size)])


def swap(values):
    return lax.all_to_all(values, "expert", split_axis=0, concat_axis=0, tiled=True)


def after(values, *others):
    return lax.optimization_barrier((values,) + others)[0]


def plane_body(tokens, cotangent, gate_probs, expert_ids, gate_up, down):
    half = gate_up.shape[2] // 2
    quarter = tokens.shape[1] // 4
    ids, probs = expert_ids.T, gate_probs.T
    *local, slots = dispatch_rows(ids, probs, tokens, cotangent)
    weights = (gate_up[0], down[0])
    _, _, cut_x1, cut_y1, _ = split_rows(2 * PAIR, PAIR, half)
    _, _, cut_x2, cut_y2, _ = split_rows(PAIR, 32, half)

    def other_core(rows):
        return exchange(rows, "expert", 1)

    def to_plane(to_x, to_y):
        return exchange(to_x, "dp", 1), exchange(to_y, "dp", 2)

    rows_2 = exchange(local[2], "expert", 4)
    rows_1 = exchange(local[1], "expert", 2)
    own_0, *sent_0, inner_0 = expert_rows(
        (local[0], other_core(local[0][CAP:])), *weights, None
    )
    got_0 = tuple(exchange(part, "dp", mask + 1) for mask, part in enumerate(sent_0))
    rows_2, rows_1 = after((rows_2, rows_1), inner_0)
    other_2, other_1 = other_core(rows_2[CAP:]), other_core(rows_1[CAP:])
    rows_3 = exchange(after(local[3], rows_2), "expert", 6)
    own_1, to_x, to_y, inner_1, inner_2 = expert_rows(
        (rows_1, other_1, rows_2, other_2), *weights, PAIR
    )
    got_x1, got_y1 = to_plane(*after((to_x, to_y), *got_0))
    sums = gradients(((PAIR, None, 0, 0),), (own_0, *got_0), half, quarter)
    back_1, back_2 = after((inner_1, inner_2), *sums)
    inner_1, inner_2 = exchange(back_1, "expert", 2), exchange(back_2, "expert", 4)
    rows_3 = after(rows_3, inner_1, inner_2)
    own_2, to_x, to_y, inner_3 = expert_rows(
        (rows_3, other_core(rows_3[CAP:])), *weights, 32
    )
    got_x2, got_y2 = to_plane(to_x, to_y)
    got_x1, got_y1 = after((got_x1, got_y1), inner_3)
    low_1, top_1 = to_plane(got_y1[:cut_y1], got_x1[:cut_x1])
    returned = (inner_0, inner_1, inner_2, exchange(inner_3, "expert", 6))
    other = other_core(jnp.concatenate([part[CAP:] for part in returned], axis=0))
    grad_probs = prob_gradients(returned, other, slots, probs)
    got_x2, got_y2 = after((got_x2, got_y2), other)
    low_2, top_2 = to_plane(got_y2[:cut_y2], got_x2[:cut_x2])
    sums = gradients(
        ((2 * PAIR, PAIR, 0, 0),), (own_1, got_x1, got_y1, top_1, low_1), half, quarter, sums
    )
    grad_gu, grad_down = gradients(
        ((PAIR, 32, 0, 0),), (own_2, got_x2, got_y2, top_2, low_2), half, quarter, sums, True
    )
    return (grad_probs.T, grad_gu[None], grad_down[None])


def widen(values, slices, expert_count):
    tail = values.shape[1:]
    spread = values.reshape((EXPERTS, 1, CAP) + tail)
    spread = jnp.broadcast_to(spread, (EXPERTS, slices, CAP) + tail)
    return spread.reshape((expert_count, CAP) + tail)


def sliced_body(tokens, cotangent, gate_probs, expert_ids, gate_up, down):
    expert_count = lax.axis_size("expert")
    slices = expert_count // EXPERTS
    tok_count, width = tokens.shape
    choose_count = expert_ids.shape[1]
    half = gate_up.shape[2] // 2
    slot_rows = EXPERTS * CAP
    flat_ids = expert_ids.reshape(-1)
    choose = (flat_ids[:, None] == jnp.arange(EXPERTS, dtype=jnp.int32)[None, :]).astype(jnp.int32)
    earlier = jnp.cumsum(choose, axis=0) - choose
    slot_of = flat_ids * CAP + jnp.sum(earlier * choose, axis=1)
    picked = jnp.arange(slot_rows, dtype=jnp.int32)[:, None] == slot_of[None, :]
    picked_tok = jnp.any(picked.reshape(slot_rows, tok_count, choose_count), axis=2).astype(BF16)
    slot_prob = jnp.sum(jnp.where(picked, gate_probs.reshape(-1)[None, :], 0.0), axis=1)
    local_x = jnp.dot(picked_tok, tokens, preferred_element_type=F32).astype(BF16)
    local_dy = jnp.dot(picked_tok, cotangent, preferred_element_type=F32)
    local_scaled = (slot_prob[:, None] * local_dy).astype(BF16)
    rows_x = swap(widen(local_x, slices, expert_count)).reshape(-1, width)
    rows_s = swap(widen(local_scaled, slices, expert_count)).reshape(-1, width)
    both = jnp.dot(rows_x, gate_up[0], preferred_element_type=F32)
    gate, up = both[:, :half], both[:, half:]
    sigmoid = jax.nn.sigmoid(gate)
    activated = gate * sigmoid
    hidden = (activated * up).astype(BF16)
    grad_hidden = lax.dot_general(
        rows_s, down[0], (((1,), (1,)), ((), ())), preferred_element_type=F32
    )
    inner = jnp.sum(hidden.astype(F32) * grad_hidden, axis=1)
    grad_gate = (grad_hidden * up * sigmoid * (1.0 + gate * (1.0 - sigmoid))).astype(BF16)
    grad_up = (grad_hidden * activated).astype(BF16)
    grad_both = jnp.concatenate([grad_gate, grad_up], axis=1)
    over_rows = (((0,), (0,)), ((), ()))
    grad_gu = lax.dot_general(rows_x, grad_both, over_rows, preferred_element_type=F32)
    grad_down = lax.dot_general(hidden, rows_s, over_rows, preferred_element_type=F32)
    returned = swap(inner.reshape(expert_count, CAP))
    per_slot = jnp.sum(returned.reshape(EXPERTS, slices, CAP), axis=1).reshape(slot_rows)
    grad_probs = jnp.sum(jnp.where(picked, per_slot[:, None], 0.0), axis=0)
    grad_probs = grad_probs.reshape(tok_count, choose_count) / gate_probs
    reduced_gu = lax.psum_scatter(grad_gu.astype(BF16), "dp", scatter_dimension=0, tiled=True)
    reduced_down = lax.psum_scatter(grad_down.astype(BF16), "dp", scatter_dimension=1, tiled=True)
    return (grad_probs, reduced_gu[None], reduced_down[None])


def solution(mesh):
    whole_experts = mesh.shape["expert"] == EXPERTS and mesh.shape["dp"] == 4
    return jax.shard_map(
        plane_body if whole_experts else sliced_body,
        mesh=mesh,
        in_specs=(
            P(("dp", "expert"), None),
            P(("dp", "expert"), None),
            P(("dp", "expert"), None),
            P(("dp", "expert"), None),
            P("expert", None, None),
            P("expert", None, None),
        ),
        out_specs=(P(("dp", "expert"), None), P("expert", "dp", None), P("expert", None, "dp")),
        check_vma=False,
    )
```

```python
import functools

import jax
import jax.numpy as jnp
from jax import lax
from jax.experimental import pallas as pl
from jax.experimental.pallas import tpu as pltpu
from jax.sharding import PartitionSpec as P

EXPERTS = 8
CAP = 40
PAIR = 2 * CAP
LANES = 128
TILE = 256
MIB = 1024 * 1024
BF16 = jnp.bfloat16
F32 = jnp.float32


def dispatch_kernel(ids_ref, probs_ref, x_ref, dy_ref, *outs):
    row_refs, slot_ref = outs[:-1], outs[-1]
    me = lax.axis_index("expert")
    tok = x_ref.shape[0]
    width = x_ref.shape[1]
    numbers = lax.broadcasted_iota(jnp.int32, (EXPERTS, tok), 0)
    first = jnp.bitwise_xor(ids_ref[0:1, :], me) == numbers
    second = jnp.bitwise_xor(ids_ref[1:2, :], me) == numbers
    either = jnp.where(first | second, 1.0, 0.0)
    prob = jnp.where(first, probs_ref[0:1, :], 0.0) + jnp.where(second, probs_ref[1:2, :], 0.0)
    before = jnp.where(
        lax.broadcasted_iota(jnp.int32, (tok, tok), 0)
        < lax.broadcasted_iota(jnp.int32, (tok, tok), 1),
        1.0,
        0.0,
    )
    position = jnp.dot(either.astype(BF16), before.astype(BF16), preferred_element_type=F32)
    slot = position.astype(jnp.int32) + numbers * CAP
    slot_ref[0:1, :] = jnp.sum(jnp.where(first, slot, 0), axis=0, keepdims=True)
    slot_ref[1:2, :] = jnp.sum(jnp.where(second, slot, 0), axis=0, keepdims=True)
    target = jnp.where(either > 0.5, position, -1.0)
    places = lax.broadcasted_iota(jnp.int32, (CAP, tok), 0).astype(F32)
    picks = [
        jnp.where(places == target[e : e + 1, :], 1.0, 0.0) for e in range(EXPERTS)
    ]
    row_prob = jnp.concatenate(
        [jnp.sum(picks[e] * prob[e : e + 1, :], axis=1, keepdims=True) for e in range(EXPERTS)],
        axis=0,
    )
    pick = jnp.concatenate(picks, axis=0).astype(BF16)
    step = 512
    for at in range(0, width, step):
        rows_x = jnp.dot(pick, x_ref[:, at : at + step], preferred_element_type=F32)
        rows_dy = jnp.dot(pick, dy_ref[:, at : at + step], preferred_element_type=F32)
        scaled = row_prob * rows_dy
        for pair, ref in enumerate(row_refs):
            part = slice(pair * PAIR, (pair + 1) * PAIR)
            ref[:, at : at + step] = rows_x[part].astype(BF16)
            ref[:, width + at : width + at + step] = scaled[part].astype(BF16)


def dispatch_rows(ids, probs, tokens, cotangent):
    tok, width = tokens.shape
    return pl.pallas_call(
        dispatch_kernel,
        out_shape=[jax.ShapeDtypeStruct((PAIR, 2 * width), BF16)] * (EXPERTS // 2)
        + [jax.ShapeDtypeStruct((2, tok), jnp.int32)],
        compiler_params=pltpu.CompilerParams(vmem_limit_bytes=16 * MIB),
        cost_estimate=pl.CostEstimate(
            flops=4 * EXPERTS * CAP * tok * width, bytes_accessed=4_000_000, transcendentals=0
        ),
        name="dispatch_rows",
    )(ids, probs, tokens, cotangent)


def split_rows(count, top, half):
    blocks = 3 * half // TILE
    low = count - top
    from_x, from_y = (blocks + 4) * top, (blocks + 4) * low
    sizes = (from_x + blocks * low + 4 * count, from_y + blocks * top + 4 * count)
    return blocks, low, from_x, from_y, sizes


def expert_kernel(pairs, top, relays, *refs):
    row_refs, (gate_ref, up_ref, down_ref), rest = (
        refs[: 2 * pairs],
        refs[2 * pairs : 2 * pairs + 3],
        refs[2 * pairs + 3 :],
    )
    relay_refs, rest = rest[: len(relays)], rest[len(relays) :]
    *out_refs, x_rows, s_rows, s_turned, total = rest
    direct = top is None
    if direct:
        plane_refs, inner_refs = out_refs[:4], out_refs[4:]
        own_ref, to_x, to_y = plane_refs[:3]
    else:
        (own_ref, to_x, to_y), inner_refs = out_refs[:3], out_refs[3:]
    count = pairs * PAIR
    width = gate_ref.shape[0]
    steps = pl.num_programs(0)
    half = TILE * 3
    quarter = width // 4
    blocks, low, from_x, from_y, sizes = split_rows(count, top or 0, half)
    step = pl.program_id(0)
    group = lax.axis_index("dp")

    @pl.when(step == 0)
    def _():
        for ref, relay, size, at in zip((to_x, to_y), relay_refs, relays, sizes):
            ref[at : at + size] = relay[:size]
        for rows, start in ((x_rows, 0), (s_rows, width)):
            rows[...] = jnp.concatenate(
                [ref[:CAP, start : start + width].astype(F32) for ref in row_refs],
                axis=0,
            ).astype(BF16)
        for q in range(4):
            rows = (x_rows, s_rows)[q // 2]

            def cut(mask):
                at = jnp.bitwise_xor(group, mask) * quarter + q % 2 * TILE
                return rows[:, pl.ds(pl.multiple_of(at, TILE), TILE)]

            at = blocks + q
            if direct:
                for mask, ref in enumerate(plane_refs):
                    ref[at * count : (at + 1) * count] = cut(mask)
                continue
            own_ref[at * count : (at + 1) * count] = cut(0)
            far = cut(3)
            to_x[at * top : (at + 1) * top] = far[:top]
            to_y[at * low : (at + 1) * low] = far[top:]
            start = from_x + blocks * low + q * count
            to_x[start : start + count] = cut(1)
            start = from_y + blocks * top + q * count
            to_y[start : start + count] = cut(2)
        s_turned[...] = s_rows[...].T
        total[...] = jnp.zeros_like(total)

    x = x_rows[...]
    gate = jnp.dot(x, gate_ref[...], preferred_element_type=F32)
    up = jnp.dot(x, up_ref[...], preferred_element_type=F32)
    grad_hidden = jnp.dot(down_ref[...], s_turned[...], preferred_element_type=F32).T
    sigmoid = 1.0 / (1.0 + jnp.exp(-gate))
    activated = gate * sigmoid
    hidden = (activated * up).astype(BF16)
    grad_gate = (grad_hidden * up * sigmoid * (1.0 + gate * (1.0 - sigmoid))).astype(BF16)
    grad_up = (grad_hidden * activated).astype(BF16)
    total[...] += jnp.sum(hidden.astype(F32) * grad_hidden, axis=1, keepdims=True)
    for part, values in enumerate((grad_gate, grad_up, hidden)):
        block = part * steps + step

        def rows_at(start, count):
            return pl.ds(pl.multiple_of(start + block * count, 16), count)

        if direct:
            for ref in plane_refs:
                ref[rows_at(0, count)] = values
            continue
        own_ref[rows_at(0, count)] = values
        to_x[rows_at(0, top)] = values[:top]
        to_x[rows_at(from_x, low)] = values[top:]
        to_y[rows_at(0, low)] = values[top:]
        to_y[rows_at(from_y, top)] = values[:top]

    @pl.when(step == steps - 1)
    def _():
        for pair, ref in enumerate(inner_refs):
            part = total[pair * PAIR : (pair + 1) * PAIR]
            ref[...] = jnp.broadcast_to(part, ref.shape)


def expert_rows(rows, weight_gu, weight_down, top, relay=(), relays=()):
    pairs = len(rows) // 2
    count = pairs * PAIR
    width, both = weight_gu.shape
    half = both // 2
    steps = half // TILE
    blocks, _, _, _, sizes = split_rows(count, top or 0, half)
    whole_rows = (blocks + 4) * count
    if top is None:
        sizes = [whole_rows] * 4
    else:
        sizes = [whole_rows] + [size + extra for size, extra in zip(sizes, relays or (0, 0))]
    shapes = [(size, TILE) for size in sizes]

    def whole(shape):
        return pl.BlockSpec(shape, lambda h: (0, 0))

    return pl.pallas_call(
        functools.partial(expert_kernel, pairs, top, tuple(relays)),
        grid=(steps,),
        in_specs=[
            *[whole(part.shape) for part in rows],
            pl.BlockSpec((width, TILE), lambda h: (0, h)),
            pl.BlockSpec((width, TILE), lambda h: (0, h + steps)),
            pl.BlockSpec((TILE, width), lambda h: (h, 0)),
            *[whole(part.shape) for part in relay],
        ],
        out_specs=[whole(shape) for shape in shapes] + [whole((PAIR, LANES))] * pairs,
        out_shape=[jax.ShapeDtypeStruct(shape, BF16) for shape in shapes]
        + [jax.ShapeDtypeStruct((PAIR, LANES), F32)] * pairs,
        scratch_shapes=[
            pltpu.VMEM((count, width), BF16),
            pltpu.VMEM((count, width), BF16),
            pltpu.VMEM((width, count), BF16),
            pltpu.VMEM((count, 1), F32),
        ],
        compiler_params=pltpu.CompilerParams(vmem_limit_bytes=20 * MIB),
        cost_estimate=pl.CostEstimate(flops=1_000, bytes_accessed=1_000, transcendentals=0),
        name="expert_rows",
    )(*rows, weight_gu, weight_gu, weight_down, *relay)


def gradient_kernel(chunks, half, adding, *refs):
    groups = []
    for chunk in chunks:
        size = 4 if chunk[1] is None else 5
        groups.append(refs[:size])
        refs = refs[size:]
    if adding:
        (acc_gu, acc_down), refs = refs[:2], refs[2:]
    out_gu, out_down, turned, s_rows = refs
    both = 2 * half // TILE

    def far_parts(block, top, low, at_top, at_low, far_top, far_low):
        return [
            far_top[at_top + block * top : at_top + (block + 1) * top],
            far_low[at_low + block * low : at_low + (block + 1) * low],
        ]

    def factor(block):
        parts = []
        for (count, top, at_top, at_low), group in zip(chunks, groups):
            if top is None:
                parts += [ref[block * count : (block + 1) * count] for ref in group]
                continue
            own, got_x, got_y, *far = group
            _, low, from_x, from_y, _ = split_rows(count, top, half)
            parts += [
                own[block * count : (block + 1) * count],
                got_x[block * top : (block + 1) * top],
                got_x[from_x + block * low : from_x + (block + 1) * low],
                got_y[from_y + block * top : from_y + (block + 1) * top],
                got_y[block * low : (block + 1) * low],
            ] + far_parts(block, top, low, at_top, at_low, *far)
        return jnp.concatenate(parts, axis=0)

    def piece(q):
        parts = []
        for (count, top, at_top, at_low), group in zip(chunks, groups):
            if top is None:
                block = 3 * half // TILE + q
                parts += [ref[block * count : (block + 1) * count] for ref in group]
                continue
            own, got_x, got_y, *far = group
            blocks, low, from_x, from_y, _ = split_rows(count, top, half)
            block = blocks + q
            at_x = from_x + blocks * low + q * count
            at_y = from_y + blocks * top + q * count
            parts += [
                own[block * count : (block + 1) * count],
                got_x[at_x : at_x + count],
                got_y[at_y : at_y + count],
            ] + far_parts(block, top, low, at_top, at_low, *far)
        return jnp.concatenate(parts, axis=0)

    for q in range(2):
        turned[q * TILE : (q + 1) * TILE, :] = piece(q).T
        s_rows[:, q * TILE : (q + 1) * TILE] = piece(2 + q)
    for block in range(both):
        at = slice(block * TILE, (block + 1) * TILE)
        grad = jnp.dot(turned[...], factor(block), preferred_element_type=F32)
        if adding:
            grad = grad + acc_gu[:, at]
        out_gu[:, at] = grad.astype(out_gu.dtype)
    for block in range(half // TILE):
        at = slice(block * TILE, (block + 1) * TILE)
        grad = jnp.dot(factor(both + block).T, s_rows[...], preferred_element_type=F32)
        if adding:
            grad = grad + acc_down[at, :]
        out_down[at, :] = grad.astype(out_down.dtype)


def gradients(chunks, pieces, half, quarter, sums=(), final=False):
    kept = BF16 if final else F32
    rows = 4 * sum(chunk[0] for chunk in chunks)
    vmem = pl.BlockSpec(memory_space=pltpu.VMEM)
    return pl.pallas_call(
        functools.partial(gradient_kernel, chunks, half, len(sums)),
        in_specs=[vmem] * (len(pieces) + len(sums)),
        out_specs=[vmem] * 2,
        out_shape=[
            jax.ShapeDtypeStruct((quarter, 2 * half), kept),
            jax.ShapeDtypeStruct((half, quarter), kept),
        ],
        scratch_shapes=[pltpu.VMEM((quarter, rows), BF16), pltpu.VMEM((rows, quarter), BF16)],
        compiler_params=pltpu.CompilerParams(vmem_limit_bytes=20 * MIB),
        cost_estimate=pl.CostEstimate(flops=1_000, bytes_accessed=1_000, transcendentals=0),
        name="gradients",
    )(*pieces, *sums)


def prob_kernel(own_0, own_1, own_2, own_3, other_ref, slot_ref, prob_ref, out_ref):
    owns = (own_0, own_1, own_2, own_3)
    tok = slot_ref.shape[1]
    places = lax.broadcasted_iota(jnp.int32, (CAP, tok), 0)
    for choice in range(2):
        slot = slot_ref[choice : choice + 1, :]
        grad = jnp.zeros((CAP, tok), F32)
        for e in range(EXPERTS):
            chunk = e // 2
            if e % 2 == 0:
                values = owns[chunk][:CAP, :]
            else:
                values = other_ref[chunk * CAP : (chunk + 1) * CAP, :]
            grad += jnp.where(places + e * CAP == slot, values, 0.0)
        grad = jnp.sum(grad, axis=0, keepdims=True)
        out_ref[choice : choice + 1, :] = grad / prob_ref[choice : choice + 1, :]


def prob_gradients(owns, other, slots, probs):
    return pl.pallas_call(
        prob_kernel,
        out_shape=jax.ShapeDtypeStruct(probs.shape, F32),
        compiler_params=pltpu.CompilerParams(vmem_limit_bytes=4 * MIB),
        cost_estimate=pl.CostEstimate(flops=1_000, bytes_accessed=1_000, transcendentals=0),
        name="prob_gradients",
    )(*owns, other, slots, probs)


def exchange(values, axis, mask):
    size = lax.axis_size(axis)
    return lax.ppermute(values, axis, [(n, n ^ mask) for n in range(size)])


def swap(values):
    return lax.all_to_all(values, "expert", split_axis=0, concat_axis=0, tiled=True)


def after(values, *others):
    return lax.optimization_barrier((values,) + others)[0]


def plane_body(tokens, cotangent, gate_probs, expert_ids, gate_up, down):
    half = gate_up.shape[2] // 2
    quarter = tokens.shape[1] // 4
    ids, probs = expert_ids.T, gate_probs.T
    *local, slots = dispatch_rows(ids, probs, tokens, cotangent)
    weights = (gate_up[0], down[0])
    _, _, cut_x1, cut_y1, _ = split_rows(2 * PAIR, PAIR, half)
    _, _, cut_x2, cut_y2, _ = split_rows(PAIR, 32, half)

    def other_core(rows):
        return exchange(rows, "expert", 1)

    def to_plane(to_x, to_y):
        return exchange(to_x, "dp", 1), exchange(to_y, "dp", 2)

    rows_2 = exchange(local[2], "expert", 4)
    rows_1 = exchange(local[1], "expert", 2)
    own_0, *sent_0, inner_0 = expert_rows(
        (local[0], other_core(local[0][CAP:])), *weights, None
    )
    got_0 = tuple(exchange(part, "dp", mask + 1) for mask, part in enumerate(sent_0))
    rows_2, rows_1 = after((rows_2, rows_1), inner_0)
    other_2, other_1 = other_core(rows_2[CAP:]), other_core(rows_1[CAP:])
    rows_3 = exchange(after(local[3], rows_2), "expert", 6)
    own_1, to_x, to_y, inner_1, inner_2 = expert_rows(
        (rows_1, other_1, rows_2, other_2), *weights, PAIR
    )
    got_x1, got_y1 = to_plane(*after((to_x, to_y), *got_0))
    sums = gradients(((PAIR, None, 0, 0),), (own_0, *got_0), half, quarter)
    back_1, back_2 = after((inner_1, inner_2), *sums)
    inner_1, inner_2 = exchange(back_1, "expert", 2), exchange(back_2, "expert", 4)
    rows_3 = after(rows_3, *sums)
    own_2, to_x, to_y, inner_3 = expert_rows(
        (rows_3, other_core(rows_3[CAP:])), *weights, 32
    )
    got_x2, got_y2 = to_plane(to_x, to_y)
    got_x1, got_y1 = after((got_x1, got_y1), inner_3)
    low_1, top_1 = to_plane(got_y1[:cut_y1], got_x1[:cut_x1])
    returned = (inner_0, inner_1, inner_2, exchange(inner_3, "expert", 6))
    other = other_core(jnp.concatenate([part[CAP:] for part in returned], axis=0))
    grad_probs = prob_gradients(returned, other, slots, probs)
    got_x2, got_y2 = after((got_x2, got_y2), other)
    low_2, top_2 = to_plane(got_y2[:cut_y2], got_x2[:cut_x2])
    sums = gradients(
        ((2 * PAIR, PAIR, 0, 0),), (own_1, got_x1, got_y1, top_1, low_1), half, quarter, sums
    )
    grad_gu, grad_down = gradients(
        ((PAIR, 32, 0, 0),), (own_2, got_x2, got_y2, top_2, low_2), half, quarter, sums, True
    )
    return (grad_probs.T, grad_gu[None], grad_down[None])


def widen(values, slices, expert_count):
    tail = values.shape[1:]
    spread = values.reshape((EXPERTS, 1, CAP) + tail)
    spread = jnp.broadcast_to(spread, (EXPERTS, slices, CAP) + tail)
    return spread.reshape((expert_count, CAP) + tail)


def sliced_body(tokens, cotangent, gate_probs, expert_ids, gate_up, down):
    expert_count = lax.axis_size("expert")
    slices = expert_count // EXPERTS
    tok_count, width = tokens.shape
    choose_count = expert_ids.shape[1]
    half = gate_up.shape[2] // 2
    slot_rows = EXPERTS * CAP
    flat_ids = expert_ids.reshape(-1)
    choose = (flat_ids[:, None] == jnp.arange(EXPERTS, dtype=jnp.int32)[None, :]).astype(jnp.int32)
    earlier = jnp.cumsum(choose, axis=0) - choose
    slot_of = flat_ids * CAP + jnp.sum(earlier * choose, axis=1)
    picked = jnp.arange(slot_rows, dtype=jnp.int32)[:, None] == slot_of[None, :]
    picked_tok = jnp.any(picked.reshape(slot_rows, tok_count, choose_count), axis=2).astype(BF16)
    slot_prob = jnp.sum(jnp.where(picked, gate_probs.reshape(-1)[None, :], 0.0), axis=1)
    local_x = jnp.dot(picked_tok, tokens, preferred_element_type=F32).astype(BF16)
    local_dy = jnp.dot(picked_tok, cotangent, preferred_element_type=F32)
    local_scaled = (slot_prob[:, None] * local_dy).astype(BF16)
    rows_x = swap(widen(local_x, slices, expert_count)).reshape(-1, width)
    rows_s = swap(widen(local_scaled, slices, expert_count)).reshape(-1, width)
    both = jnp.dot(rows_x, gate_up[0], preferred_element_type=F32)
    gate, up = both[:, :half], both[:, half:]
    sigmoid = jax.nn.sigmoid(gate)
    activated = gate * sigmoid
    hidden = (activated * up).astype(BF16)
    grad_hidden = lax.dot_general(
        rows_s, down[0], (((1,), (1,)), ((), ())), preferred_element_type=F32
    )
    inner = jnp.sum(hidden.astype(F32) * grad_hidden, axis=1)
    grad_gate = (grad_hidden * up * sigmoid * (1.0 + gate * (1.0 - sigmoid))).astype(BF16)
    grad_up = (grad_hidden * activated).astype(BF16)
    grad_both = jnp.concatenate([grad_gate, grad_up], axis=1)
    over_rows = (((0,), (0,)), ((), ()))
    grad_gu = lax.dot_general(rows_x, grad_both, over_rows, preferred_element_type=F32)
    grad_down = lax.dot_general(hidden, rows_s, over_rows, preferred_element_type=F32)
    returned = swap(inner.reshape(expert_count, CAP))
    per_slot = jnp.sum(returned.reshape(EXPERTS, slices, CAP), axis=1).reshape(slot_rows)
    grad_probs = jnp.sum(jnp.where(picked, per_slot[:, None], 0.0), axis=0)
    grad_probs = grad_probs.reshape(tok_count, choose_count) / gate_probs
    reduced_gu = lax.psum_scatter(grad_gu.astype(BF16), "dp", scatter_dimension=0, tiled=True)
    reduced_down = lax.psum_scatter(grad_down.astype(BF16), "dp", scatter_dimension=1, tiled=True)
    return (grad_probs, reduced_gu[None], reduced_down[None])


def solution(mesh):
    whole_experts = mesh.shape["expert"] == EXPERTS and mesh.shape["dp"] == 4
    return jax.shard_map(
        plane_body if whole_experts else sliced_body,
        mesh=mesh,
        in_specs=(
            P(("dp", "expert"), None),
            P(("dp", "expert"), None),
            P(("dp", "expert"), None),
            P(("dp", "expert"), None),
            P("expert", None, None),
            P("expert", None, None),
        ),
        out_specs=(P(("dp", "expert"), None), P("expert", "dp", None), P("expert", None, "dp")),
        check_vma=False,
    )
```
